128 devices in a mesh: gx: 8 (over x_lo, y), gy: 4 (over x_hi, core), gz: 4 (over z).
Axes of the slice: x: 4 (x_hi: 2, x_lo: 2; x = x_hi * 2 + x_lo), y: 4, z: 4, core: 2. Of those that a mesh axis runs over, the one named last changes fastest.
Arguments:
- velocity: float32 [3, 80, 80, 2560], P(None, 'gx', 'gy', 'gz'), may hold values from -6 to 6
- obstacle_element_mask: int32 [16, 16, 512], P('gx', 'gy', 'gz'), may hold values 0 or 1
- element_metric_scale: float32 [16, 16, 512], P('gx', 'gy', 'gz'), may hold values from 0.5 to 8
Outputs:
- smoothed: float32 [80, 80, 2560], P('gx', 'gy', 'gz')
- coarse: float32 [16, 16, 512], P('gx', 'gy', 'gz')
The draws below stay inside these ranges and needn't reach their ends.
All inputs are finite; a program needn't handle non-finite values. No bound on the sum of `obstacle_element_mask` on one device may be relied on, other than what follows from the above.
Results may differ from the reference program's by a relative error of at most 0.00012.
Values sent between devices are 32-bit elements; how exact they have to be, the bound alone decides.
No kernel may reach another device: no remote copies, remote signals or barrier semaphores. Data moves between devices by JAX's collectives and lax.ppermute only.
A program may use at most 384 MiB of HBM per device.

```python
import math
import jax
import jax.numpy as jnp
import numpy as np
from jax import lax

ELEMENTS_X = 16
ELEMENTS_Y = 16
ELEMENTS_Z = 512
NX = 80
NY = 80
NZ = 2560


def plant(values, stream_key, least, top_value):
    shape = values.shape
    spot = [jax.random.randint(jax.random.fold_in(stream_key, axis), (), 0, shape[axis]) for axis in range(len(shape))]
    values = values.at[tuple(spot)].set(least)
    longest = shape.index(max(shape))
    spot[longest] = (spot[longest] + 1) % shape[longest]
    return values.at[tuple(spot)].set(top_value)


def block_levels(own_key, dims, cuts, smallest, largest):
    def one(dim, blocks):
        draws = jax.random.uniform(jax.random.fold_in(jax.random.fold_in(own_key, 6), dim), (blocks,), jnp.float32, smallest / len(cuts), largest / len(cuts))
        return jnp.repeat(jnp.exp(draws), dims[dim] // blocks).reshape((-1,) + (1,) * (len(dims) - dim - 1))

    factor_of = one(*cuts[0])
    for cut in cuts[1:]:
        factor_of = factor_of * one(*cut)
    return factor_of


def bell_draw(key, shape, spread, most, cuts=(), kind=jnp.bfloat16):
    entries = jax.random.normal(key, shape, jnp.float32) * spread
    if len(cuts) > 0:
        entries = block_levels(key, shape, cuts, -0.22, 0.18) * entries
    return jnp.clip(entries, min=-most, max=most).astype(kind)


def setup_inputs(seed: int = 0) -> dict:
    seeds = jax.random.split(jax.random.key(seed), 4)
    velocity = bell_draw(seeds[0], (3, NX, NY, NZ), 1.0, 6.0, ((1, 8), (2, 4), (3, 4)), jnp.float32)
    obstacle_element_mask = plant((jax.random.randint(seeds[1], (ELEMENTS_X, ELEMENTS_Y, ELEMENTS_Z), 0, 8) < 1).astype(jnp.int32), jax.random.fold_in(seeds[1], 1), 0, 1)
    element_metric_scale = jnp.clip(jnp.exp(math.log(8.0) - 2.7725887 * jax.random.uniform(seeds[2], (ELEMENTS_X, ELEMENTS_Y, ELEMENTS_Z), jnp.float32) ** block_levels(seeds[2], (ELEMENTS_X, ELEMENTS_Y, ELEMENTS_Z), ((0, 8), (1, 4), (2, 4)), -0.2, 0.2)), 0.5, 8.0)
    return dict(velocity=velocity, obstacle_element_mask=obstacle_element_mask, element_metric_scale=element_metric_scale)


lift_factor = 10.0
time_step = 0.05
penalty = 4.0

def lobatto_points():
    return np.array([-1.0, -math.sqrt(3.0 / 7.0), 0.0, math.sqrt(3.0 / 7.0), 1.0])

def lobatto_weights():
    return np.array([0.1, 49.0 / 90.0, 32.0 / 45.0, 49.0 / 90.0, 0.1])

def derivative_matrix():
    points = lobatto_points()
    scales = np.array([np.prod([points[i] - points[k] for k in range(5) if k != i]) for i in range(5)])
    result = np.zeros((5, 5))
    for i in range(5):
        for j in range(5):
            if i != j:
                result[i, j] = scales[i] / (scales[j] * (points[i] - points[j]))
        result[i, i] = -np.sum(result[i])
    return result

def eigen_basis_table():
    return np.array([[math.sqrt((1.0 if k == 0 else 2.0) / 5.0) * math.cos(math.pi * (i + 0.5) * k / 5.0) for k in range(5)] for i in range(5)])

def eigen_value_table():
    return np.array([4.0 * math.sin(math.pi * k / 10.0) ** 2 for k in range(5)])

def hat_weight_table():
    points = lobatto_points()
    weights = lobatto_weights()
    return np.array([weights * (1.0 - points) / 2.0, weights * (1.0 + points) / 2.0])

def apply_along(matrix, field, axis):
    weights = jnp.asarray(matrix, jnp.float32)
    out_width = weights.shape[0]
    in_width = weights.shape[1]
    extent = field.shape
    if axis == 0:
        blocks = field.reshape(extent[0] // in_width, in_width, extent[1], extent[2])
        result = jnp.einsum('ij,ajbc->aibc', weights, blocks, precision=lax.Precision.HIGHEST)
        return result.reshape(extent[0] // in_width * out_width, extent[1], extent[2])
    if axis == 1:
        blocks = field.reshape(extent[0], extent[1] // in_width, in_width, extent[2])
        result = jnp.einsum('ij,abjc->abic', weights, blocks, precision=lax.Precision.HIGHEST)
        return result.reshape(extent[0], extent[1] // in_width * out_width, extent[2])
    blocks = field.reshape(extent[0], extent[1], extent[2] // in_width, in_width)
    result = jnp.einsum('ij,abcj->abci', weights, blocks, precision=lax.Precision.HIGHEST)
    return result.reshape(extent[0], extent[1], extent[2] // in_width * out_width)

def to_nodes(values):
    return jnp.repeat(jnp.repeat(jnp.repeat(values, 5, axis=0), 5, axis=1), 5, axis=2)

def face_masks(extent, axis):
    position = jnp.arange(extent) % 5
    layout = [1, 1, 1]
    layout[axis] = extent
    left_end = (position == 0).astype(jnp.float32).reshape(layout)
    right_end = (position == 4).astype(jnp.float32).reshape(layout)
    return (left_end, right_end)

def neighbours(padded, axis):
    inner = padded[1:-1, 1:-1, 1:-1]
    extent = inner.shape[axis]
    lower = [slice(1, -1)] * 3
    upper = [slice(1, -1)] * 3
    lower[axis] = slice(0, extent)
    upper[axis] = slice(2, extent + 2)
    return (inner, padded[tuple(lower)], padded[tuple(upper)])

def convective(padded):
    dmatrix = derivative_matrix()
    terms = []
    for c in range(3):
        total = jnp.zeros(padded.shape[1:], jnp.float32)[1:-1, 1:-1, 1:-1]
        for a in range(3):
            normal_in, normal_lo, normal_hi = neighbours(padded[a], a)
            moved_in, moved_lo, moved_hi = neighbours(padded[c], a)
            flux_in = normal_in * moved_in
            left_end, right_end = face_masks(normal_in.shape[a], a)
            speed_lo = jnp.maximum(jnp.abs(normal_in), jnp.abs(normal_lo))
            speed_hi = jnp.maximum(jnp.abs(normal_in), jnp.abs(normal_hi))
            jump_lo = -0.5 * (normal_lo * moved_lo - flux_in) - 0.5 * speed_lo * (moved_lo - moved_in)
            upper_jump_value = 0.5 * (normal_hi * moved_hi - flux_in) - 0.5 * speed_hi * (moved_hi - moved_in)
            total = total + apply_along(dmatrix, flux_in, a) + lift_factor * (left_end * jump_lo + right_end * upper_jump_value)
        terms.append(total)
    return terms

def divergence(triples):
    dmatrix = derivative_matrix()
    total = 0.0
    for a in range(3):
        inner, lower, upper = triples[a]
        left_end, right_end = face_masks(inner.shape[a], a)
        total = total + apply_along(dmatrix, inner, a) + lift_factor * (left_end * -0.5 * (lower - inner) + right_end * 0.5 * (upper - inner))
    return total

def smooth(pressure_right_side, element_metric_scale):
    basis = eigen_basis_table()
    coeffs = pressure_right_side
    for axis in range(3):
        coeffs = apply_along(basis.T, coeffs, axis)
    extent = pressure_right_side.shape
    modal = jnp.asarray(eigen_value_table(), jnp.float32)
    modes = jnp.tile(modal, extent[0] // 5)[:, None, None] + jnp.tile(modal, extent[1] // 5)[None, :, None] + jnp.tile(modal, extent[2] // 5)[None, None, :]
    coeffs = coeffs / (to_nodes(element_metric_scale) * modes + 1.0)
    for axis in range(3):
        coeffs = apply_along(basis, coeffs, axis)
    return coeffs

def vertex_partials(pressure_right_side):
    hats = hat_weight_table()
    reduced = pressure_right_side
    for axis in range(3):
        reduced = apply_along(hats, reduced, axis)
    extent = reduced.shape
    blocks = reduced.reshape(extent[0] // 2, 2, extent[1] // 2, 2, extent[2] // 2, 2)
    corner_vertex_list = 0.0
    for a in range(2):
        for b in range(2):
            for c in range(2):
                corner_vertex_list = corner_vertex_list + jnp.pad(blocks[:, a, :, b, :, c], ((a, 1 - a), (b, 1 - b), (c, 1 - c)))
    return corner_vertex_list

def reference(velocity, obstacle_element_mask, element_metric_scale):
    padded = jnp.pad(velocity, ((0, 0), (1, 1), (1, 1), (1, 1)))
    damping = 1.0 + penalty * to_nodes(obstacle_element_mask.astype(jnp.float32))
    terms = convective(padded)
    provisional = jnp.stack([(velocity[c] - time_step * terms[c]) / damping for c in range(3)])
    widened = jnp.pad(provisional, ((0, 0), (1, 1), (1, 1), (1, 1)))
    triples = [neighbours(widened[a], a) for a in range(3)]
    pressure_right_side = -divergence(triples)
    smoothed = smooth(pressure_right_side, element_metric_scale)
    corner_vertex_list = vertex_partials(pressure_right_side)
    coarse = corner_vertex_list[:-1, :-1, :-1]
    return (smoothed, coarse)
```

```python
import functools
import math

import jax
import jax.numpy as jnp
import ml_dtypes
import numpy as np
from jax import lax
from jax.experimental import pallas as pl
from jax.experimental.pallas import tpu as pltpu
from jax.sharding import PartitionSpec as P

LIFT = 10.0
STEP = 0.05
PENALTY = 4.0

BX, BY, BZ = 10, 20, 640
EX, EY, EZ = 2, 4, 128
PY = 24
ROWS = BX * PY
TILES = BZ // 128
WINDOWS = ((0, 256, 0, 384), (256, 512, 128, 640), (512, 640, 384, 640))
ZEDGE = 16

F32 = jnp.float32
BF16 = jnp.bfloat16


def lobatto_points():
    return np.array([-1.0, -math.sqrt(3.0 / 7.0), 0.0, math.sqrt(3.0 / 7.0), 1.0])


def lobatto_weights():
    return np.array([0.1, 49.0 / 90.0, 32.0 / 45.0, 49.0 / 90.0, 0.1])


def derivative_matrix():
    points = lobatto_points()
    scales = np.array(
        [np.prod([points[i] - points[k] for k in range(5) if k != i]) for i in range(5)]
    )
    result = np.zeros((5, 5))
    for i in range(5):
        for j in range(5):
            if i != j:
                result[i, j] = scales[i] / (scales[j] * (points[i] - points[j]))
        result[i, i] = -np.sum(result[i])
    return result


def eigen_basis_table():
    return np.array(
        [
            [
                math.sqrt((1.0 if k == 0 else 2.0) / 5.0) * math.cos(math.pi * (i + 0.5) * k / 5.0)
                for k in range(5)
            ]
            for i in range(5)
        ]
    )


def eigen_value_table():
    return np.array([4.0 * math.sin(math.pi * k / 10.0) ** 2 for k in range(5)])


def hat_weight_table():
    points = lobatto_points()
    weights = lobatto_weights()
    return np.array([weights * (1.0 - points) / 2.0, weights * (1.0 + points) / 2.0])


def inner_matrix():
    result = derivative_matrix()
    result[0, 0] += 0.5 * LIFT
    result[4, 4] -= 0.5 * LIFT
    return result


def line_operator(elements, coupled):
    inner = inner_matrix()
    size = 5 * elements
    m = np.zeros((size, size))
    for e in range(elements):
        m[5 * e : 5 * e + 5, 5 * e : 5 * e + 5] = inner
        if coupled and e > 0:
            m[5 * e, 5 * e - 1] = -0.5 * LIFT
        if coupled and e < elements - 1:
            m[5 * e + 4, 5 * e + 5] = 0.5 * LIFT
    return m


def hats_line(elements):
    h = hat_weight_table()
    m = np.zeros((elements + 1, 5 * elements))
    for e in range(elements):
        m[e, 5 * e : 5 * e + 5] += h[0]
        m[e + 1, 5 * e : 5 * e + 5] += h[1]
    return m


def slopes_line(elements):
    h = hat_weight_table()
    d = derivative_matrix()
    g = h @ d
    g[0, 0] += LIFT * h[0, 0]
    g[1, 4] -= LIFT * h[1, 4]
    m = np.zeros((elements + 1, 5 * elements))
    for e in range(elements):
        m[e, 5 * e : 5 * e + 5] += g[0]
        m[e + 1, 5 * e : 5 * e + 5] += g[1]
    return m


def pad_rows(m):
    out = np.zeros((m.shape[0], BX, PY))
    out[:, :, :BY] = m.reshape(m.shape[0], BX, BY)
    return out.reshape(m.shape[0], ROWS)


def pad_both(m):
    return pad_rows(pad_rows(m).T).T


def pad_to(m, rows, columns):
    out = np.zeros((rows, columns))
    out[: m.shape[0], : m.shape[1]] = m
    return out


class Packed:

    def __init__(self):
        self.parts = []
        self.places = {}
        self.rows = 0

    def add(self, name, m, parts=2):
        m = np.asarray(m, np.float64)
        hi = m.astype(np.float32).astype(ml_dtypes.bfloat16)
        lo = (m - hi.astype(np.float64)).astype(np.float32).astype(ml_dtypes.bfloat16)
        places = []
        for part in (hi, lo)[:parts]:
            wide = np.zeros((part.shape[0], 256), ml_dtypes.bfloat16)
            wide[:, : part.shape[1]] = part
            places.append((self.rows, part.shape[0], part.shape[1]))
            self.parts.append(wide)
            self.rows += part.shape[0]
        self.places[name] = places

    def add_windows(self, name, m):
        for i, (n0, n1, k0, k1) in enumerate(WINDOWS):
            self.add(name + str(i), m[k0:k1, n0:n1])

    def array(self):
        return jnp.asarray(np.concatenate(self.parts))

    def get(self, ref, name):
        out = [ref[r : r + n, 0:c] for r, n, c in self.places[name]]
        return out[0] if len(out) == 1 else out


def split(x):
    hi = x.astype(BF16)
    return hi, (x - hi.astype(F32)).astype(BF16)


def dot(a, b):
    return jnp.dot(a, b, preferred_element_type=F32)


def left_dot(m, hi, lo):
    return dot(m[0], hi) + dot(m[1], hi) + dot(m[0], lo)


def right_dot(hi, lo, m):
    return dot(hi, m[0]) + dot(lo, m[0]) + dot(hi, m[1])


def flag(name, low):
    edge = 0 if low else lax.axis_size(name) - 1
    return jnp.where(lax.axis_index(name) == edge, 0.0, 1.0)


def pack_kernel(v, mask, x_lo, x_hi, y_lo, y_hi, z_lo, z_hi, solid):
    solid[...] = mask[...].astype(F32).reshape(8, EZ)
    x_lo[...] = v[:, 0] * flag("gx", True)
    x_hi[...] = v[:, BX - 1] * flag("gx", False)
    y_low, y_high = flag("gy", True), flag("gy", False)
    lane = lax.broadcasted_iota(jnp.int32, (BY, 128), 1)
    low = jnp.zeros((BY, 128), F32)
    high = jnp.zeros((BY, 128), F32)
    for c in range(3):
        for x in range(BX):
            y_lo[c, x : x + 1, :] = v[c, x, 0:1, :] * y_low
            y_hi[c, x : x + 1, :] = v[c, x, BY - 1 : BY, :] * y_high
            here = lane == 16 * c + x
            low = jnp.where(here, jnp.broadcast_to(v[c, x, :, 0:1], (BY, 128)), low)
            high = jnp.where(here, jnp.broadcast_to(v[c, x, :, BZ - 1 : BZ], (BY, 128)), high)
    z_lo[0:BY, :] = low * flag("gz", True)
    z_hi[0:BY, :] = high * flag("gz", False)
    z_lo[BY:PY, :] = jnp.zeros((PY - BY, 128), F32)
    z_hi[BY:PY, :] = jnp.zeros((PY - BY, 128), F32)


def plane_sums(planes, scale):
    d = inner_matrix() * scale
    outs = []
    for i in range(5):
        total = None
        for j in range(5):
            if abs(d[i, j]) < 1e-12:
                continue
            term = float(d[i, j]) * planes[j]
            total = term if total is None else total + term
        outs.append(total)
    return outs


def step_kernel(
    packed, v, hx_lo, hx_hi, hy_lo, hy_hi, hz_lo, hz_hi, solid, weights,
    rhs, xp, xm, yp, ym, zp, zm, own,
    V, FH, FL, conv, prov, PH, PL,
):
    for c in range(3):
        V[c, 0, 0:BY, 128:768] = hx_lo[c]
        V[c, BX + 1, 0:BY, 128:768] = hx_hi[c]
        V[c, 0, BY:PY, 128:768] = jnp.zeros((PY - BY, BZ), F32)
        V[c, BX + 1, BY:PY, 128:768] = jnp.zeros((PY - BY, BZ), F32)
        for x in range(BX):
            V[c, x + 1, 0:BY, 128:768] = v[c, x]
            V[c, x + 1, 20:22, 128:768] = jnp.broadcast_to(hy_hi[c, x : x + 1, :], (2, BZ))
            V[c, x + 1, 22:24, 128:768] = jnp.broadcast_to(hy_lo[c, x : x + 1, :], (2, BZ))
            k = 16 * c + x
            V[c, x + 1, :, 0:128] = jnp.broadcast_to(hz_lo[:, k : k + 1], (PY, 128))
            V[c, x + 1, :, 768:896] = jnp.broadcast_to(hz_hi[:, k : k + 1], (PY, 128))

    def products(t, carry):
        src = pl.ds(pl.multiple_of(128 + 128 * t, 128), 128)
        dst = pl.ds(pl.multiple_of(128 * t, 128), 128)
        for q in range(BX // 2):
            a = [V[c, 1 + 2 * q : 3 + 2 * q, :, src].reshape(2 * PY, 128) for c in range(3)]
            pairs = (a[0] * a[1], a[1] * a[1], a[1] * a[2], a[0] * a[2], a[2] * a[2])
            for f, value in enumerate(pairs):
                hi, lo = split(value)
                FH[f, 2 * PY * q : 2 * PY * (q + 1), dst] = hi
                FL[f, 2 * PY * q : 2 * PY * (q + 1), dst] = lo
        return carry

    lax.fori_loop(0, TILES, products, 0)

    my = packed.get(weights, "my")
    for i, (n0, n1, k0, k1) in enumerate(WINDOWS):
        b = packed.get(weights, "bz" + str(i))
        for c in range(3):
            along_z = (3, 2, 4)[c]
            y = left_dot(my, FH[c, :, n0:n1], FL[c, :, n0:n1])
            z = right_dot(FH[along_z, :, k0:k1], FL[along_z, :, k0:k1], b)
            conv[c, :, :, n0:n1] = (y + z).reshape(BX, PY, n1 - n0)

    def along_x(t, carry):
        src = pl.ds(pl.multiple_of(128 + 128 * t, 128), 128)
        dst = pl.ds(pl.multiple_of(128 * t, 128), 128)
        for e in range(EX):
            v0 = [V[0, 1 + 5 * e + i, :, src] for i in range(5)]
            for c in range(3):
                flux = [v0[i] * V[c, 1 + 5 * e + i, :, src] for i in range(5)]
                for i, total in enumerate(plane_sums(flux, -STEP)):
                    conv[c, 5 * e + i, :, dst] = conv[c, 5 * e + i, :, dst] + total
        return carry

    lax.fori_loop(0, TILES, along_x, 0)

    solid = spread_out(packed, weights, [solid[...].astype(BF16)])
    conv_scale = -0.5 * LIFT * STEP
    lane = lax.broadcasted_iota(jnp.int32, (PY, 128), 1)
    row = lax.broadcasted_iota(jnp.int32, (PY, 128), 0)
    row_left = (lax.rem(row, 5) == 0) & (row < BY)
    row_right = (lax.rem(row, 5) == 4) & (row < BY)
    y_face = jnp.where(row_left | row_right, conv_scale, 0.0)
    y_sign = jnp.where(row_left, conv_scale, jnp.where(row_right, -conv_scale, 0.0))
    damp = [1.0 / (1.0 + PENALTY * solid[PY * e : PY * (e + 1)]) for e in range(EX)]
    for t in range(TILES):
        point = lax.rem(lane + 128 * t, 5)
        z_left = point == 0
        z_face = jnp.where(z_left | (point == 4), conv_scale, 0.0)
        z_sign = jnp.where(z_left, conv_scale, jnp.where(point == 4, -conv_scale, 0.0))
        here = slice(128 + 128 * t, 256 + 128 * t)
        before = slice(128 * t, 128 + 128 * t)
        after = slice(256 + 128 * t, 384 + 128 * t)
        out = slice(128 * t, 128 + 128 * t)
        for x in range(BX):
            a = [V[c, x + 1, :, here] for c in range(3)]
            total = [conv[c, x, :, out] for c in range(3)]
            w = []
            for c in range(3):
                lo = pltpu.roll(jnp.where(lane == 127, V[c, x + 1, :, before], a[c]), 1, 1)
                hi = pltpu.roll(jnp.where(lane == 0, V[c, x + 1, :, after], a[c]), 127, 1)
                w.append(jnp.where(z_left, lo, hi))
            p = z_face * jnp.maximum(jnp.abs(a[2]), jnp.abs(w[2]))
            q = p + z_sign * w[2]
            total = [total[c] + (p * a[c] - q * w[c]) for c in range(3)]
            w = [
                jnp.where(row_left, pltpu.roll(a[c], 1, 0), pltpu.roll(a[c], PY - 1, 0))
                for c in range(3)
            ]
            p = y_face * jnp.maximum(jnp.abs(a[1]), jnp.abs(w[1]))
            q = p + y_sign * w[1]
            total = [total[c] + (p * a[c] - q * w[c]) for c in range(3)]
            if x % 5 in (0, 4):
                other = x if x % 5 == 0 else x + 2
                sign = 1.0 if x % 5 == 0 else -1.0
                w = [V[c, other, :, here] for c in range(3)]
                p = conv_scale * jnp.maximum(jnp.abs(a[0]), jnp.abs(w[0]))
                q = p + (sign * conv_scale) * w[0]
                total = [total[c] + (p * a[c] - q * w[c]) for c in range(3)]
            factor = damp[x // 5][:, out]
            for c in range(3):
                prov[c, x, :, out] = (a[c] + total[c]) * factor

    for q in range(BX // 2):
        for c in range(3):
            hi, lo = split(prov[c, 2 * q : 2 * q + 2].reshape(2 * PY, BZ))
            PH[c, 2 * PY * q : 2 * PY * (q + 1), :] = hi
            PL[c, 2 * PY * q : 2 * PY * (q + 1), :] = lo
    ry = packed.get(weights, "ry")
    for i, (n0, n1, k0, k1) in enumerate(WINDOWS):
        b = packed.get(weights, "rz" + str(i))
        y = left_dot(ry, PH[1, :, n0:n1], PL[1, :, n0:n1])
        z = right_dot(PH[2, :, k0:k1], PL[2, :, k0:k1], b)
        rhs[:, :, n0:n1] = (y + z).reshape(BX, PY, n1 - n0)

    def right_x(t, carry):
        dst = pl.ds(pl.multiple_of(128 * t, 128), 128)
        planes = [prov[0, x, :, dst] for x in range(BX)]
        outs = plane_sums(planes[:5], -1.0) + plane_sums(planes[5:], -1.0)
        outs[4] = outs[4] - 0.5 * LIFT * planes[5]
        outs[5] = outs[5] + 0.5 * LIFT * planes[4]
        for x in range(BX):
            rhs[x, :, dst] = rhs[x, :, dst] + outs[x]
        return carry

    lax.fori_loop(0, TILES, right_x, 0)

    first = [1.0 - flag(name, True) for name in ("gx", "gy", "gz")]
    x_low, y_low, z_low = (flag(name, True) for name in ("gx", "gy", "gz"))
    x_high, y_high, z_high = (flag(name, False) for name in ("gx", "gy", "gz"))
    parts = []
    c0, c1, c2, d0, d1 = (
        sum(part.astype(F32) for part in packed.get(weights, n)) for n in ("c0", "c1", "c2", "d0", "d1")
    )
    for c, m in enumerate((c0 + first[0] * d0, c1 + first[1] * d1, c2)):
        hi, lo = split(m)
        parts.append(dot(hi, PH[c]) + dot(lo, PH[c]) + dot(hi, PL[c]))
    hi, lo = split(parts[0] + parts[1])
    coarse = right_dot(hi, lo, packed.get(weights, "hz"))
    hi, lo = split(parts[2])
    coarse = coarse + right_dot(hi, lo, packed.get(weights, "gz"))
    lane16 = lax.broadcasted_iota(jnp.int32, (16, 128), 1)
    vertices = coarse[:, 0:128] - jnp.where(
        lane16 == 0, (0.5 * LIFT * 0.1) * first[2] * parts[2][:, 0:128], 0.0
    )
    row16 = lax.broadcasted_iota(jnp.int32, (16, 128), 0)
    there = jnp.where(row16 >= 10, x_high, 1.0) * jnp.where(lax.rem(row16, 5) == 4, y_high, 1.0)
    vertices = vertices * there
    edge = coarse[:, 128:256] * (there * z_high)
    edge_next = pltpu.roll(edge, 1, 1)
    own[...] = vertices

    xp[0:PY, :] = prov[0, BX - 1] * x_high
    xm[...] = prov[0, 0] * x_low
    xp[24:32, :] = jnp.zeros((8, BZ), F32)
    xp[24:29, 0:128] = vertices[10:15]
    xp[24:29, 128:256] = edge[10:15]
    yp[8:24, :] = jnp.zeros((16, BZ), F32)
    ym[8:16, :] = jnp.zeros((8, BZ), F32)
    lane24 = lax.broadcasted_iota(jnp.int32, (PY, 128), 1)
    low = jnp.zeros((PY, 128), F32)
    high = jnp.zeros((PY, 128), F32)
    for x in range(BX):
        yp[x : x + 1, :] = prov[1, x, BY - 1 : BY, :] * y_high
        ym[x : x + 1, :] = prov[1, x, 0:1, :] * y_low
        low = jnp.where(lane24 == x, jnp.broadcast_to(prov[2, x, :, 0:1], (PY, 128)), low)
        high = jnp.where(lane24 == x, jnp.broadcast_to(prov[2, x, :, BZ - 1 : BZ], (PY, 128)), high)
    yp[16:17, 0:128] = vertices[4:5]
    yp[17:18, 0:128] = vertices[9:10]
    yp[16:17, 128:256] = edge[4:5] + edge_next[9:10]
    zm[...] = low * z_low
    zp[...] = high * z_high
    zp[0:4, :] = zp[0:4, :] + (edge[0:4] + edge_next[5:9])


def spread_out(packed, weights, parts):
    rows_of = packed.get(weights, "rows_of")
    wide = []
    for i in range(3):
        m = packed.get(weights, "spread" + str(i))
        wide.append(sum(dot(part, m) for part in parts))
    return sum(dot(rows_of, part) for part in split(jnp.concatenate(wide, axis=1))[: len(parts)])


def smooth_kernel(
    packed, rhs, hx_lo, hx_hi, hy_lo, hy_hi, hz_lo, hz_hi, own, scale, weights, modes,
    smoothed, coarse, AH, AL, BH, BL,
):
    lift = 0.5 * LIFT
    lane = lax.broadcasted_iota(jnp.int32, (PY, 128), 1)
    row = lax.broadcasted_iota(jnp.int32, (PY, BZ), 0)
    for q in range(BX // 2):
        planes = []
        for x in (2 * q, 2 * q + 1):
            r = rhs[x]
            if x == 0:
                r = r + lift * hx_lo[0:PY, :]
            if x == BX - 1:
                r = r - lift * hx_hi[...]
            r = r + jnp.where(row == 0, lift * jnp.broadcast_to(hy_lo[x : x + 1, :], (PY, BZ)), 0.0)
            r = r - jnp.where(
                row == BY - 1, lift * jnp.broadcast_to(hy_hi[x : x + 1, :], (PY, BZ)), 0.0
            )
            left = r[:, 0:128] + jnp.where(
                lane == 0, lift * jnp.broadcast_to(hz_lo[:, x : x + 1], (PY, 128)), 0.0
            )
            right = r[:, BZ - 128 : BZ] - jnp.where(
                lane == 127, lift * jnp.broadcast_to(hz_hi[:, x : x + 1], (PY, 128)), 0.0
            )
            planes.append(jnp.concatenate([left, r[:, 128 : BZ - 128], right], axis=1))
        hi, lo = split(jnp.concatenate(planes, axis=0))
        AH[2 * PY * q : 2 * PY * (q + 1), :] = hi
        AL[2 * PY * q : 2 * PY * (q + 1), :] = lo

    for n0, n1, _, _ in WINDOWS:
        hi, lo = split(left_dot(packed.get(weights, "tf"), AH[:, n0:n1], AL[:, n0:n1]))
        BH[:, n0:n1] = hi
        BL[:, n0:n1] = lo

    factor = spread_out(packed, weights, split(scale[...].reshape(8, EZ)))
    values = eigen_value_table()
    for i, (n0, n1, k0, k1) in enumerate(WINDOWS):
        m = packed.get(weights, "sf" + str(i))
        c = right_dot(BH[:, k0:k1], BL[:, k0:k1], m).reshape(BX, PY, n1 - n0)
        done = []
        for x in range(BX):
            f = factor[PY * (x // 5) : PY * (x // 5 + 1), n0:n1]
            done.append(c[x] / (f * (modes[:, n0:n1] + float(values[x % 5])) + 1.0))
        hi, lo = split(jnp.concatenate(done, axis=0))
        AH[:, n0:n1] = hi
        AL[:, n0:n1] = lo

    for i, (n0, n1, k0, k1) in enumerate(WINDOWS):
        m = packed.get(weights, "sb" + str(i))
        hi, lo = split(right_dot(AH[:, k0:k1], AL[:, k0:k1], m))
        BH[:, n0:n1] = hi
        BL[:, n0:n1] = lo

    for n0, n1, _, _ in WINDOWS:
        c = left_dot(packed.get(weights, "tb"), BH[:, n0:n1], BL[:, n0:n1]).reshape(BX, PY, n1 - n0)
        smoothed[:, :, n0:n1] = c[:, 0:BY]

    lane4 = lax.broadcasted_iota(jnp.int32, (4, 128), 1)
    row4 = lax.broadcasted_iota(jnp.int32, (4, 128), 0)
    for vx in range(EX):
        total = own[5 * vx : 5 * vx + 4, :]
        if vx == 0:
            total = total + hx_lo[24:28, 0:128]
        total = total + jnp.where(
            row4 == 0, jnp.broadcast_to(hy_lo[16 + vx : 17 + vx, 0:128], (4, 128)), 0.0
        )
        k = ZEDGE + vx
        total = total + jnp.where(
            lane4 == 0, jnp.broadcast_to(hz_lo[0:4, k : k + 1], (4, 128)), 0.0
        )
        coarse[vx] = total


def constants():
    step, smooth = Packed(), Packed()
    eye_x = np.eye(BX)
    step.add("my", pad_both(np.kron(eye_x, -STEP * line_operator(EY, False))))
    step.add("ry", pad_both(np.kron(eye_x, -line_operator(EY, True))))
    step.add_windows("bz", -STEP * line_operator(EZ, False).T)
    step.add_windows("rz", -line_operator(EZ, True).T)
    basis = eigen_basis_table()
    sx = np.kron(np.eye(EX), basis)
    sy = np.kron(np.eye(EY), basis)
    sz = np.kron(np.eye(EZ), basis)
    t = np.kron(sx, sy)
    smooth.add("tf", pad_both(t.T))
    smooth.add("tb", pad_both(t))
    smooth.add_windows("sf", sz)
    smooth.add_windows("sb", sz.T)
    spread = np.kron(np.eye(EZ), np.ones((1, 5)))
    rows_of = np.zeros((EX * PY, 8))
    for e in range(EX):
        for y in range(BY):
            rows_of[PY * e + y, EY * e + y // 5] = 1.0
    for packed in (step, smooth):
        packed.add("rows_of", rows_of, 1)
        for i, (n0, n1, _, _) in enumerate(WINDOWS):
            packed.add("spread" + str(i), spread[:, n0:n1], 1)
    values = eigen_value_table()
    modes = np.zeros((PY, BZ))
    for y in range(BY):
        modes[y] = values[y % 5] + np.tile(values, EZ)
    hx, hy, hz = hats_line(EX), hats_line(EY), hats_line(EZ)
    gx, gy, gz = slopes_line(EX), slopes_line(EY), slopes_line(EZ)
    for name, m in (("hz", hz), ("gz", gz)):
        wide = np.zeros((BZ, 256))
        wide[:, 0:EZ] = m[:EZ].T
        wide[:, 128 + ZEDGE] = m[EZ]
        step.add(name, wide)
    half = 0.5 * LIFT * hat_weight_table()[0, 0]
    ex, ey = np.zeros_like(gx), np.zeros_like(gy)
    ex[0, 0] = -half
    ey[0, 0] = -half
    for name, m in (
        ("c0", np.kron(gx, hy)),
        ("c1", np.kron(hx, gy)),
        ("c2", np.kron(hx, hy)),
        ("d0", np.kron(ex, hy)),
        ("d1", np.kron(hx, ey)),
    ):
        step.add(name, pad_to(pad_rows(-m), 16, ROWS))
    return step, smooth, modes.astype(np.float32)


def shift(x, axis, by):
    size = lax.axis_size(axis)
    return lax.ppermute(x, axis, [(i, (i + by) % size) for i in range(size)])


def like(*shape):
    return jax.ShapeDtypeStruct(shape, F32)


def run(kernel, outs, operands, scratch=(), name=None, flops=0, moved=0):
    vmem = pl.BlockSpec(memory_space=pltpu.VMEM)
    return pl.pallas_call(
        kernel,
        out_shape=outs,
        in_specs=[vmem] * len(operands),
        out_specs=[vmem] * len(outs),
        scratch_shapes=list(scratch),
        compiler_params=pltpu.CompilerParams(vmem_limit_bytes=40 * 2**20),
        cost_estimate=pl.CostEstimate(flops=flops, bytes_accessed=moved, transcendentals=0),
        name=name,
    )(*operands)


def shards(velocity, obstacle_element_mask, element_metric_scale):
    step, smooth, modes = constants()
    faces = run(
        pack_kernel,
        [like(3, BY, BZ)] * 2 + [like(3, BX, BZ)] * 2 + [like(PY, 128)] * 2 + [like(8, EZ)],
        [velocity, obstacle_element_mask],
        name="pack",
        flops=10**10,
        moved=4 << 20,
    )
    halo = [
        shift(faces[1], "gx", 1),
        shift(faces[0], "gx", -1),
        shift(faces[3], "gy", 1),
        shift(faces[2], "gy", -1),
        shift(faces[5], "gz", 1),
    ]
    halo[0], last = lax.optimization_barrier((halo[0], faces[4]))
    halo.append(shift(last, "gz", -1))
    rhs, xp, xm, yp, ym, zp, zm, own = run(
        functools.partial(step_kernel, step),
        [
            like(BX, PY, BZ),
            like(32, BZ),
            like(PY, BZ),
            like(24, BZ),
            like(16, BZ),
            like(PY, 128),
            like(PY, 128),
            like(16, 128),
        ],
        [velocity, *halo, faces[6], step.array()],
        scratch=[
            pltpu.VMEM((3, BX + 2, PY, 896), F32),
            pltpu.VMEM((5, ROWS, BZ), BF16),
            pltpu.VMEM((5, ROWS, BZ), BF16),
            pltpu.VMEM((3, BX, PY, BZ), F32),
            pltpu.VMEM((3, BX, PY, BZ), F32),
            pltpu.VMEM((3, ROWS, BZ), BF16),
            pltpu.VMEM((3, ROWS, BZ), BF16),
        ],
        name="step",
        flops=4 * 10**9,
        moved=8 << 20,
    )
    gx_lo = shift(xp, "gx", 1)
    gx_hi = shift(xm, "gx", -1)
    yp = yp + jnp.pad(gx_lo[28:29, 0:256], ((16, 7), (0, BZ - 256)))
    gy_lo = shift(yp, "gy", 1)
    gy_hi = shift(ym, "gy", -1)
    zp = zp + jnp.pad(gx_lo[24:28, 128:256], ((0, 20), (0, 0)))
    zp = zp + jnp.pad(gy_lo[16:17, 128:256], ((0, 23), (0, 0)))
    gz_lo = shift(zp, "gz", 1)
    gz_hi = shift(zm, "gz", -1)
    smoothed, coarse = run(
        functools.partial(smooth_kernel, smooth),
        [like(BX, BY, BZ), like(EX, EY, EZ)],
        [rhs, gx_lo, gx_hi, gy_lo, gy_hi, gz_lo, gz_hi, own, element_metric_scale]
        + [smooth.array(), jnp.asarray(modes)],
        scratch=[pltpu.VMEM((ROWS, BZ), BF16)] * 4,
        name="smooth",
        flops=3 * 10**9,
        moved=6 << 20,
    )
    return (smoothed, coarse)


def solution(mesh):
    return jax.shard_map(
        shards,
        mesh=mesh,
        in_specs=(P(None, "gx", "gy", "gz"), P("gx", "gy", "gz"), P("gx", "gy", "gz")),
        out_specs=(P("gx", "gy", "gz"), P("gx", "gy", "gz")),
        check_vma=False,
    )
```

```python
import functools
import math

import jax
import jax.numpy as jnp
import ml_dtypes
import numpy as np
from jax import lax
from jax.experimental import pallas as pl
from jax.experimental.pallas import tpu as pltpu
from jax.sharding import PartitionSpec as P

LIFT = 10.0
STEP = 0.05
PENALTY = 4.0

BX, BY, BZ = 10, 20, 640
EX, EY, EZ = 2, 4, 128
PY = 24
ROWS = BX * PY
TILES = BZ // 128
WINDOWS = ((0, 256, 0, 384), (256, 512, 128, 640), (512, 640, 384, 640))
ZEDGE = 16

F32 = jnp.float32
BF16 = jnp.bfloat16


def lobatto_points():
    return np.array([-1.0, -math.sqrt(3.0 / 7.0), 0.0, math.sqrt(3.0 / 7.0), 1.0])


def lobatto_weights():
    return np.array([0.1, 49.0 / 90.0, 32.0 / 45.0, 49.0 / 90.0, 0.1])


def derivative_matrix():
    points = lobatto_points()
    scales = np.array(
        [np.prod([points[i] - points[k] for k in range(5) if k != i]) for i in range(5)]
    )
    result = np.zeros((5, 5))
    for i in range(5):
        for j in range(5):
            if i != j:
                result[i, j] = scales[i] / (scales[j] * (points[i] - points[j]))
        result[i, i] = -np.sum(result[i])
    return result


def eigen_basis_table():
    return np.array(
        [
            [
                math.sqrt((1.0 if k == 0 else 2.0) / 5.0) * math.cos(math.pi * (i + 0.5) * k / 5.0)
                for k in range(5)
            ]
            for i in range(5)
        ]
    )


def eigen_value_table():
    return np.array([4.0 * math.sin(math.pi * k / 10.0) ** 2 for k in range(5)])


def hat_weight_table():
    points = lobatto_points()
    weights = lobatto_weights()
    return np.array([weights * (1.0 - points) / 2.0, weights * (1.0 + points) / 2.0])


def inner_matrix():
    result = derivative_matrix()
    result[0, 0] += 0.5 * LIFT
    result[4, 4] -= 0.5 * LIFT
    return result


def line_operator(elements, coupled):
    inner = inner_matrix()
    size = 5 * elements
    m = np.zeros((size, size))
    for e in range(elements):
        m[5 * e : 5 * e + 5, 5 * e : 5 * e + 5] = inner
        if coupled and e > 0:
            m[5 * e, 5 * e - 1] = -0.5 * LIFT
        if coupled and e < elements - 1:
            m[5 * e + 4, 5 * e + 5] = 0.5 * LIFT
    return m


def hats_line(elements):
    h = hat_weight_table()
    m = np.zeros((elements + 1, 5 * elements))
    for e in range(elements):
        m[e, 5 * e : 5 * e + 5] += h[0]
        m[e + 1, 5 * e : 5 * e + 5] += h[1]
    return m


def slopes_line(elements):
    h = hat_weight_table()
    d = derivative_matrix()
    g = h @ d
    g[0, 0] += LIFT * h[0, 0]
    g[1, 4] -= LIFT * h[1, 4]
    m = np.zeros((elements + 1, 5 * elements))
    for e in range(elements):
        m[e, 5 * e : 5 * e + 5] += g[0]
        m[e + 1, 5 * e : 5 * e + 5] += g[1]
    return m


def pad_rows(m):
    out = np.zeros((m.shape[0], BX, PY))
    out[:, :, :BY] = m.reshape(m.shape[0], BX, BY)
    return out.reshape(m.shape[0], ROWS)


def pad_both(m):
    return pad_rows(pad_rows(m).T).T


def pad_to(m, rows, columns):
    out = np.zeros((rows, columns))
    out[: m.shape[0], : m.shape[1]] = m
    return out


class Packed:

    def __init__(self):
        self.parts = []
        self.places = {}
        self.rows = 0

    def add(self, name, m, parts=2):
        m = np.asarray(m, np.float64)
        hi = m.astype(np.float32).astype(ml_dtypes.bfloat16)
        lo = (m - hi.astype(np.float64)).astype(np.float32).astype(ml_dtypes.bfloat16)
        places = []
        for part in (hi, lo)[:parts]:
            wide = np.zeros((part.shape[0], 256), ml_dtypes.bfloat16)
            wide[:, : part.shape[1]] = part
            places.append((self.rows, part.shape[0], part.shape[1]))
            self.parts.append(wide)
            self.rows += part.shape[0]
        self.places[name] = places

    def add_windows(self, name, m):
        for i, (n0, n1, k0, k1) in enumerate(WINDOWS):
            self.add(name + str(i), m[k0:k1, n0:n1])

    def array(self):
        return jnp.asarray(np.concatenate(self.parts))

    def get(self, ref, name):
        out = [ref[r : r + n, 0:c] for r, n, c in self.places[name]]
        return out[0] if len(out) == 1 else out


def split(x):
    hi = x.astype(BF16)
    return hi, (x - hi.astype(F32)).astype(BF16)


def dot(a, b):
    return jnp.dot(a, b, preferred_element_type=F32)


def left_dot(m, hi, lo):
    return dot(m[0], hi) + dot(m[1], hi) + dot(m[0], lo)


def right_dot(hi, lo, m):
    return dot(hi, m[0]) + dot(lo, m[0]) + dot(hi, m[1])


def flag(name, low):
    edge = 0 if low else lax.axis_size(name) - 1
    return jnp.where(lax.axis_index(name) == edge, 0.0, 1.0)


def pack_kernel(v, x_lo, x_hi, y_lo, y_hi, z_lo, z_hi):
    x_lo[:, 0:BY, :] = v[:, 0] * flag("gx", True)
    x_hi[:, 0:BY, :] = v[:, BX - 1] * flag("gx", False)
    x_lo[:, BY:PY, :] = jnp.zeros((3, PY - BY, BZ), F32)
    x_hi[:, BY:PY, :] = jnp.zeros((3, PY - BY, BZ), F32)
    y_low, y_high = flag("gy", True), flag("gy", False)
    lane = lax.broadcasted_iota(jnp.int32, (BY, 128), 1)
    low = jnp.zeros((BY, 128), F32)
    high = jnp.zeros((BY, 128), F32)
    for c in range(3):
        for x in range(BX):
            y_lo[c, x : x + 1, :] = v[c, x, 0:1, :] * y_low
            y_hi[c, x : x + 1, :] = v[c, x, BY - 1 : BY, :] * y_high
            here = lane == 16 * c + x
            low = jnp.where(here, jnp.broadcast_to(v[c, x, :, 0:1], (BY, 128)), low)
            high = jnp.where(here, jnp.broadcast_to(v[c, x, :, BZ - 1 : BZ], (BY, 128)), high)
    z_lo[0:BY, :] = low * flag("gz", True)
    z_hi[0:BY, :] = high * flag("gz", False)
    z_lo[BY:PY, :] = jnp.zeros((PY - BY, 128), F32)
    z_hi[BY:PY, :] = jnp.zeros((PY - BY, 128), F32)


def plane_sums(planes, scale):
    d = inner_matrix() * scale
    outs = []
    for i in range(5):
        total = None
        for j in range(5):
            if abs(d[i, j]) < 1e-12:
                continue
            term = float(d[i, j]) * planes[j]
            total = term if total is None else total + term
        outs.append(total)
    return outs


def volume_kernel(packed, v, after, weights, conv, V, FH, FL):
    del after
    for c in range(3):
        for x in range(BX):
            V[c, x, 0:BY, :] = v[c, x]
            V[c, x, BY:PY, :] = jnp.zeros((PY - BY, BZ), F32)

    def products(t, carry):
        dst = pl.ds(pl.multiple_of(128 * t, 128), 128)
        for q in range(BX // 2):
            a = [V[c, 2 * q : 2 * q + 2, :, dst].reshape(2 * PY, 128) for c in range(3)]
            pairs = (a[0] * a[1], a[1] * a[1], a[1] * a[2], a[0] * a[2], a[2] * a[2])
            for f, value in enumerate(pairs):
                hi, lo = split(value)
                FH[f, 2 * PY * q : 2 * PY * (q + 1), dst] = hi
                FL[f, 2 * PY * q : 2 * PY * (q + 1), dst] = lo
        return carry

    lax.fori_loop(0, TILES, products, 0)

    my = packed.get(weights, "my")
    for i, (n0, n1, k0, k1) in enumerate(WINDOWS):
        b = packed.get(weights, "bz" + str(i))
        for c in range(3):
            along_z = (3, 2, 4)[c]
            y = left_dot(my, FH[c, :, n0:n1], FL[c, :, n0:n1])
            z = right_dot(FH[along_z, :, k0:k1], FL[along_z, :, k0:k1], b)
            conv[c, :, :, n0:n1] = (y + z).reshape(BX, PY, n1 - n0)

    def along_x(t, carry):
        dst = pl.ds(pl.multiple_of(128 * t, 128), 128)
        for e in range(EX):
            v0 = [V[0, 5 * e + i, :, dst] for i in range(5)]
            for c in range(3):
                flux = [v0[i] * V[c, 5 * e + i, :, dst] for i in range(5)]
                for i, total in enumerate(plane_sums(flux, -STEP)):
                    conv[c, 5 * e + i, :, dst] = conv[c, 5 * e + i, :, dst] + total
        return carry

    lax.fori_loop(0, TILES, along_x, 0)


def lift_kernel(
    packed, v, conv, hx_lo, hx_hi, hy_lo, hy_hi, hz_lo, hz_hi, mask, weights,
    prov, PH, PL, xp, xm, yp, ym, zp, zm, own, V,
):
    for c in range(3):
        V[c, 0, :, 128:768] = hx_lo[c]
        V[c, BX + 1, :, 128:768] = hx_hi[c]
        for x in range(BX):
            V[c, x + 1, 0:BY, 128:768] = v[c, x]
            V[c, x + 1, 20:22, 128:768] = jnp.broadcast_to(hy_hi[c, x : x + 1, :], (2, BZ))
            V[c, x + 1, 22:24, 128:768] = jnp.broadcast_to(hy_lo[c, x : x + 1, :], (2, BZ))
            k = 16 * c + x
            V[c, x + 1, :, 0:128] = jnp.broadcast_to(hz_lo[:, k : k + 1], (PY, 128))
            V[c, x + 1, :, 768:896] = jnp.broadcast_to(hz_hi[:, k : k + 1], (PY, 128))

    solid = spread_out(packed, weights, [mask[...].astype(F32).reshape(8, EZ).astype(BF16)])
    conv_scale = -0.5 * LIFT * STEP
    lane = lax.broadcasted_iota(jnp.int32, (PY, 128), 1)
    row = lax.broadcasted_iota(jnp.int32, (PY, 128), 0)
    row_left = (lax.rem(row, 5) == 0) & (row < BY)
    row_right = (lax.rem(row, 5) == 4) & (row < BY)
    y_face = jnp.where(row_left | row_right, conv_scale, 0.0)
    y_sign = jnp.where(row_left, conv_scale, jnp.where(row_right, -conv_scale, 0.0))
    damp = [1.0 / (1.0 + PENALTY * solid[PY * e : PY * (e + 1)]) for e in range(EX)]
    for t in range(TILES):
        point = lax.rem(lane + 128 * t, 5)
        z_left = point == 0
        z_face = jnp.where(z_left | (point == 4), conv_scale, 0.0)
        z_sign = jnp.where(z_left, conv_scale, jnp.where(point == 4, -conv_scale, 0.0))
        here = slice(128 + 128 * t, 256 + 128 * t)
        before = slice(128 * t, 128 + 128 * t)
        after = slice(256 + 128 * t, 384 + 128 * t)
        out = slice(128 * t, 128 + 128 * t)
        for x in range(BX):
            a = [V[c, x + 1, :, here] for c in range(3)]
            total = [conv[c, x, :, out] for c in range(3)]
            w = []
            for c in range(3):
                lo = pltpu.roll(jnp.where(lane == 127, V[c, x + 1, :, before], a[c]), 1, 1)
                hi = pltpu.roll(jnp.where(lane == 0, V[c, x + 1, :, after], a[c]), 127, 1)
                w.append(jnp.where(z_left, lo, hi))
            p = z_face * jnp.maximum(jnp.abs(a[2]), jnp.abs(w[2]))
            q = p + z_sign * w[2]
            total = [total[c] + (p * a[c] - q * w[c]) for c in range(3)]
            w = [
                jnp.where(row_left, pltpu.roll(a[c], 1, 0), pltpu.roll(a[c], PY - 1, 0))
                for c in range(3)
            ]
            p = y_face * jnp.maximum(jnp.abs(a[1]), jnp.abs(w[1]))
            q = p + y_sign * w[1]
            total = [total[c] + (p * a[c] - q * w[c]) for c in range(3)]
            if x % 5 in (0, 4):
                sign = 1.0 if x % 5 == 0 else -1.0
                w = [V[c, x if x % 5 == 0 else x + 2, :, here] for c in range(3)]
                p = conv_scale * jnp.maximum(jnp.abs(a[0]), jnp.abs(w[0]))
                q = p + (sign * conv_scale) * w[0]
                total = [total[c] + (p * a[c] - q * w[c]) for c in range(3)]
            factor = damp[x // 5][:, out]
            for c in range(3):
                prov[c, x, :, out] = (a[c] + total[c]) * factor

    for q in range(BX // 2):
        for c in range(3):
            hi, lo = split(prov[c, 2 * q : 2 * q + 2].reshape(2 * PY, BZ))
            PH[c, 2 * PY * q : 2 * PY * (q + 1), :] = hi
            PL[c, 2 * PY * q : 2 * PY * (q + 1), :] = lo
    first = [1.0 - flag(name, True) for name in ("gx", "gy", "gz")]
    x_low, y_low, z_low = (flag(name, True) for name in ("gx", "gy", "gz"))
    x_high, y_high, z_high = (flag(name, False) for name in ("gx", "gy", "gz"))
    parts = []
    c0, c1, c2, d0, d1 = (
        sum(part.astype(F32) for part in packed.get(weights, n)) for n in ("c0", "c1", "c2", "d0", "d1")
    )
    for c, m in enumerate((c0 + first[0] * d0, c1 + first[1] * d1, c2)):
        hi, lo = split(m)
        parts.append(dot(hi, PH[c]) + dot(lo, PH[c]) + dot(hi, PL[c]))
    hi, lo = split(parts[0] + parts[1])
    coarse = right_dot(hi, lo, packed.get(weights, "hz"))
    hi, lo = split(parts[2])
    coarse = coarse + right_dot(hi, lo, packed.get(weights, "gz"))
    lane16 = lax.broadcasted_iota(jnp.int32, (16, 128), 1)
    vertices = coarse[:, 0:128] - jnp.where(
        lane16 == 0, (0.5 * LIFT * 0.1) * first[2] * parts[2][:, 0:128], 0.0
    )
    row16 = lax.broadcasted_iota(jnp.int32, (16, 128), 0)
    there = jnp.where(row16 >= 10, x_high, 1.0) * jnp.where(lax.rem(row16, 5) == 4, y_high, 1.0)
    vertices = vertices * there
    edge = coarse[:, 128:256] * (there * z_high)
    edge_next = pltpu.roll(edge, 1, 1)
    own[...] = vertices

    xp[0:PY, :] = prov[0, BX - 1] * x_high
    xm[...] = prov[0, 0] * x_low
    xp[24:32, :] = jnp.zeros((8, BZ), F32)
    xp[24:29, 0:128] = vertices[10:15]
    xp[24:29, 128:256] = edge[10:15]
    yp[8:24, :] = jnp.zeros((16, BZ), F32)
    ym[8:16, :] = jnp.zeros((8, BZ), F32)
    lane24 = lax.broadcasted_iota(jnp.int32, (PY, 128), 1)
    low = jnp.zeros((PY, 128), F32)
    high = jnp.zeros((PY, 128), F32)
    for x in range(BX):
        yp[x : x + 1, :] = prov[1, x, BY - 1 : BY, :] * y_high
        ym[x : x + 1, :] = prov[1, x, 0:1, :] * y_low
        low = jnp.where(lane24 == x, jnp.broadcast_to(prov[2, x, :, 0:1], (PY, 128)), low)
        high = jnp.where(lane24 == x, jnp.broadcast_to(prov[2, x, :, BZ - 1 : BZ], (PY, 128)), high)
    yp[16:17, 0:128] = vertices[4:5]
    yp[17:18, 0:128] = vertices[9:10]
    yp[16:17, 128:256] = edge[4:5] + edge_next[9:10]
    zm[...] = low * z_low
    zp[...] = high * z_high
    zp[0:4, :] = zp[0:4, :] + (edge[0:4] + edge_next[5:9])


def right_kernel(packed, prov, PH, PL, weights, rhs):
    ry = packed.get(weights, "ry")
    for i, (n0, n1, k0, k1) in enumerate(WINDOWS):
        b = packed.get(weights, "rz" + str(i))
        y = left_dot(ry, PH[1, :, n0:n1], PL[1, :, n0:n1])
        z = right_dot(PH[2, :, k0:k1], PL[2, :, k0:k1], b)
        rhs[:, :, n0:n1] = (y + z).reshape(BX, PY, n1 - n0)

    def right_x(t, carry):
        dst = pl.ds(pl.multiple_of(128 * t, 128), 128)
        planes = [prov[0, x, :, dst] for x in range(BX)]
        outs = plane_sums(planes[:5], -1.0) + plane_sums(planes[5:], -1.0)
        outs[4] = outs[4] - 0.5 * LIFT * planes[5]
        outs[5] = outs[5] + 0.5 * LIFT * planes[4]
        for x in range(BX):
            rhs[x, :, dst] = rhs[x, :, dst] + outs[x]
        return carry

    lax.fori_loop(0, TILES, right_x, 0)


def spread_out(packed, weights, parts):
    rows_of = packed.get(weights, "rows_of")
    wide = []
    for i in range(3):
        m = packed.get(weights, "spread" + str(i))
        wide.append(sum(dot(part, m) for part in parts))
    return sum(dot(rows_of, part) for part in split(jnp.concatenate(wide, axis=1))[: len(parts)])


def smooth_kernel(
    packed, rhs, hx_lo, hx_hi, hy_lo, hy_hi, hz_lo, hz_hi, own, scale, weights, modes,
    smoothed, coarse, AH, AL, BH, BL,
):
    lift = 0.5 * LIFT
    lane = lax.broadcasted_iota(jnp.int32, (PY, 128), 1)
    row = lax.broadcasted_iota(jnp.int32, (PY, BZ), 0)
    for q in range(BX // 2):
        planes = []
        for x in (2 * q, 2 * q + 1):
            r = rhs[x]
            if x == 0:
                r = r + lift * hx_lo[0:PY, :]
            if x == BX - 1:
                r = r - lift * hx_hi[...]
            r = r + jnp.where(row == 0, lift * jnp.broadcast_to(hy_lo[x : x + 1, :], (PY, BZ)), 0.0)
            r = r - jnp.where(
                row == BY - 1, lift * jnp.broadcast_to(hy_hi[x : x + 1, :], (PY, BZ)), 0.0
            )
            left = r[:, 0:128] + jnp.where(
                lane == 0, lift * jnp.broadcast_to(hz_lo[:, x : x + 1], (PY, 128)), 0.0
            )
            right = r[:, BZ - 128 : BZ] - jnp.where(
                lane == 127, lift * jnp.broadcast_to(hz_hi[:, x : x + 1], (PY, 128)), 0.0
            )
            planes.append(jnp.concatenate([left, r[:, 128 : BZ - 128], right], axis=1))
        hi, lo = split(jnp.concatenate(planes, axis=0))
        AH[2 * PY * q : 2 * PY * (q + 1), :] = hi
        AL[2 * PY * q : 2 * PY * (q + 1), :] = lo

    for n0, n1, _, _ in WINDOWS:
        hi, lo = split(left_dot(packed.get(weights, "tf"), AH[:, n0:n1], AL[:, n0:n1]))
        BH[:, n0:n1] = hi
        BL[:, n0:n1] = lo

    factor = spread_out(packed, weights, split(scale[...].reshape(8, EZ)))
    values = eigen_value_table()
    for i, (n0, n1, k0, k1) in enumerate(WINDOWS):
        m = packed.get(weights, "sf" + str(i))
        c = right_dot(BH[:, k0:k1], BL[:, k0:k1], m).reshape(BX, PY, n1 - n0)
        done = []
        for x in range(BX):
            f = factor[PY * (x // 5) : PY * (x // 5 + 1), n0:n1]
            done.append(c[x] / (f * (modes[:, n0:n1] + float(values[x % 5])) + 1.0))
        hi, lo = split(jnp.concatenate(done, axis=0))
        AH[:, n0:n1] = hi
        AL[:, n0:n1] = lo

    for i, (n0, n1, k0, k1) in enumerate(WINDOWS):
        m = packed.get(weights, "sb" + str(i))
        hi, lo = split(right_dot(AH[:, k0:k1], AL[:, k0:k1], m))
        BH[:, n0:n1] = hi
        BL[:, n0:n1] = lo

    for n0, n1, _, _ in WINDOWS:
        c = left_dot(packed.get(weights, "tb"), BH[:, n0:n1], BL[:, n0:n1]).reshape(BX, PY, n1 - n0)
        smoothed[:, :, n0:n1] = c[:, 0:BY]

    lane4 = lax.broadcasted_iota(jnp.int32, (4, 128), 1)
    row4 = lax.broadcasted_iota(jnp.int32, (4, 128), 0)
    for vx in range(EX):
        total = own[5 * vx : 5 * vx + 4, :]
        if vx == 0:
            total = total + hx_lo[24:28, 0:128]
        total = total + jnp.where(
            row4 == 0, jnp.broadcast_to(hy_lo[16 + vx : 17 + vx, 0:128], (4, 128)), 0.0
        )
        k = ZEDGE + vx
        total = total + jnp.where(
            lane4 == 0, jnp.broadcast_to(hz_lo[0:4, k : k + 1], (4, 128)), 0.0
        )
        coarse[vx] = total


def constants():
    volume, lift, right, smooth = Packed(), Packed(), Packed(), Packed()
    eye_x = np.eye(BX)
    volume.add("my", pad_both(np.kron(eye_x, -STEP * line_operator(EY, False))))
    right.add("ry", pad_both(np.kron(eye_x, -line_operator(EY, True))))
    volume.add_windows("bz", -STEP * line_operator(EZ, False).T)
    right.add_windows("rz", -line_operator(EZ, True).T)
    basis = eigen_basis_table()
    sx = np.kron(np.eye(EX), basis)
    sy = np.kron(np.eye(EY), basis)
    sz = np.kron(np.eye(EZ), basis)
    t = np.kron(sx, sy)
    smooth.add("tf", pad_both(t.T))
    smooth.add("tb", pad_both(t))
    smooth.add_windows("sf", sz)
    smooth.add_windows("sb", sz.T)
    spread = np.kron(np.eye(EZ), np.ones((1, 5)))
    rows_of = np.zeros((EX * PY, 8))
    for e in range(EX):
        for y in range(BY):
            rows_of[PY * e + y, EY * e + y // 5] = 1.0
    for packed in (lift, smooth):
        packed.add("rows_of", rows_of, 1)
        for i, (n0, n1, _, _) in enumerate(WINDOWS):
            packed.add("spread" + str(i), spread[:, n0:n1], 1)
    values = eigen_value_table()
    modes = np.zeros((PY, BZ))
    for y in range(BY):
        modes[y] = values[y % 5] + np.tile(values, EZ)
    hx, hy, hz = hats_line(EX), hats_line(EY), hats_line(EZ)
    gx, gy, gz = slopes_line(EX), slopes_line(EY), slopes_line(EZ)
    for name, m in (("hz", hz), ("gz", gz)):
        wide = np.zeros((BZ, 256))
        wide[:, 0:EZ] = m[:EZ].T
        wide[:, 128 + ZEDGE] = m[EZ]
        lift.add(name, wide)
    half = 0.5 * LIFT * hat_weight_table()[0, 0]
    ex, ey = np.zeros_like(gx), np.zeros_like(gy)
    ex[0, 0] = -half
    ey[0, 0] = -half
    for name, m in (
        ("c0", np.kron(gx, hy)),
        ("c1", np.kron(hx, gy)),
        ("c2", np.kron(hx, hy)),
        ("d0", np.kron(ex, hy)),
        ("d1", np.kron(hx, ey)),
    ):
        lift.add(name, pad_to(pad_rows(-m), 16, ROWS))
    return volume, lift, right, smooth, modes.astype(np.float32)


def shift(x, axis, by):
    size = lax.axis_size(axis)
    return lax.ppermute(x, axis, [(i, (i + by) % size) for i in range(size)])


def like(*shape):
    return jax.ShapeDtypeStruct(shape, F32)


def run(kernel, outs, operands, scratch=(), name=None, flops=0):
    vmem = pl.BlockSpec(memory_space=pltpu.VMEM)
    return pl.pallas_call(
        kernel,
        out_shape=outs,
        in_specs=[vmem] * len(operands),
        out_specs=[vmem] * len(outs),
        scratch_shapes=list(scratch),
        compiler_params=pltpu.CompilerParams(vmem_limit_bytes=32 * 2**20),
        cost_estimate=pl.CostEstimate(flops=flops, bytes_accessed=4 << 20, transcendentals=0),
        name=name,
    )(*operands)


def shards(velocity, obstacle_element_mask, element_metric_scale):
    volume, lift, right, smooth, modes = constants()
    faces = run(
        pack_kernel,
        [like(3, PY, BZ)] * 2 + [like(3, BX, BZ)] * 2 + [like(PY, 128)] * 2,
        [velocity],
        name="pack",
        flops=10**10,
    )
    halo = [
        shift(faces[1], "gx", 1),
        shift(faces[0], "gx", -1),
        shift(faces[3], "gy", 1),
        shift(faces[2], "gy", -1),
        shift(faces[5], "gz", 1),
    ]
    halo[0], last = lax.optimization_barrier((halo[0], faces[4]))
    halo.append(shift(last, "gz", -1))
    field = like(3, BX, PY, BZ)
    half = jax.ShapeDtypeStruct((3, ROWS, BZ), BF16)
    (conv,) = run(
        functools.partial(volume_kernel, volume),
        [field],
        [velocity, faces[4], volume.array()],
        scratch=[pltpu.VMEM((3, BX, PY, BZ), F32)] + [pltpu.VMEM((5, ROWS, BZ), BF16)] * 2,
        name="volume",
        flops=4 * 10**9,
    )
    prov, ph, plo, xp, xm, yp, ym, zp, zm, own = run(
        functools.partial(lift_kernel, lift),
        [field, half, half]
        + [like(32, BZ), like(PY, BZ), like(24, BZ), like(16, BZ), like(PY, 128), like(PY, 128)]
        + [like(16, 128)],
        [velocity, conv, *halo, obstacle_element_mask, lift.array()],
        scratch=[pltpu.VMEM((3, BX + 2, PY, 896), F32)],
        name="lift",
        flops=4 * 10**9,
    )
    (rhs,) = run(
        functools.partial(right_kernel, right),
        [like(BX, PY, BZ)],
        [prov, ph, plo, right.array()],
        name="right",
        flops=2 * 10**9,
    )
    gx_lo = shift(xp, "gx", 1)
    gx_hi = shift(xm, "gx", -1)
    yp = yp + jnp.pad(gx_lo[28:29, 0:256], ((16, 7), (0, BZ - 256)))
    gy_lo = shift(yp, "gy", 1)
    gy_hi = shift(ym, "gy", -1)
    zp = zp + jnp.pad(gx_lo[24:28, 128:256], ((0, 20), (0, 0)))
    zp = zp + jnp.pad(gy_lo[16:17, 128:256], ((0, 23), (0, 0)))
    gz_lo = shift(zp, "gz", 1)
    gz_hi = shift(zm, "gz", -1)
    smoothed, coarse = run(
        functools.partial(smooth_kernel, smooth),
        [like(BX, BY, BZ), like(EX, EY, EZ)],
        [rhs, gx_lo, gx_hi, gy_lo, gy_hi, gz_lo, gz_hi, own, element_metric_scale]
        + [smooth.array(), jnp.asarray(modes)],
        scratch=[pltpu.VMEM((ROWS, BZ), BF16)] * 4,
        name="smooth",
        flops=3 * 10**9,
    )
    return (smoothed, coarse)


def solution(mesh):
    return jax.shard_map(
        shards,
        mesh=mesh,
        in_specs=(P(None, "gx", "gy", "gz"), P("gx", "gy", "gz"), P("gx", "gy", "gz")),
        out_specs=(P("gx", "gy", "gz"), P("gx", "gy", "gz")),
        check_vma=False,
    )
```

```python
import functools
import math

import jax
import jax.numpy as jnp
import ml_dtypes
import numpy as np
from jax import lax
from jax.experimental import pallas as pl
from jax.experimental.pallas import tpu as pltpu
from jax.sharding import PartitionSpec as P

LIFT = 10.0
STEP = 0.05
PENALTY = 4.0

BX, BY, BZ = 10, 20, 640
EX, EY, EZ = 2, 4, 128
PY = 24
ROWS = BX * PY
TILES = BZ // 128
WINDOWS = ((0, 256, 0, 384), (256, 512, 128, 640), (512, 640, 384, 640))
ZEDGE = 16

F32 = jnp.float32
BF16 = jnp.bfloat16


def lobatto_points():
    return np.array([-1.0, -math.sqrt(3.0 / 7.0), 0.0, math.sqrt(3.0 / 7.0), 1.0])


def lobatto_weights():
    return np.array([0.1, 49.0 / 90.0, 32.0 / 45.0, 49.0 / 90.0, 0.1])


def derivative_matrix():
    points = lobatto_points()
    scales = np.array(
        [np.prod([points[i] - points[k] for k in range(5) if k != i]) for i in range(5)]
    )
    result = np.zeros((5, 5))
    for i in range(5):
        for j in range(5):
            if i != j:
                result[i, j] = scales[i] / (scales[j] * (points[i] - points[j]))
        result[i, i] = -np.sum(result[i])
    return result


def eigen_basis_table():
    return np.array(
        [
            [
                math.sqrt((1.0 if k == 0 else 2.0) / 5.0) * math.cos(math.pi * (i + 0.5) * k / 5.0)
                for k in range(5)
            ]
            for i in range(5)
        ]
    )


def eigen_value_table():
    return np.array([4.0 * math.sin(math.pi * k / 10.0) ** 2 for k in range(5)])


def hat_weight_table():
    points = lobatto_points()
    weights = lobatto_weights()
    return np.array([weights * (1.0 - points) / 2.0, weights * (1.0 + points) / 2.0])


def inner_matrix():
    result = derivative_matrix()
    result[0, 0] += 0.5 * LIFT
    result[4, 4] -= 0.5 * LIFT
    return result


def line_operator(elements, coupled):
    inner = inner_matrix()
    size = 5 * elements
    m = np.zeros((size, size))
    for e in range(elements):
        m[5 * e : 5 * e + 5, 5 * e : 5 * e + 5] = inner
        if coupled and e > 0:
            m[5 * e, 5 * e - 1] = -0.5 * LIFT
        if coupled and e < elements - 1:
            m[5 * e + 4, 5 * e + 5] = 0.5 * LIFT
    return m


def hats_line(elements):
    h = hat_weight_table()
    m = np.zeros((elements + 1, 5 * elements))
    for e in range(elements):
        m[e, 5 * e : 5 * e + 5] += h[0]
        m[e + 1, 5 * e : 5 * e + 5] += h[1]
    return m


def slopes_line(elements):
    h = hat_weight_table()
    d = derivative_matrix()
    g = h @ d
    g[0, 0] += LIFT * h[0, 0]
    g[1, 4] -= LIFT * h[1, 4]
    m = np.zeros((elements + 1, 5 * elements))
    for e in range(elements):
        m[e, 5 * e : 5 * e + 5] += g[0]
        m[e + 1, 5 * e : 5 * e + 5] += g[1]
    return m


def pad_rows(m):
    out = np.zeros((m.shape[0], BX, PY))
    out[:, :, :BY] = m.reshape(m.shape[0], BX, BY)
    return out.reshape(m.shape[0], ROWS)


def pad_both(m):
    return pad_rows(pad_rows(m).T).T


def pad_to(m, rows, columns):
    out = np.zeros((rows, columns))
    out[: m.shape[0], : m.shape[1]] = m
    return out


class Packed:

    def __init__(self):
        self.parts = []
        self.places = {}
        self.rows = 0

    def add(self, name, m, parts=2):
        m = np.asarray(m, np.float64)
        hi = m.astype(np.float32).astype(ml_dtypes.bfloat16)
        lo = (m - hi.astype(np.float64)).astype(np.float32).astype(ml_dtypes.bfloat16)
        places = []
        for part in (hi, lo)[:parts]:
            wide = np.zeros((part.shape[0], 256), ml_dtypes.bfloat16)
            wide[:, : part.shape[1]] = part
            places.append((self.rows, part.shape[0], part.shape[1]))
            self.parts.append(wide)
            self.rows += part.shape[0]
        self.places[name] = places

    def add_windows(self, name, m):
        for i, (n0, n1, k0, k1) in enumerate(WINDOWS):
            self.add(name + str(i), m[k0:k1, n0:n1])

    def array(self):
        return jnp.asarray(np.concatenate(self.parts))

    def both(self, ref, name):
        r, n, c = self.places[name][0]
        return ref[r : r + 2 * n, 0:c]

    def get(self, ref, name):
        out = [ref[r : r + n, 0:c] for r, n, c in self.places[name]]
        return out[0] if len(out) == 1 else out


def split(x):
    hi = x.astype(BF16)
    return hi, (x - hi.astype(F32)).astype(BF16)


def stacked(x):
    return jnp.concatenate(split(x), axis=0)


def dot(a, b):
    return jnp.dot(a, b, preferred_element_type=F32)


def left_dot(m, hi, lo):
    rows = m.shape[0] // 2
    both = dot(m, hi)
    return both[:rows] + both[rows:] + dot(m[:rows], lo)


def right_dot(hi, lo, m):
    return dot(hi, m[0]) + dot(lo, m[0]) + dot(hi, m[1])


def stack_dot(x, m):
    rows = x.shape[0] // 2
    both = dot(x, m[0])
    return both[:rows] + both[rows:] + dot(x[:rows], m[1])


def flag(name, low):
    edge = 0 if low else lax.axis_size(name) - 1
    return jnp.where(lax.axis_index(name) == edge, 0.0, 1.0)


def pack_kernel(v, y_lo, y_hi, z_lo, z_hi):
    y_low, y_high = flag("gy", True), flag("gy", False)
    lane = lax.broadcasted_iota(jnp.int32, (BY, 128), 1)
    low = jnp.zeros((BY, 128), F32)
    high = jnp.zeros((BY, 128), F32)
    for c in range(3):
        for x in range(BX):
            y_lo[BX * c + x : BX * c + x + 1, :] = v[c, x, 0:1, :] * y_low
            y_hi[BX * c + x : BX * c + x + 1, :] = v[c, x, BY - 1 : BY, :] * y_high
            here = lane == 16 * c + x
            low = jnp.where(here, jnp.broadcast_to(v[c, x, :, 0:1], (BY, 128)), low)
            high = jnp.where(here, jnp.broadcast_to(v[c, x, :, BZ - 1 : BZ], (BY, 128)), high)
    z_lo[0:BY, :] = low * flag("gz", True)
    z_hi[0:BY, :] = high * flag("gz", False)
    z_lo[BY:PY, :] = jnp.zeros((PY - BY, 128), F32)
    z_hi[BY:PY, :] = jnp.zeros((PY - BY, 128), F32)


def plane_sums(planes, scale):
    d = inner_matrix() * scale
    outs = []
    for i in range(5):
        total = None
        for j in range(5):
            if abs(d[i, j]) < 1e-12:
                continue
            term = float(d[i, j]) * planes[j]
            total = term if total is None else total + term
        outs.append(total)
    return outs


def volume_kernel(packed, v, after, weights, conv, V, FH, FL):
    del after
    for c in range(3):
        for x in range(BX):
            V[c, x, 0:BY, :] = v[c, x]
            V[c, x, BY:PY, :] = jnp.zeros((PY - BY, BZ), F32)

    def products(t, carry):
        dst = pl.ds(pl.multiple_of(128 * t, 128), 128)
        for q in range(BX // 2):
            a = [V[c, 2 * q : 2 * q + 2, :, dst].reshape(2 * PY, 128) for c in range(3)]
            pairs = (a[0] * a[1], a[1] * a[1], a[1] * a[2], a[0] * a[2], a[2] * a[2])
            for f, value in enumerate(pairs):
                hi, lo = split(value)
                FH[f, 2 * PY * q : 2 * PY * (q + 1), dst] = hi
                FL[f, 2 * PY * q : 2 * PY * (q + 1), dst] = lo
        return carry

    lax.fori_loop(0, TILES, products, 0)

    my = packed.both(weights, "my")
    for i, (n0, n1, k0, k1) in enumerate(WINDOWS):
        high = FH[2:5, :, k0:k1].reshape(3 * ROWS, k1 - k0)
        low = FL[2:5, :, k0:k1].reshape(3 * ROWS, k1 - k0)
        z = right_dot(high, low, packed.get(weights, "bz" + str(i)))
        for c in range(3):
            along_z = ROWS * (1, 0, 2)[c]
            y = left_dot(my, FH[c, :, n0:n1], FL[c, :, n0:n1])
            total = y + z[along_z : along_z + ROWS]
            conv[c, :, :, n0:n1] = total.reshape(BX, PY, n1 - n0)

    def along_x(t, carry):
        dst = pl.ds(pl.multiple_of(128 * t, 128), 128)
        for e in range(EX):
            v0 = [V[0, 5 * e + i, :, dst] for i in range(5)]
            for c in range(3):
                flux = [v0[i] * V[c, 5 * e + i, :, dst] for i in range(5)]
                for i, total in enumerate(plane_sums(flux, -STEP)):
                    conv[c, 5 * e + i, :, dst] = conv[c, 5 * e + i, :, dst] + total
        return carry

    lax.fori_loop(0, TILES, along_x, 0)


def lift_kernel(
    packed, v, conv, hx_lo, hx_hi, hy_lo, hy_hi, hz_lo, hz_hi, mask, weights,
    prov, PH, PL, xp, xm, yp, ym, zp, zm, own, V,
):
    for c in range(3):
        V[c, 0, 0:BY, 128:768] = hx_lo[c] * flag("gx", True)
        V[c, BX + 1, 0:BY, 128:768] = hx_hi[c] * flag("gx", False)
        V[c, 0, BY:PY, 128:768] = jnp.zeros((PY - BY, BZ), F32)
        V[c, BX + 1, BY:PY, 128:768] = jnp.zeros((PY - BY, BZ), F32)
        for x in range(BX):
            r = BX * c + x
            V[c, x + 1, 0:BY, 128:768] = v[c, x]
            V[c, x + 1, 20:22, 128:768] = jnp.broadcast_to(hy_hi[r : r + 1, :], (2, BZ))
            V[c, x + 1, 22:24, 128:768] = jnp.broadcast_to(hy_lo[r : r + 1, :], (2, BZ))
            k = 16 * c + x
            V[c, x + 1, :, 0:128] = jnp.broadcast_to(hz_lo[:, k : k + 1], (PY, 128))
            V[c, x + 1, :, 768:896] = jnp.broadcast_to(hz_hi[:, k : k + 1], (PY, 128))

    solid = spread_out(packed, weights, [mask[...].astype(F32).reshape(8, EZ).astype(BF16)])
    conv_scale = -0.5 * LIFT * STEP
    lane = lax.broadcasted_iota(jnp.int32, (PY, 128), 1)
    row = lax.broadcasted_iota(jnp.int32, (PY, 128), 0)
    row_left = (lax.rem(row, 5) == 0) & (row < BY)
    row_right = (lax.rem(row, 5) == 4) & (row < BY)
    y_face = jnp.where(row_left | row_right, conv_scale, 0.0)
    y_sign = jnp.where(row_left, conv_scale, jnp.where(row_right, -conv_scale, 0.0))
    damp = [1.0 / (1.0 + PENALTY * solid[PY * e : PY * (e + 1)]) for e in range(EX)]
    for t in range(TILES):
        point = lax.rem(lane + 128 * t, 5)
        z_left = point == 0
        z_face = jnp.where(z_left | (point == 4), conv_scale, 0.0)
        z_sign = jnp.where(z_left, conv_scale, jnp.where(point == 4, -conv_scale, 0.0))
        here = slice(128 + 128 * t, 256 + 128 * t)
        before = slice(128 * t, 128 + 128 * t)
        after = slice(256 + 128 * t, 384 + 128 * t)
        out = slice(128 * t, 128 + 128 * t)
        for x in range(BX):
            a = [V[c, x + 1, :, here] for c in range(3)]
            total = [conv[c, x, :, out] for c in range(3)]
            w = []
            for c in range(3):
                lo = pltpu.roll(jnp.where(lane == 127, V[c, x + 1, :, before], a[c]), 1, 1)
                hi = pltpu.roll(jnp.where(lane == 0, V[c, x + 1, :, after], a[c]), 127, 1)
                w.append(jnp.where(z_left, lo, hi))
            p = z_face * jnp.maximum(jnp.abs(a[2]), jnp.abs(w[2]))
            q = p + z_sign * w[2]
            total = [total[c] + (p * a[c] - q * w[c]) for c in range(3)]
            w = [
                jnp.where(row_left, pltpu.roll(a[c], 1, 0), pltpu.roll(a[c], PY - 1, 0))
                for c in range(3)
            ]
            p = y_face * jnp.maximum(jnp.abs(a[1]), jnp.abs(w[1]))
            q = p + y_sign * w[1]
            total = [total[c] + (p * a[c] - q * w[c]) for c in range(3)]
            if x % 5 in (0, 4):
                sign = 1.0 if x % 5 == 0 else -1.0
                w = [V[c, x if x % 5 == 0 else x + 2, :, here] for c in range(3)]
                p = conv_scale * jnp.maximum(jnp.abs(a[0]), jnp.abs(w[0]))
                q = p + (sign * conv_scale) * w[0]
                total = [total[c] + (p * a[c] - q * w[c]) for c in range(3)]
            factor = damp[x // 5][:, out]
            for c in range(3):
                prov[c, x, :, out] = (a[c] + total[c]) * factor

    for q in range(BX // 2):
        for c in range(3):
            hi, lo = split(prov[c, 2 * q : 2 * q + 2].reshape(2 * PY, BZ))
            PH[c, 2 * PY * q : 2 * PY * (q + 1), :] = hi
            PL[c, 2 * PY * q : 2 * PY * (q + 1), :] = lo
    first = [1.0 - flag(name, True) for name in ("gx", "gy", "gz")]
    x_low, y_low, z_low = (flag(name, True) for name in ("gx", "gy", "gz"))
    x_high, y_high, z_high = (flag(name, False) for name in ("gx", "gy", "gz"))
    parts = []
    c0, c1, c2, d0, d1 = (
        sum(part.astype(F32) for part in packed.get(weights, n)) for n in ("c0", "c1", "c2", "d0", "d1")
    )
    for c, m in enumerate((c0 + first[0] * d0, c1 + first[1] * d1, c2)):
        parts.append(left_dot(stacked(m), PH[c], PL[c]))
    coarse = stack_dot(stacked(parts[0] + parts[1]), packed.get(weights, "hz"))
    coarse = coarse + stack_dot(stacked(parts[2]), packed.get(weights, "gz"))
    lane16 = lax.broadcasted_iota(jnp.int32, (16, 128), 1)
    vertices = coarse[:, 0:128] - jnp.where(
        lane16 == 0, (0.5 * LIFT * 0.1) * first[2] * parts[2][:, 0:128], 0.0
    )
    row16 = lax.broadcasted_iota(jnp.int32, (16, 128), 0)
    there = jnp.where(row16 >= 10, x_high, 1.0) * jnp.where(lax.rem(row16, 5) == 4, y_high, 1.0)
    vertices = vertices * there
    edge = coarse[:, 128:256] * (there * z_high)
    edge_next = pltpu.roll(edge, 1, 1)
    own[...] = vertices

    xp[0:PY, :] = prov[0, BX - 1] * x_high
    xm[...] = prov[0, 0] * x_low
    xp[BY:PY, :] = jnp.zeros((PY - BY, BZ), F32)
    xp[20:24, 0:128] = vertices[10:14]
    xp[20:24, 128:256] = edge[10:14]
    xp[20:21, 256:384] = vertices[14:15]
    xp[20:21, 384:512] = edge[14:15]
    yp[8:16, :] = jnp.zeros((8, BZ), F32)
    ym[8:16, :] = jnp.zeros((8, BZ), F32)
    lane24 = lax.broadcasted_iota(jnp.int32, (PY, 128), 1)
    low = jnp.zeros((PY, 128), F32)
    high = jnp.zeros((PY, 128), F32)
    for x in range(BX):
        yp[x : x + 1, :] = prov[1, x, BY - 1 : BY, :] * y_high
        ym[x : x + 1, :] = prov[1, x, 0:1, :] * y_low
        low = jnp.where(lane24 == x, jnp.broadcast_to(prov[2, x, :, 0:1], (PY, 128)), low)
        high = jnp.where(lane24 == x, jnp.broadcast_to(prov[2, x, :, BZ - 1 : BZ], (PY, 128)), high)
    yp[10:11, 0:128] = vertices[4:5]
    yp[11:12, 0:128] = vertices[9:10]
    yp[10:11, 128:256] = edge[4:5] + edge_next[9:10]
    zm[...] = low * z_low
    zp[...] = high * z_high
    zp[0:4, :] = zp[0:4, :] + (edge[0:4] + edge_next[5:9])


def right_kernel(packed, prov, PH, PL, weights, rhs):
    ry = packed.both(weights, "ry")
    for i, (n0, n1, k0, k1) in enumerate(WINDOWS):
        b = packed.get(weights, "rz" + str(i))
        y = left_dot(ry, PH[1, :, n0:n1], PL[1, :, n0:n1])
        z = right_dot(PH[2, :, k0:k1], PL[2, :, k0:k1], b)
        rhs[:, :, n0:n1] = (y + z).reshape(BX, PY, n1 - n0)

    def right_x(t, carry):
        dst = pl.ds(pl.multiple_of(128 * t, 128), 128)
        planes = [prov[0, x, :, dst] for x in range(BX)]
        outs = plane_sums(planes[:5], -1.0) + plane_sums(planes[5:], -1.0)
        outs[4] = outs[4] - 0.5 * LIFT * planes[5]
        outs[5] = outs[5] + 0.5 * LIFT * planes[4]
        for x in range(BX):
            rhs[x, :, dst] = rhs[x, :, dst] + outs[x]
        return carry

    lax.fori_loop(0, TILES, right_x, 0)


def spread_out(packed, weights, parts):
    rows_of = packed.get(weights, "rows_of")
    wide = []
    for i in range(3):
        m = packed.get(weights, "spread" + str(i))
        wide.append(sum(dot(part, m) for part in parts))
    return sum(dot(rows_of, part) for part in split(jnp.concatenate(wide, axis=1))[: len(parts)])


def smooth_kernel(
    packed, rhs, hx_lo, hx_hi, hy_lo, hy_hi, hz_lo, hz_hi, own, scale, weights, modes,
    smoothed, coarse, A, B,
):
    lift = 0.5 * LIFT
    lane = lax.broadcasted_iota(jnp.int32, (PY, 128), 1)
    row = lax.broadcasted_iota(jnp.int32, (PY, BZ), 0)
    for q in range(BX // 2):
        planes = []
        for x in (2 * q, 2 * q + 1):
            r = rhs[x]
            if x == 0:
                r = r + lift * hx_lo[...]
            if x == BX - 1:
                r = r - lift * hx_hi[...]
            r = r + jnp.where(row == 0, lift * jnp.broadcast_to(hy_lo[x : x + 1, :], (PY, BZ)), 0.0)
            r = r - jnp.where(
                row == BY - 1, lift * jnp.broadcast_to(hy_hi[x : x + 1, :], (PY, BZ)), 0.0
            )
            left = r[:, 0:128] + jnp.where(
                lane == 0, lift * jnp.broadcast_to(hz_lo[:, x : x + 1], (PY, 128)), 0.0
            )
            right = r[:, BZ - 128 : BZ] - jnp.where(
                lane == 127, lift * jnp.broadcast_to(hz_hi[:, x : x + 1], (PY, 128)), 0.0
            )
            planes.append(jnp.concatenate([left, r[:, 128 : BZ - 128], right], axis=1))
        hi, lo = split(jnp.concatenate(planes, axis=0))
        A[2 * PY * q : 2 * PY * (q + 1), :] = hi
        A[ROWS + 2 * PY * q : ROWS + 2 * PY * (q + 1), :] = lo

    tf = packed.both(weights, "tf")
    for n0, n1, _, _ in WINDOWS:
        B[:, n0:n1] = stacked(left_dot(tf, A[0:ROWS, n0:n1], A[ROWS:, n0:n1]))

    factor = spread_out(packed, weights, split(scale[...].reshape(8, EZ)))
    values = eigen_value_table()
    for i, (n0, n1, k0, k1) in enumerate(WINDOWS):
        c = stack_dot(B[:, k0:k1], packed.get(weights, "sf" + str(i))).reshape(BX, PY, n1 - n0)
        done = []
        for x in range(BX):
            f = factor[PY * (x // 5) : PY * (x // 5 + 1), n0:n1]
            done.append(c[x] / (f * (modes[:, n0:n1] + float(values[x % 5])) + 1.0))
        A[:, n0:n1] = stacked(jnp.concatenate(done, axis=0))

    for i, (n0, n1, k0, k1) in enumerate(WINDOWS):
        B[:, n0:n1] = stacked(stack_dot(A[:, k0:k1], packed.get(weights, "sb" + str(i))))

    tb = packed.both(weights, "tb")
    for n0, n1, _, _ in WINDOWS:
        c = left_dot(tb, B[0:ROWS, n0:n1], B[ROWS:, n0:n1]).reshape(BX, PY, n1 - n0)
        smoothed[:, :, n0:n1] = c[:, 0:BY]

    lane4 = lax.broadcasted_iota(jnp.int32, (4, 128), 1)
    row4 = lax.broadcasted_iota(jnp.int32, (4, 128), 0)
    for vx in range(EX):
        total = own[5 * vx : 5 * vx + 4, :]
        if vx == 0:
            total = total + hx_lo[20:24, 0:128]
        total = total + jnp.where(
            row4 == 0, jnp.broadcast_to(hy_lo[10 + vx : 11 + vx, 0:128], (4, 128)), 0.0
        )
        k = ZEDGE + vx
        total = total + jnp.where(
            lane4 == 0, jnp.broadcast_to(hz_lo[0:4, k : k + 1], (4, 128)), 0.0
        )
        coarse[vx] = total


def constants():
    volume, lift, right, smooth = Packed(), Packed(), Packed(), Packed()
    eye_x = np.eye(BX)
    volume.add("my", pad_both(np.kron(eye_x, -STEP * line_operator(EY, False))))
    right.add("ry", pad_both(np.kron(eye_x, -line_operator(EY, True))))
    volume.add_windows("bz", -STEP * line_operator(EZ, False).T)
    right.add_windows("rz", -line_operator(EZ, True).T)
    basis = eigen_basis_table()
    sx = np.kron(np.eye(EX), basis)
    sy = np.kron(np.eye(EY), basis)
    sz = np.kron(np.eye(EZ), basis)
    t = np.kron(sx, sy)
    smooth.add("tf", pad_both(t.T))
    smooth.add("tb", pad_both(t))
    smooth.add_windows("sf", sz)
    smooth.add_windows("sb", sz.T)
    spread = np.kron(np.eye(EZ), np.ones((1, 5)))
    rows_of = np.zeros((EX * PY, 8))
    for e in range(EX):
        for y in range(BY):
            rows_of[PY * e + y, EY * e + y // 5] = 1.0
    for packed in (lift, smooth):
        packed.add("rows_of", rows_of, 1)
        for i, (n0, n1, _, _) in enumerate(WINDOWS):
            packed.add("spread" + str(i), spread[:, n0:n1], 1)
    values = eigen_value_table()
    modes = np.zeros((PY, BZ))
    for y in range(BY):
        modes[y] = values[y % 5] + np.tile(values, EZ)
    hx, hy, hz = hats_line(EX), hats_line(EY), hats_line(EZ)
    gx, gy, gz = slopes_line(EX), slopes_line(EY), slopes_line(EZ)
    for name, m in (("hz", hz), ("gz", gz)):
        wide = np.zeros((BZ, 256))
        wide[:, 0:EZ] = m[:EZ].T
        wide[:, 128 + ZEDGE] = m[EZ]
        lift.add(name, wide)
    half = 0.5 * LIFT * hat_weight_table()[0, 0]
    ex, ey = np.zeros_like(gx), np.zeros_like(gy)
    ex[0, 0] = -half
    ey[0, 0] = -half
    for name, m in (
        ("c0", np.kron(gx, hy)),
        ("c1", np.kron(hx, gy)),
        ("c2", np.kron(hx, hy)),
        ("d0", np.kron(ex, hy)),
        ("d1", np.kron(hx, ey)),
    ):
        lift.add(name, pad_to(pad_rows(-m), 16, ROWS))
    return volume, lift, right, smooth, modes.astype(np.float32)


def shift(x, axis, by):
    size = lax.axis_size(axis)
    return lax.ppermute(x, axis, [(i, (i + by) % size) for i in range(size)])


def like(*shape):
    return jax.ShapeDtypeStruct(shape, F32)


def run(kernel, outs, operands, scratch=(), name=None, flops=0):
    vmem = pl.BlockSpec(memory_space=pltpu.VMEM)
    return pl.pallas_call(
        kernel,
        out_shape=outs,
        in_specs=[vmem] * len(operands),
        out_specs=[vmem] * len(outs),
        scratch_shapes=list(scratch),
        compiler_params=pltpu.CompilerParams(vmem_limit_bytes=32 * 2**20),
        cost_estimate=pl.CostEstimate(flops=flops, bytes_accessed=4 << 20, transcendentals=0),
        name=name,
    )(*operands)


def shards(velocity, obstacle_element_mask, element_metric_scale):
    volume, lift, right, smooth, modes = constants()
    faces = run(
        pack_kernel,
        [like(3 * BX, BZ)] * 2 + [like(PY, 128)] * 2,
        [velocity],
        name="pack",
        flops=10**10,
    )
    halo = [
        shift(velocity[:, BX - 1], "gx", 1),
        shift(velocity[:, 0], "gx", -1),
        shift(faces[1], "gy", 1),
        shift(faces[0], "gy", -1),
        shift(faces[3], "gz", 1),
    ]
    halo[0], last = lax.optimization_barrier((halo[0], faces[2]))
    halo.append(shift(last, "gz", -1))
    field = like(3, BX, PY, BZ)
    half = jax.ShapeDtypeStruct((3, ROWS, BZ), BF16)
    (conv,) = run(
        functools.partial(volume_kernel, volume),
        [field],
        [velocity, faces[2], volume.array()],
        scratch=[pltpu.VMEM((3, BX, PY, BZ), F32)] + [pltpu.VMEM((5, ROWS, BZ), BF16)] * 2,
        name="volume",
        flops=4 * 10**9,
    )
    prov, ph, plo, xp, xm, yp, ym, zp, zm, own = run(
        functools.partial(lift_kernel, lift),
        [field, half, half]
        + [like(PY, BZ), like(PY, BZ), like(16, BZ), like(16, BZ), like(PY, 128), like(PY, 128)]
        + [like(16, 128)],
        [velocity, conv, *halo, obstacle_element_mask, lift.array()],
        scratch=[pltpu.VMEM((3, BX + 2, PY, 896), F32)],
        name="lift",
        flops=4 * 10**9,
    )
    (rhs,) = run(
        functools.partial(right_kernel, right),
        [like(BX, PY, BZ)],
        [prov, ph, plo, right.array()],
        name="right",
        flops=2 * 10**9,
    )
    gx_lo = shift(xp, "gx", 1)
    gz_hi = shift(zm, "gz", -1)
    gx_lo, gz_hi = lax.optimization_barrier((gx_lo, gz_hi))
    gx_hi = shift(xm, "gx", -1)
    yp = yp + jnp.pad(gx_lo[20:21, 256:512], ((10, 5), (0, BZ - 256)))
    gy_lo = shift(yp, "gy", 1)
    gy_hi = shift(ym, "gy", -1)
    zp = zp + jnp.pad(gx_lo[20:24, 128:256], ((0, 20), (0, 0)))
    zp = zp + jnp.pad(gy_lo[10:11, 128:256], ((0, 23), (0, 0)))
    gz_lo = shift(zp, "gz", 1)
    smoothed, coarse = run(
        functools.partial(smooth_kernel, smooth),
        [like(BX, BY, BZ), like(EX, EY, EZ)],
        [rhs, gx_lo, gx_hi, gy_lo, gy_hi, gz_lo, gz_hi, own, element_metric_scale]
        + [smooth.array(), jnp.asarray(modes)],
        scratch=[pltpu.VMEM((2 * ROWS, BZ), BF16)] * 2,
        name="smooth",
        flops=3 * 10**9,
    )
    return (smoothed, coarse)


def solution(mesh):
    return jax.shard_map(
        shards,
        mesh=mesh,
        in_specs=(P(None, "gx", "gy", "gz"), P("gx", "gy", "gz"), P("gx", "gy", "gz")),
        out_specs=(P("gx", "gy", "gz"), P("gx", "gy", "gz")),
        check_vma=False,
    )
```

```python
import functools
import math

import jax
import jax.numpy as jnp
import ml_dtypes
import numpy as np
from jax import lax
from jax.experimental import pallas as pl
from jax.experimental.pallas import tpu as pltpu
from jax.sharding import PartitionSpec as P

LIFT = 10.0
STEP = 0.05
PENALTY = 4.0

BX, BY, BZ = 10, 20, 640
EX, EY, EZ = 2, 4, 128
PY = 24
ROWS = BX * PY
TILES = BZ // 128
WINDOWS = ((0, 250, 0, 251), (250, 500, 249, 501), (500, 640, 499, 640))
LANES = ((0, 256), (256, 512), (512, 640))
ZEDGE = 16

F32 = jnp.float32
BF16 = jnp.bfloat16


def lobatto_points():
    return np.array([-1.0, -math.sqrt(3.0 / 7.0), 0.0, math.sqrt(3.0 / 7.0), 1.0])


def lobatto_weights():
    return np.array([0.1, 49.0 / 90.0, 32.0 / 45.0, 49.0 / 90.0, 0.1])


def derivative_matrix():
    points = lobatto_points()
    scales = np.array(
        [np.prod([points[i] - points[k] for k in range(5) if k != i]) for i in range(5)]
    )
    result = np.zeros((5, 5))
    for i in range(5):
        for j in range(5):
            if i != j:
                result[i, j] = scales[i] / (scales[j] * (points[i] - points[j]))
        result[i, i] = -np.sum(result[i])
    return result


def eigen_basis_table():
    return np.array(
        [
            [
                math.sqrt((1.0 if k == 0 else 2.0) / 5.0) * math.cos(math.pi * (i + 0.5) * k / 5.0)
                for k in range(5)
            ]
            for i in range(5)
        ]
    )


def eigen_value_table():
    return np.array([4.0 * math.sin(math.pi * k / 10.0) ** 2 for k in range(5)])


def hat_weight_table():
    points = lobatto_points()
    weights = lobatto_weights()
    return np.array([weights * (1.0 - points) / 2.0, weights * (1.0 + points) / 2.0])


def inner_matrix():
    result = derivative_matrix()
    result[0, 0] += 0.5 * LIFT
    result[4, 4] -= 0.5 * LIFT
    return result


def line_operator(elements, coupled):
    inner = inner_matrix()
    size = 5 * elements
    m = np.zeros((size, size))
    for e in range(elements):
        m[5 * e : 5 * e + 5, 5 * e : 5 * e + 5] = inner
        if coupled and e > 0:
            m[5 * e, 5 * e - 1] = -0.5 * LIFT
        if coupled and e < elements - 1:
            m[5 * e + 4, 5 * e + 5] = 0.5 * LIFT
    return m


def hats_line(elements):
    h = hat_weight_table()
    m = np.zeros((elements + 1, 5 * elements))
    for e in range(elements):
        m[e, 5 * e : 5 * e + 5] += h[0]
        m[e + 1, 5 * e : 5 * e + 5] += h[1]
    return m


def slopes_line(elements):
    h = hat_weight_table()
    d = derivative_matrix()
    g = h @ d
    g[0, 0] += LIFT * h[0, 0]
    g[1, 4] -= LIFT * h[1, 4]
    m = np.zeros((elements + 1, 5 * elements))
    for e in range(elements):
        m[e, 5 * e : 5 * e + 5] += g[0]
        m[e + 1, 5 * e : 5 * e + 5] += g[1]
    return m


def pad_rows(m):
    out = np.zeros((m.shape[0], BX, PY))
    out[:, :, :BY] = m.reshape(m.shape[0], BX, BY)
    return out.reshape(m.shape[0], ROWS)


def pad_both(m):
    return pad_rows(pad_rows(m).T).T


def pad_to(m, rows, columns):
    out = np.zeros((rows, columns))
    out[: m.shape[0], : m.shape[1]] = m
    return out


class Packed:

    def __init__(self):
        self.parts = []
        self.places = {}
        self.rows = 0

    def add(self, name, m, parts=2):
        m = np.asarray(m, np.float64)
        hi = m.astype(np.float32).astype(ml_dtypes.bfloat16)
        lo = (m - hi.astype(np.float64)).astype(np.float32).astype(ml_dtypes.bfloat16)
        places = []
        for part in (hi, lo)[:parts]:
            wide = np.zeros((part.shape[0], 256), ml_dtypes.bfloat16)
            wide[:, : part.shape[1]] = part
            places.append((self.rows, part.shape[0], part.shape[1]))
            self.parts.append(wide)
            self.rows += part.shape[0]
        self.places[name] = places

    def add_windows(self, name, m, coupled=True):
        for i, (n0, n1, k0, k1) in enumerate(WINDOWS):
            self.add(name + str(i), m[k0:k1, n0:n1] if coupled else m[n0:n1, n0:n1])

    def array(self):
        return jnp.asarray(np.concatenate(self.parts))

    def both(self, ref, name):
        r, n, c = self.places[name][0]
        return ref[r : r + 2 * n, 0:c]

    def get(self, ref, name):
        out = [ref[r : r + n, 0:c] for r, n, c in self.places[name]]
        return out[0] if len(out) == 1 else out


def split(x):
    hi = x.astype(BF16)
    return hi, (x - hi.astype(F32)).astype(BF16)


def stacked(x):
    return jnp.concatenate(split(x), axis=0)


def dot(a, b):
    return jnp.dot(a, b, preferred_element_type=F32)


def left_dot(m, hi, lo):
    rows = m.shape[0] // 2
    both = dot(m, hi)
    return both[:rows] + both[rows:] + dot(m[:rows], lo)


def right_dot(hi, lo, m):
    return dot(hi, m[0]) + dot(lo, m[0]) + dot(hi, m[1])


def stack_dot(x, m):
    rows = x.shape[0] // 2
    both = dot(x, m[0])
    return both[:rows] + both[rows:] + dot(x[:rows], m[1])


def flag(name, low):
    edge = 0 if low else lax.axis_size(name) - 1
    return jnp.where(lax.axis_index(name) == edge, 0.0, 1.0)


def face_kernel(v_lo, v_hi, x_lo, x_hi):
    for c in range(3):
        x_lo[c, 0:BY, :] = v_lo[c] * flag("gx", True)
        x_hi[c, 0:BY, :] = v_hi[c] * flag("gx", False)
        x_lo[c, BY:PY, :] = jnp.zeros((PY - BY, BZ), F32)
        x_hi[c, BY:PY, :] = jnp.zeros((PY - BY, BZ), F32)


def pack_kernel(v, y_lo, y_hi, z_lo, z_hi):
    y_low, y_high = flag("gy", True), flag("gy", False)
    lane = lax.broadcasted_iota(jnp.int32, (BY, 128), 1)
    low = jnp.zeros((BY, 128), F32)
    high = jnp.zeros((BY, 128), F32)
    for c in range(3):
        for x in range(BX):
            y_lo[BX * c + x : BX * c + x + 1, :] = v[c, x, 0:1, :] * y_low
            y_hi[BX * c + x : BX * c + x + 1, :] = v[c, x, BY - 1 : BY, :] * y_high
            here = lane == 16 * c + x
            low = jnp.where(here, jnp.broadcast_to(v[c, x, :, 0:1], (BY, 128)), low)
            high = jnp.where(here, jnp.broadcast_to(v[c, x, :, BZ - 1 : BZ], (BY, 128)), high)
    z_lo[0:BY, :] = low * flag("gz", True)
    z_hi[0:BY, :] = high * flag("gz", False)
    z_lo[BY:PY, :] = jnp.zeros((PY - BY, 128), F32)
    z_hi[BY:PY, :] = jnp.zeros((PY - BY, 128), F32)


def plane_sums(planes, scale):
    d = inner_matrix() * scale
    outs = []
    for i in range(5):
        total = None
        for j in range(5):
            if abs(d[i, j]) < 1e-12:
                continue
            term = float(d[i, j]) * planes[j]
            total = term if total is None else total + term
        outs.append(total)
    return outs


def volume_kernel(packed, v, after, weights, conv, V, FH, FL):
    del after
    for c in range(3):
        for x in range(BX):
            V[c, x, 0:BY, :] = v[c, x]
            V[c, x, BY:PY, :] = jnp.zeros((PY - BY, BZ), F32)

    def products(t, carry):
        dst = pl.ds(pl.multiple_of(128 * t, 128), 128)
        for q in range(BX // 2):
            a = [V[c, 2 * q : 2 * q + 2, :, dst].reshape(2 * PY, 128) for c in range(3)]
            pairs = (a[0] * a[1], a[1] * a[1], a[1] * a[2], a[0] * a[2], a[2] * a[2])
            for f, value in enumerate(pairs):
                hi, lo = split(value)
                FH[f, 2 * PY * q : 2 * PY * (q + 1), dst] = hi
                FL[f, 2 * PY * q : 2 * PY * (q + 1), dst] = lo
        return carry

    lax.fori_loop(0, TILES, products, 0)

    for i, (n0, n1, k0, k1) in enumerate(WINDOWS):
        high = FH[2:5, :, k0:k1].reshape(3 * ROWS, k1 - k0)
        low = FL[2:5, :, k0:k1].reshape(3 * ROWS, k1 - k0)
        z = right_dot(high, low, packed.get(weights, "bz" + str(i)))
        for c in range(3):
            along_z = ROWS * (1, 0, 2)[c]
            conv[c, :, :, n0:n1] = z[along_z : along_z + ROWS].reshape(BX, PY, n1 - n0)
    my = packed.both(weights, "my")
    for n0, n1 in LANES:
        for c in range(3):
            y = left_dot(my, FH[c, :, n0:n1], FL[c, :, n0:n1]).reshape(BX, PY, n1 - n0)
            conv[c, :, :, n0:n1] = conv[c, :, :, n0:n1] + y

    def along_x(t, carry):
        dst = pl.ds(pl.multiple_of(128 * t, 128), 128)
        for e in range(EX):
            v0 = [V[0, 5 * e + i, :, dst] for i in range(5)]
            for c in range(3):
                flux = [v0[i] * V[c, 5 * e + i, :, dst] for i in range(5)]
                for i, total in enumerate(plane_sums(flux, -STEP)):
                    conv[c, 5 * e + i, :, dst] = conv[c, 5 * e + i, :, dst] + total
        return carry

    lax.fori_loop(0, TILES, along_x, 0)


def lift_kernel(
    packed, v, conv, hx_lo, hx_hi, hy_lo, hy_hi, hz_lo, hz_hi, mask, weights,
    prov, PH, PL, xp, xm, yp, ym, zp, zm, own, V,
):
    for c in range(3):
        V[c, 0, :, 128:768] = hx_lo[c]
        V[c, BX + 1, :, 128:768] = hx_hi[c]
        for x in range(BX):
            r = BX * c + x
            V[c, x + 1, 0:BY, 128:768] = v[c, x]
            V[c, x + 1, 20:22, 128:768] = jnp.broadcast_to(hy_hi[r : r + 1, :], (2, BZ))
            V[c, x + 1, 22:24, 128:768] = jnp.broadcast_to(hy_lo[r : r + 1, :], (2, BZ))
            k = 16 * c + x
            V[c, x + 1, :, 0:128] = jnp.broadcast_to(hz_lo[:, k : k + 1], (PY, 128))
            V[c, x + 1, :, 768:896] = jnp.broadcast_to(hz_hi[:, k : k + 1], (PY, 128))

    solid = spread_out(packed, weights, [mask[...].astype(F32).reshape(8, EZ).astype(BF16)])
    solid = jnp.concatenate(solid, axis=1)
    conv_scale = -0.5 * LIFT * STEP
    lane = lax.broadcasted_iota(jnp.int32, (PY, 128), 1)
    row = lax.broadcasted_iota(jnp.int32, (PY, 128), 0)
    row_left = (lax.rem(row, 5) == 0) & (row < BY)
    row_right = (lax.rem(row, 5) == 4) & (row < BY)
    y_face = jnp.where(row_left | row_right, conv_scale, 0.0)
    y_sign = jnp.where(row_left, conv_scale, jnp.where(row_right, -conv_scale, 0.0))
    damp = [1.0 / (1.0 + PENALTY * solid[PY * e : PY * (e + 1)]) for e in range(EX)]
    for t in range(TILES):
        point = lax.rem(lane + 128 * t, 5)
        z_left = point == 0
        z_face = jnp.where(z_left | (point == 4), conv_scale, 0.0)
        z_sign = jnp.where(z_left, conv_scale, jnp.where(point == 4, -conv_scale, 0.0))
        here = slice(128 + 128 * t, 256 + 128 * t)
        before = slice(128 * t, 128 + 128 * t)
        after = slice(256 + 128 * t, 384 + 128 * t)
        out = slice(128 * t, 128 + 128 * t)
        for x in range(BX):
            a = [V[c, x + 1, :, here] for c in range(3)]
            total = [conv[c, x, :, out] for c in range(3)]
            w = []
            for c in range(3):
                lo = pltpu.roll(jnp.where(lane == 127, V[c, x + 1, :, before], a[c]), 1, 1)
                hi = pltpu.roll(jnp.where(lane == 0, V[c, x + 1, :, after], a[c]), 127, 1)
                w.append(jnp.where(z_left, lo, hi))
            p = z_face * jnp.maximum(jnp.abs(a[2]), jnp.abs(w[2]))
            q = p + z_sign * w[2]
            total = [total[c] + (p * a[c] - q * w[c]) for c in range(3)]
            w = [
                jnp.where(row_left, pltpu.roll(a[c], 1, 0), pltpu.roll(a[c], PY - 1, 0))
                for c in range(3)
            ]
            p = y_face * jnp.maximum(jnp.abs(a[1]), jnp.abs(w[1]))
            q = p + y_sign * w[1]
            total = [total[c] + (p * a[c] - q * w[c]) for c in range(3)]
            if x % 5 in (0, 4):
                sign = 1.0 if x % 5 == 0 else -1.0
                w = [V[c, x if x % 5 == 0 else x + 2, :, here] for c in range(3)]
                p = conv_scale * jnp.maximum(jnp.abs(a[0]), jnp.abs(w[0]))
                q = p + (sign * conv_scale) * w[0]
                total = [total[c] + (p * a[c] - q * w[c]) for c in range(3)]
            factor = damp[x // 5][:, out]
            for c in range(3):
                prov[c, x, :, out] = (a[c] + total[c]) * factor

    for q in range(BX // 2):
        for c in range(3):
            hi, lo = split(prov[c, 2 * q : 2 * q + 2].reshape(2 * PY, BZ))
            PH[c, 2 * PY * q : 2 * PY * (q + 1), :] = hi
            PL[c, 2 * PY * q : 2 * PY * (q + 1), :] = lo
    first = [1.0 - flag(name, True) for name in ("gx", "gy", "gz")]
    x_low, y_low, z_low = (flag(name, True) for name in ("gx", "gy", "gz"))
    x_high, y_high, z_high = (flag(name, False) for name in ("gx", "gy", "gz"))
    parts = []
    c0, c1, c2, d0, d1 = (
        sum(part.astype(F32) for part in packed.get(weights, n)) for n in ("c0", "c1", "c2", "d0", "d1")
    )
    for c, m in enumerate((c0 + first[0] * d0, c1 + first[1] * d1, c2)):
        parts.append(left_dot(stacked(m), PH[c], PL[c]))
    coarse = stack_dot(stacked(parts[0] + parts[1]), packed.get(weights, "hz"))
    coarse = coarse + stack_dot(stacked(parts[2]), packed.get(weights, "gz"))
    lane16 = lax.broadcasted_iota(jnp.int32, (16, 128), 1)
    vertices = coarse[:, 0:128] - jnp.where(
        lane16 == 0, (0.5 * LIFT * 0.1) * first[2] * parts[2][:, 0:128], 0.0
    )
    row16 = lax.broadcasted_iota(jnp.int32, (16, 128), 0)
    there = jnp.where(row16 >= 10, x_high, 1.0) * jnp.where(lax.rem(row16, 5) == 4, y_high, 1.0)
    vertices = vertices * there
    edge = coarse[:, 128:256] * (there * z_high)
    edge_next = pltpu.roll(edge, 1, 1)
    own[...] = vertices

    xp[0:PY, :] = prov[0, BX - 1] * x_high
    xm[...] = prov[0, 0] * x_low
    xp[BY:PY, :] = jnp.zeros((PY - BY, BZ), F32)
    xp[20:24, 0:128] = vertices[10:14]
    xp[20:24, 128:256] = edge[10:14]
    xp[20:21, 256:384] = vertices[14:15]
    xp[20:21, 384:512] = edge[14:15]
    yp[8:16, :] = jnp.zeros((8, BZ), F32)
    ym[8:16, :] = jnp.zeros((8, BZ), F32)
    lane24 = lax.broadcasted_iota(jnp.int32, (PY, 128), 1)
    low = jnp.zeros((PY, 128), F32)
    high = jnp.zeros((PY, 128), F32)
    for x in range(BX):
        yp[x : x + 1, :] = prov[1, x, BY - 1 : BY, :] * y_high
        ym[x : x + 1, :] = prov[1, x, 0:1, :] * y_low
        low = jnp.where(lane24 == x, jnp.broadcast_to(prov[2, x, :, 0:1], (PY, 128)), low)
        high = jnp.where(lane24 == x, jnp.broadcast_to(prov[2, x, :, BZ - 1 : BZ], (PY, 128)), high)
    yp[10:11, 0:128] = vertices[4:5]
    yp[11:12, 0:128] = vertices[9:10]
    yp[10:11, 128:256] = edge[4:5] + edge_next[9:10]
    zm[...] = low * z_low
    zp[...] = high * z_high
    zp[0:4, :] = zp[0:4, :] + (edge[0:4] + edge_next[5:9])


def right_kernel(packed, prov, PH, PL, weights, rhs):
    for i, (n0, n1, k0, k1) in enumerate(WINDOWS):
        z = right_dot(PH[2, :, k0:k1], PL[2, :, k0:k1], packed.get(weights, "rz" + str(i)))
        rhs[:, :, n0:n1] = z.reshape(BX, PY, n1 - n0)
    ry = packed.both(weights, "ry")
    for n0, n1 in LANES:
        y = left_dot(ry, PH[1, :, n0:n1], PL[1, :, n0:n1]).reshape(BX, PY, n1 - n0)
        rhs[:, :, n0:n1] = rhs[:, :, n0:n1] + y

    def right_x(t, carry):
        dst = pl.ds(pl.multiple_of(128 * t, 128), 128)
        planes = [prov[0, x, :, dst] for x in range(BX)]
        outs = plane_sums(planes[:5], -1.0) + plane_sums(planes[5:], -1.0)
        outs[4] = outs[4] - 0.5 * LIFT * planes[5]
        outs[5] = outs[5] + 0.5 * LIFT * planes[4]
        for x in range(BX):
            rhs[x, :, dst] = rhs[x, :, dst] + outs[x]
        return carry

    lax.fori_loop(0, TILES, right_x, 0)


def spread_out(packed, weights, parts):
    rows_of = packed.get(weights, "rows_of")
    nodes = []
    for i in range(3):
        m = packed.get(weights, "spread" + str(i))
        wide = sum(dot(part, m) for part in parts)
        nodes.append(sum(dot(rows_of, part) for part in split(wide)[: len(parts)]))
    return nodes


def divisor_kernel(packed, scale, after, weights, modes, inverse):
    del after
    factor = spread_out(packed, weights, split(scale[...].reshape(8, EZ)))
    values = eigen_value_table()
    for i, (n0, n1, _, _) in enumerate(WINDOWS):
        for x in range(BX):
            f = factor[i][PY * (x // 5) : PY * (x // 5 + 1)]
            inverse[x, :, 256 * i : 256 * i + n1 - n0] = 1.0 / (
                f * (modes[:, 0 : n1 - n0] + float(values[x % 5])) + 1.0
            )


def smooth_kernel(
    packed, rhs, hx_lo, hx_hi, hy_lo, hy_hi, hz_lo, hz_hi, own, inverse, weights,
    smoothed, coarse, A, B,
):
    lift = 0.5 * LIFT
    lane = lax.broadcasted_iota(jnp.int32, (PY, 128), 1)
    row = lax.broadcasted_iota(jnp.int32, (PY, BZ), 0)
    for q in range(BX // 2):
        planes = []
        for x in (2 * q, 2 * q + 1):
            r = rhs[x]
            if x == 0:
                r = r + lift * hx_lo[...]
            if x == BX - 1:
                r = r - lift * hx_hi[...]
            r = r + jnp.where(row == 0, lift * jnp.broadcast_to(hy_lo[x : x + 1, :], (PY, BZ)), 0.0)
            r = r - jnp.where(
                row == BY - 1, lift * jnp.broadcast_to(hy_hi[x : x + 1, :], (PY, BZ)), 0.0
            )
            left = r[:, 0:128] + jnp.where(
                lane == 0, lift * jnp.broadcast_to(hz_lo[:, x : x + 1], (PY, 128)), 0.0
            )
            right = r[:, BZ - 128 : BZ] - jnp.where(
                lane == 127, lift * jnp.broadcast_to(hz_hi[:, x : x + 1], (PY, 128)), 0.0
            )
            planes.append(jnp.concatenate([left, r[:, 128 : BZ - 128], right], axis=1))
        hi, lo = split(jnp.concatenate(planes, axis=0))
        A[2 * PY * q : 2 * PY * (q + 1), 0:BZ] = hi
        A[ROWS + 2 * PY * q : ROWS + 2 * PY * (q + 1), 0:BZ] = lo

    tf = packed.both(weights, "tf")
    for n0, n1 in LANES:
        B[:, n0:n1] = stacked(left_dot(tf, A[0:ROWS, n0:n1], A[ROWS:, n0:n1]))

    for i, (n0, n1, _, _) in enumerate(WINDOWS):
        size = n1 - n0
        c = stack_dot(B[:, n0:n1], packed.get(weights, "sf" + str(i))).reshape(BX, PY, size)
        c = (c * inverse[:, :, 256 * i : 256 * i + size]).reshape(ROWS, size)
        c = stack_dot(stacked(c), packed.get(weights, "sb" + str(i)))
        A[:, 256 * i : 256 * i + size] = stacked(c)

    tb = packed.both(weights, "tb")
    for i, (n0, n1, _, _) in enumerate(WINDOWS):
        here = slice(256 * i, 256 * i + n1 - n0)
        c = left_dot(tb, A[0:ROWS, here], A[ROWS:, here]).reshape(BX, PY, n1 - n0)
        smoothed[:, :, n0:n1] = c[:, 0:BY]

    lane4 = lax.broadcasted_iota(jnp.int32, (4, 128), 1)
    row4 = lax.broadcasted_iota(jnp.int32, (4, 128), 0)
    for vx in range(EX):
        total = own[5 * vx : 5 * vx + 4, :]
        if vx == 0:
            total = total + hx_lo[20:24, 0:128]
        total = total + jnp.where(
            row4 == 0, jnp.broadcast_to(hy_lo[10 + vx : 11 + vx, 0:128], (4, 128)), 0.0
        )
        k = ZEDGE + vx
        total = total + jnp.where(
            lane4 == 0, jnp.broadcast_to(hz_lo[0:4, k : k + 1], (4, 128)), 0.0
        )
        coarse[vx] = total


def constants():
    volume, lift, right, smooth, scales = (Packed() for _ in range(5))
    eye_x = np.eye(BX)
    volume.add("my", pad_both(np.kron(eye_x, -STEP * line_operator(EY, False))))
    right.add("ry", pad_both(np.kron(eye_x, -line_operator(EY, True))))
    volume.add_windows("bz", -STEP * line_operator(EZ, False).T)
    right.add_windows("rz", -line_operator(EZ, True).T)
    basis = eigen_basis_table()
    sx = np.kron(np.eye(EX), basis)
    sy = np.kron(np.eye(EY), basis)
    sz = np.kron(np.eye(EZ), basis)
    t = np.kron(sx, sy)
    smooth.add("tf", pad_both(t.T))
    smooth.add("tb", pad_both(t))
    smooth.add_windows("sf", sz, False)
    smooth.add_windows("sb", sz.T, False)
    spread = np.kron(np.eye(EZ), np.ones((1, 5)))
    rows_of = np.zeros((EX * PY, 8))
    for e in range(EX):
        for y in range(BY):
            rows_of[PY * e + y, EY * e + y // 5] = 1.0
    for packed, cuts in ((lift, LANES), (scales, WINDOWS)):
        packed.add("rows_of", rows_of, 1)
        for i, cut in enumerate(cuts):
            packed.add("spread" + str(i), spread[:, cut[0] : cut[1]], 1)
    values = eigen_value_table()
    modes = np.zeros((PY, BZ))
    for y in range(BY):
        modes[y] = values[y % 5] + np.tile(values, EZ)
    hx, hy, hz = hats_line(EX), hats_line(EY), hats_line(EZ)
    gx, gy, gz = slopes_line(EX), slopes_line(EY), slopes_line(EZ)
    for name, m in (("hz", hz), ("gz", gz)):
        wide = np.zeros((BZ, 256))
        wide[:, 0:EZ] = m[:EZ].T
        wide[:, 128 + ZEDGE] = m[EZ]
        lift.add(name, wide)
    half = 0.5 * LIFT * hat_weight_table()[0, 0]
    ex, ey = np.zeros_like(gx), np.zeros_like(gy)
    ex[0, 0] = -half
    ey[0, 0] = -half
    for name, m in (
        ("c0", np.kron(gx, hy)),
        ("c1", np.kron(hx, gy)),
        ("c2", np.kron(hx, hy)),
        ("d0", np.kron(ex, hy)),
        ("d1", np.kron(hx, ey)),
    ):
        lift.add(name, pad_to(pad_rows(-m), 16, ROWS))
    return volume, lift, right, smooth, scales, modes.astype(np.float32)


def shift(x, axis, by):
    size = lax.axis_size(axis)
    return lax.ppermute(x, axis, [(i, (i + by) % size) for i in range(size)])


def like(*shape):
    return jax.ShapeDtypeStruct(shape, F32)


def run(kernel, outs, operands, scratch=(), name=None, flops=0):
    vmem = pl.BlockSpec(memory_space=pltpu.VMEM)
    return pl.pallas_call(
        kernel,
        out_shape=outs,
        in_specs=[vmem] * len(operands),
        out_specs=[vmem] * len(outs),
        scratch_shapes=list(scratch),
        compiler_params=pltpu.CompilerParams(vmem_limit_bytes=32 * 2**20),
        cost_estimate=pl.CostEstimate(flops=flops, bytes_accessed=4 << 20, transcendentals=0),
        name=name,
    )(*operands)


def shards(velocity, obstacle_element_mask, element_metric_scale):
    volume, lift, right, smooth, scales, modes = constants()
    x_faces = run(
        face_kernel,
        [like(3, PY, BZ)] * 2,
        [velocity[:, 0], velocity[:, BX - 1]],
        name="face",
        flops=10**10,
    )
    faces = run(
        pack_kernel,
        [like(3 * BX, BZ)] * 2 + [like(PY, 128)] * 2,
        [velocity],
        name="pack",
        flops=10**10,
    )
    halo = [
        shift(x_faces[1], "gx", 1),
        shift(x_faces[0], "gx", -1),
        shift(faces[1], "gy", 1),
        shift(faces[0], "gy", -1),
        shift(faces[3], "gz", 1),
    ]
    halo[0], last = lax.optimization_barrier((halo[0], faces[2]))
    halo.append(shift(last, "gz", -1))
    field = like(3, BX, PY, BZ)
    half = jax.ShapeDtypeStruct((3, ROWS, BZ), BF16)
    (conv,) = run(
        functools.partial(volume_kernel, volume),
        [field],
        [velocity, faces[2], volume.array()],
        scratch=[pltpu.VMEM((3, BX, PY, BZ), F32)] + [pltpu.VMEM((5, ROWS, BZ), BF16)] * 2,
        name="volume",
        flops=4 * 10**9,
    )
    prov, ph, plo, xp, xm, yp, ym, zp, zm, own = run(
        functools.partial(lift_kernel, lift),
        [field, half, half]
        + [like(PY, BZ), like(PY, BZ), like(16, BZ), like(16, BZ), like(PY, 128), like(PY, 128)]
        + [like(16, 128)],
        [velocity, conv, *halo, obstacle_element_mask, lift.array()],
        scratch=[pltpu.VMEM((3, BX + 2, PY, 896), F32)],
        name="lift",
        flops=4 * 10**9,
    )
    (rhs,) = run(
        functools.partial(right_kernel, right),
        [like(BX, PY, BZ)],
        [prov, ph, plo, right.array()],
        name="right",
        flops=2 * 10**9,
    )
    gx_lo = shift(xp, "gx", 1)
    gz_hi = shift(zm, "gz", -1)
    gx_lo, gz_hi = lax.optimization_barrier((gx_lo, gz_hi))
    gx_hi = shift(xm, "gx", -1)
    yp = yp + jnp.pad(gx_lo[20:21, 256:512], ((10, 5), (0, BZ - 256)))
    gy_lo = shift(yp, "gy", 1)
    gy_hi = shift(ym, "gy", -1)
    zp = zp + jnp.pad(gx_lo[20:24, 128:256], ((0, 20), (0, 0)))
    zp = zp + jnp.pad(gy_lo[10:11, 128:256], ((0, 23), (0, 0)))
    gz_lo = shift(zp, "gz", 1)
    (inverse,) = run(
        functools.partial(divisor_kernel, scales),
        [like(BX, PY, 768)],
        [element_metric_scale, gy_lo, scales.array(), jnp.asarray(modes)],
        name="divisor",
        flops=2 * 10**9,
    )
    smoothed, coarse = run(
        functools.partial(smooth_kernel, smooth),
        [like(BX, BY, BZ), like(EX, EY, EZ)],
        [rhs, gx_lo, gx_hi, gy_lo, gy_hi, gz_lo, gz_hi, own, inverse]
        + [smooth.array()],
        scratch=[pltpu.VMEM((2 * ROWS, 768), BF16), pltpu.VMEM((2 * ROWS, BZ), BF16)],
        name="smooth",
        flops=3 * 10**9,
    )
    return (smoothed, coarse)


def solution(mesh):
    return jax.shard_map(
        shards,
        mesh=mesh,
        in_specs=(P(None, "gx", "gy", "gz"), P("gx", "gy", "gz"), P("gx", "gy", "gz")),
        out_specs=(P("gx", "gy", "gz"), P("gx", "gy", "gz")),
        check_vma=False,
    )
```

```python
import functools
import math

import jax
import jax.numpy as jnp
import ml_dtypes
import numpy as np
from jax import lax
from jax.experimental import pallas as pl
from jax.experimental.pallas import tpu as pltpu
from jax.sharding import PartitionSpec as P

LIFT = 10.0
STEP = 0.05
PENALTY = 4.0
LIFT_SCALE = -0.5 * LIFT * STEP

BX, BY, BZ = 10, 20, 640
EX, EY, EZ = 2, 4, 128
PY = 24
ROWS = BX * PY
TILES = BZ // 128
WINDOWS = ((0, 250, 0, 251), (250, 500, 249, 501), (500, 640, 499, 640))
LANES = ((0, 256), (256, 512), (512, 640))
ZEDGE = 16

F32 = jnp.float32
BF16 = jnp.bfloat16


def lobatto_points():
    return np.array([-1.0, -math.sqrt(3.0 / 7.0), 0.0, math.sqrt(3.0 / 7.0), 1.0])


def lobatto_weights():
    return np.array([0.1, 49.0 / 90.0, 32.0 / 45.0, 49.0 / 90.0, 0.1])


def derivative_matrix():
    points = lobatto_points()
    scales = np.array(
        [np.prod([points[i] - points[k] for k in range(5) if k != i]) for i in range(5)]
    )
    result = np.zeros((5, 5))
    for i in range(5):
        for j in range(5):
            if i != j:
                result[i, j] = scales[i] / (scales[j] * (points[i] - points[j]))
        result[i, i] = -np.sum(result[i])
    return result


def eigen_basis_table():
    return np.array(
        [
            [
                math.sqrt((1.0 if k == 0 else 2.0) / 5.0) * math.cos(math.pi * (i + 0.5) * k / 5.0)
                for k in range(5)
            ]
            for i in range(5)
        ]
    )


def eigen_value_table():
    return np.array([4.0 * math.sin(math.pi * k / 10.0) ** 2 for k in range(5)])


def hat_weight_table():
    points = lobatto_points()
    weights = lobatto_weights()
    return np.array([weights * (1.0 - points) / 2.0, weights * (1.0 + points) / 2.0])


def inner_matrix():
    result = derivative_matrix()
    result[0, 0] += 0.5 * LIFT
    result[4, 4] -= 0.5 * LIFT
    return result


def line_operator(elements, coupled):
    inner = inner_matrix()
    size = 5 * elements
    m = np.zeros((size, size))
    for e in range(elements):
        m[5 * e : 5 * e + 5, 5 * e : 5 * e + 5] = inner
        if coupled and e > 0:
            m[5 * e, 5 * e - 1] = -0.5 * LIFT
        if coupled and e < elements - 1:
            m[5 * e + 4, 5 * e + 5] = 0.5 * LIFT
    return m


def hats_line(elements):
    h = hat_weight_table()
    m = np.zeros((elements + 1, 5 * elements))
    for e in range(elements):
        m[e, 5 * e : 5 * e + 5] += h[0]
        m[e + 1, 5 * e : 5 * e + 5] += h[1]
    return m


def slopes_line(elements):
    h = hat_weight_table()
    d = derivative_matrix()
    g = h @ d
    g[0, 0] += LIFT * h[0, 0]
    g[1, 4] -= LIFT * h[1, 4]
    m = np.zeros((elements + 1, 5 * elements))
    for e in range(elements):
        m[e, 5 * e : 5 * e + 5] += g[0]
        m[e + 1, 5 * e : 5 * e + 5] += g[1]
    return m


def pad_rows(m):
    out = np.zeros((m.shape[0], BX, PY))
    out[:, :, :BY] = m.reshape(m.shape[0], BX, BY)
    return out.reshape(m.shape[0], ROWS)


def pad_both(m):
    return pad_rows(pad_rows(m).T).T


def pad_to(m, rows, columns):
    out = np.zeros((rows, columns))
    out[: m.shape[0], : m.shape[1]] = m
    return out


class Packed:

    def __init__(self):
        self.parts = []
        self.places = {}
        self.rows = 0

    def add(self, name, m, parts=2):
        m = np.asarray(m, np.float64)
        hi = m.astype(np.float32).astype(ml_dtypes.bfloat16)
        lo = (m - hi.astype(np.float64)).astype(np.float32).astype(ml_dtypes.bfloat16)
        places = []
        for part in (hi, lo)[:parts]:
            wide = np.zeros((part.shape[0], 256), ml_dtypes.bfloat16)
            wide[:, : part.shape[1]] = part
            places.append((self.rows, part.shape[0], part.shape[1]))
            self.parts.append(wide)
            self.rows += part.shape[0]
        self.places[name] = places

    def add_windows(self, name, m, coupled=True):
        for i, (n0, n1, k0, k1) in enumerate(WINDOWS):
            self.add(name + str(i), m[k0:k1, n0:n1] if coupled else m[n0:n1, n0:n1])

    def array(self):
        return jnp.asarray(np.concatenate(self.parts))

    def both(self, ref, name):
        r, n, c = self.places[name][0]
        return ref[r : r + 2 * n, 0:c]

    def get(self, ref, name):
        out = [ref[r : r + n, 0:c] for r, n, c in self.places[name]]
        return out[0] if len(out) == 1 else out


def split(x):
    hi = x.astype(BF16)
    return hi, (x - hi.astype(F32)).astype(BF16)


def stacked(x):
    return jnp.concatenate(split(x), axis=0)


def dot(a, b):
    return jnp.dot(a, b, preferred_element_type=F32)


def left_dot(m, hi, lo):
    rows = m.shape[0] // 2
    both = dot(m, hi)
    return both[:rows] + both[rows:] + dot(m[:rows], lo)


def right_dot(hi, lo, m):
    return dot(hi, m[0]) + dot(lo, m[0]) + dot(hi, m[1])


def stack_dot(x, m):
    rows = x.shape[0] // 2
    both = dot(x, m[0])
    return both[:rows] + both[rows:] + dot(x[:rows], m[1])


def flag(name, low):
    edge = 0 if low else lax.axis_size(name) - 1
    return jnp.where(lax.axis_index(name) == edge, 0.0, 1.0)


def face_kernel(v_lo, v_hi, x_lo, x_hi):
    for c in range(3):
        x_lo[c, 0:BY, :] = v_lo[c] * flag("gx", True)
        x_hi[c, 0:BY, :] = v_hi[c] * flag("gx", False)
        x_lo[c, BY:PY, :] = jnp.zeros((PY - BY, BZ), F32)
        x_hi[c, BY:PY, :] = jnp.zeros((PY - BY, BZ), F32)


def pack_kernel(v, y_lo, y_hi, z_lo, z_hi):
    y_low, y_high = flag("gy", True), flag("gy", False)
    lane = lax.broadcasted_iota(jnp.int32, (BY, 128), 1)
    low = jnp.zeros((BY, 128), F32)
    high = jnp.zeros((BY, 128), F32)
    for c in range(3):
        for x in range(BX):
            y_lo[BX * c + x : BX * c + x + 1, :] = v[c, x, 0:1, :] * y_low
            y_hi[BX * c + x : BX * c + x + 1, :] = v[c, x, BY - 1 : BY, :] * y_high
            here = lane == 16 * c + x
            low = jnp.where(here, jnp.broadcast_to(v[c, x, :, 0:1], (BY, 128)), low)
            high = jnp.where(here, jnp.broadcast_to(v[c, x, :, BZ - 1 : BZ], (BY, 128)), high)
    z_lo[0:BY, :] = low * flag("gz", True)
    z_hi[0:BY, :] = high * flag("gz", False)
    z_lo[BY:PY, :] = jnp.zeros((PY - BY, 128), F32)
    z_hi[BY:PY, :] = jnp.zeros((PY - BY, 128), F32)


def plane_sums(planes, scale):
    d = inner_matrix() * scale
    outs = []
    for i in range(5):
        total = None
        for j in range(5):
            if abs(d[i, j]) < 1e-12:
                continue
            term = float(d[i, j]) * planes[j]
            total = term if total is None else total + term
        outs.append(total)
    return outs


def add_lift(total, a, w, along, face, sign):
    p = face * jnp.maximum(jnp.abs(a[along]), jnp.abs(w[along]))
    q = p + sign * w[along]
    return [total[c] + (p * a[c] - q * w[c]) for c in range(3)]


def volume_kernel(packed, v, after, weights, V, conv, FH, FL):
    del after
    for c in range(3):
        for x in range(BX):
            V[c, x, 0:BY, :] = v[c, x]
            V[c, x, BY:PY, :] = jnp.zeros((PY - BY, BZ), F32)

    def products(t, carry):
        dst = pl.ds(pl.multiple_of(128 * t, 128), 128)
        for q in range(BX // 2):
            a = [V[c, 2 * q : 2 * q + 2, :, dst].reshape(2 * PY, 128) for c in range(3)]
            pairs = (a[0] * a[1], a[1] * a[1], a[1] * a[2], a[0] * a[2], a[2] * a[2])
            for f, value in enumerate(pairs):
                hi, lo = split(value)
                FH[f, 2 * PY * q : 2 * PY * (q + 1), dst] = hi
                FL[f, 2 * PY * q : 2 * PY * (q + 1), dst] = lo
        return carry

    lax.fori_loop(0, TILES, products, 0, unroll=True)

    for i, (n0, n1, k0, k1) in enumerate(WINDOWS):
        high = FH[2:5, :, k0:k1].reshape(3 * ROWS, k1 - k0)
        low = FL[2:5, :, k0:k1].reshape(3 * ROWS, k1 - k0)
        z = right_dot(high, low, packed.get(weights, "bz" + str(i)))
        for c in range(3):
            along_z = ROWS * (1, 0, 2)[c]
            conv[c, :, :, n0:n1] = z[along_z : along_z + ROWS].reshape(BX, PY, n1 - n0)
    my = packed.both(weights, "my")
    for n0, n1 in LANES:
        for c in range(3):
            y = left_dot(my, FH[c, :, n0:n1], FL[c, :, n0:n1]).reshape(BX, PY, n1 - n0)
            conv[c, :, :, n0:n1] = conv[c, :, :, n0:n1] + y

    def along_x(t, carry):
        dst = pl.ds(pl.multiple_of(128 * t, 128), 128)
        for e in range(EX):
            v0 = [V[0, 5 * e + i, :, dst] for i in range(5)]
            for c in range(3):
                flux = [v0[i] * V[c, 5 * e + i, :, dst] for i in range(5)]
                for i, total in enumerate(plane_sums(flux, -STEP)):
                    conv[c, 5 * e + i, :, dst] = conv[c, 5 * e + i, :, dst] + total
        return carry

    lax.fori_loop(0, TILES, along_x, 0, unroll=True)

    lane = lax.broadcasted_iota(jnp.int32, (PY, 128), 1)
    row = lax.broadcasted_iota(jnp.int32, (PY, 128), 0)
    row_left = (lax.rem(row, 5) == 0) & (row > 0) & (row < BY)
    row_right = (lax.rem(row, 5) == 4) & (row < BY - 1)
    y_face = jnp.where(row_left | row_right, LIFT_SCALE, 0.0)
    y_sign = jnp.where(row_left, LIFT_SCALE, jnp.where(row_right, -LIFT_SCALE, 0.0))
    for t in range(TILES):
        node = lane + 128 * t
        z_left = (lax.rem(node, 5) == 0) & (node > 0)
        z_right = (lax.rem(node, 5) == 4) & (node < BZ - 1)
        z_face = jnp.where(z_left | z_right, LIFT_SCALE, 0.0)
        z_sign = jnp.where(z_left, LIFT_SCALE, jnp.where(z_right, -LIFT_SCALE, 0.0))
        here = slice(128 * t, 128 + 128 * t)
        before = slice(128 * t - 128, 128 * t)
        after = slice(128 + 128 * t, 256 + 128 * t)
        for x in range(BX):
            a = [V[c, x, :, here] for c in range(3)]
            total = [conv[c, x, :, here] for c in range(3)]
            w = []
            for c in range(3):
                lo, hi = a[c], a[c]
                if t > 0:
                    lo = jnp.where(lane == 127, V[c, x, :, before], lo)
                if t < TILES - 1:
                    hi = jnp.where(lane == 0, V[c, x, :, after], hi)
                w.append(jnp.where(z_left, pltpu.roll(lo, 1, 1), pltpu.roll(hi, 127, 1)))
            total = add_lift(total, a, w, 2, z_face, z_sign)
            w = [
                jnp.where(row_left, pltpu.roll(a[c], 1, 0), pltpu.roll(a[c], PY - 1, 0))
                for c in range(3)
            ]
            total = add_lift(total, a, w, 1, y_face, y_sign)
            if x in (4, 5):
                sign = -1.0 if x == 4 else 1.0
                w = [V[c, 9 - x, :, here] for c in range(3)]
                total = add_lift(total, a, w, 0, LIFT_SCALE, sign * LIFT_SCALE)
            for c in range(3):
                conv[c, x, :, here] = total[c]


def lift_kernel(
    packed, V, conv, hx_lo, hx_hi, hy_lo, hy_hi, hz_lo, hz_hi, mask, weights,
    prov, PH, PL, xp, xm, yp, ym, zp, zm, own,
):
    solid = spread_out(packed, weights, [mask[...].astype(F32).reshape(8, EZ).astype(BF16)])
    solid = jnp.concatenate(solid, axis=1)
    lane = lax.broadcasted_iota(jnp.int32, (PY, 128), 1)
    row8 = lax.broadcasted_iota(jnp.int32, (8, 128), 0)
    first_lane = jnp.where(lane == 0, LIFT_SCALE, 0.0)
    last_lane = jnp.where(lane == 127, LIFT_SCALE, 0.0)
    first_row = jnp.where(row8 == 0, LIFT_SCALE, 0.0)
    last_row = jnp.where(row8 == BY - 17, LIFT_SCALE, 0.0)
    damp = [1.0 / (1.0 + PENALTY * solid[PY * e : PY * (e + 1)]) for e in range(EX)]
    for t in range(TILES):
        here = slice(128 * t, 128 + 128 * t)
        for x in range(BX):
            a = [V[c, x, :, here] for c in range(3)]
            total = [conv[c, x, :, here] for c in range(3)]
            if t in (0, TILES - 1):
                edge = hz_lo if t == 0 else hz_hi
                w = [
                    jnp.broadcast_to(edge[:, 16 * c + x : 16 * c + x + 1], (PY, 128))
                    for c in range(3)
                ]
                face = first_lane if t == 0 else last_lane
                total = add_lift(total, a, w, 2, face, face if t == 0 else -face)
            if x in (0, BX - 1):
                w = [(hx_lo if x == 0 else hx_hi)[c, :, here] for c in range(3)]
                sign = 1.0 if x == 0 else -1.0
                total = add_lift(total, a, w, 0, LIFT_SCALE, sign * LIFT_SCALE)
            factor = damp[x // 5][:, here]
            done = [(a[c] + total[c]) * factor for c in range(3)]
            for c in range(3):
                prov[c, x, 8:16, here] = done[c][8:16]
            for r0, edge, face, sign in ((0, hy_lo, first_row, first_row), (16, hy_hi, last_row, -last_row)):
                w = [
                    jnp.broadcast_to(edge[BX * c + x : BX * c + x + 1, here], (8, 128))
                    for c in range(3)
                ]
                rows = slice(r0, r0 + 8)
                zero = [jnp.zeros((8, 128), F32)] * 3
                more = add_lift(zero, [part[rows] for part in a], w, 1, face, sign)
                for c in range(3):
                    prov[c, x, rows, here] = done[c][rows] + more[c] * factor[rows]

    for q in range(BX // 2):
        for c in range(3):
            hi, lo = split(prov[c, 2 * q : 2 * q + 2].reshape(2 * PY, BZ))
            PH[c, 2 * PY * q : 2 * PY * (q + 1), :] = hi
            PL[c, 2 * PY * q : 2 * PY * (q + 1), :] = lo
    first = [1.0 - flag(name, True) for name in ("gx", "gy", "gz")]
    x_low, y_low, z_low = (flag(name, True) for name in ("gx", "gy", "gz"))
    x_high, y_high, z_high = (flag(name, False) for name in ("gx", "gy", "gz"))
    parts = []
    c0, c1, c2, d0, d1 = (
        sum(part.astype(F32) for part in packed.get(weights, n)) for n in ("c0", "c1", "c2", "d0", "d1")
    )
    for c, m in enumerate((c0 + first[0] * d0, c1 + first[1] * d1, c2)):
        parts.append(left_dot(stacked(m), PH[c], PL[c]))
    coarse = stack_dot(stacked(parts[0] + parts[1]), packed.get(weights, "hz"))
    coarse = coarse + stack_dot(stacked(parts[2]), packed.get(weights, "gz"))
    lane16 = lax.broadcasted_iota(jnp.int32, (16, 128), 1)
    vertices = coarse[:, 0:128] - jnp.where(
        lane16 == 0, (0.5 * LIFT * 0.1) * first[2] * parts[2][:, 0:128], 0.0
    )
    row16 = lax.broadcasted_iota(jnp.int32, (16, 128), 0)
    there = jnp.where(row16 >= 10, x_high, 1.0) * jnp.where(lax.rem(row16, 5) == 4, y_high, 1.0)
    vertices = vertices * there
    edge = coarse[:, 128:256] * (there * z_high)
    edge_next = pltpu.roll(edge, 1, 1)
    own[...] = vertices

    xp[0:PY, :] = prov[0, BX - 1] * x_high
    xm[...] = prov[0, 0] * x_low
    xp[BY:PY, :] = jnp.zeros((PY - BY, BZ), F32)
    xp[20:24, 0:128] = vertices[10:14]
    xp[20:24, 128:256] = edge[10:14]
    xp[20:21, 256:384] = vertices[14:15]
    xp[20:21, 384:512] = edge[14:15]
    yp[8:16, :] = jnp.zeros((8, BZ), F32)
    ym[8:16, :] = jnp.zeros((8, BZ), F32)
    lane24 = lax.broadcasted_iota(jnp.int32, (PY, 128), 1)
    low = jnp.zeros((PY, 128), F32)
    high = jnp.zeros((PY, 128), F32)
    for x in range(BX):
        yp[x : x + 1, :] = prov[1, x, BY - 1 : BY, :] * y_high
        ym[x : x + 1, :] = prov[1, x, 0:1, :] * y_low
        low = jnp.where(lane24 == x, jnp.broadcast_to(prov[2, x, :, 0:1], (PY, 128)), low)
        high = jnp.where(lane24 == x, jnp.broadcast_to(prov[2, x, :, BZ - 1 : BZ], (PY, 128)), high)
    yp[10:11, 0:128] = vertices[4:5]
    yp[11:12, 0:128] = vertices[9:10]
    yp[10:11, 128:256] = edge[4:5] + edge_next[9:10]
    zm[...] = low * z_low
    zp[...] = high * z_high
    zp[0:4, :] = zp[0:4, :] + (edge[0:4] + edge_next[5:9])


def right_kernel(packed, prov, PH, PL, weights, rhs):
    for i, (n0, n1, k0, k1) in enumerate(WINDOWS):
        z = right_dot(PH[2, :, k0:k1], PL[2, :, k0:k1], packed.get(weights, "rz" + str(i)))
        rhs[:, :, n0:n1] = z.reshape(BX, PY, n1 - n0)
    ry = packed.both(weights, "ry")
    for n0, n1 in LANES:
        y = left_dot(ry, PH[1, :, n0:n1], PL[1, :, n0:n1]).reshape(BX, PY, n1 - n0)
        rhs[:, :, n0:n1] = rhs[:, :, n0:n1] + y

    def right_x(t, carry):
        dst = pl.ds(pl.multiple_of(128 * t, 128), 128)
        planes = [prov[0, x, :, dst] for x in range(BX)]
        outs = plane_sums(planes[:5], -1.0) + plane_sums(planes[5:], -1.0)
        outs[4] = outs[4] - 0.5 * LIFT * planes[5]
        outs[5] = outs[5] + 0.5 * LIFT * planes[4]
        for x in range(BX):
            rhs[x, :, dst] = rhs[x, :, dst] + outs[x]
        return carry

    lax.fori_loop(0, TILES, right_x, 0, unroll=True)


def spread_out(packed, weights, parts):
    rows_of = packed.get(weights, "rows_of")
    nodes = []
    for i in range(3):
        m = packed.get(weights, "spread" + str(i))
        wide = sum(dot(part, m) for part in parts)
        nodes.append(sum(dot(rows_of, part) for part in split(wide)[: len(parts)]))
    return nodes


def divisor_kernel(packed, scale, after, weights, modes, inverse):
    del after
    factor = spread_out(packed, weights, split(scale[...].reshape(8, EZ)))
    values = eigen_value_table()
    for i, (n0, n1, _, _) in enumerate(WINDOWS):
        for x in range(BX):
            f = factor[i][PY * (x // 5) : PY * (x // 5 + 1)]
            inverse[x, :, 256 * i : 256 * i + n1 - n0] = 1.0 / (
                f * (modes[:, 0 : n1 - n0] + float(values[x % 5])) + 1.0
            )


def smooth_kernel(
    packed, rhs, hx_lo, hx_hi, hy_lo, hy_hi, hz_lo, hz_hi, own, inverse, weights,
    smoothed, coarse, A, B,
):
    lift = 0.5 * LIFT
    lane = lax.broadcasted_iota(jnp.int32, (PY, 128), 1)
    row = lax.broadcasted_iota(jnp.int32, (PY, BZ), 0)
    for q in range(BX // 2):
        planes = []
        for x in (2 * q, 2 * q + 1):
            r = rhs[x]
            if x == 0:
                r = r + lift * hx_lo[...]
            if x == BX - 1:
                r = r - lift * hx_hi[...]
            r = r + jnp.where(row == 0, lift * jnp.broadcast_to(hy_lo[x : x + 1, :], (PY, BZ)), 0.0)
            r = r - jnp.where(
                row == BY - 1, lift * jnp.broadcast_to(hy_hi[x : x + 1, :], (PY, BZ)), 0.0
            )
            left = r[:, 0:128] + jnp.where(
                lane == 0, lift * jnp.broadcast_to(hz_lo[:, x : x + 1], (PY, 128)), 0.0
            )
            right = r[:, BZ - 128 : BZ] - jnp.where(
                lane == 127, lift * jnp.broadcast_to(hz_hi[:, x : x + 1], (PY, 128)), 0.0
            )
            planes.append(jnp.concatenate([left, r[:, 128 : BZ - 128], right], axis=1))
        hi, lo = split(jnp.concatenate(planes, axis=0))
        A[2 * PY * q : 2 * PY * (q + 1), 0:BZ] = hi
        A[ROWS + 2 * PY * q : ROWS + 2 * PY * (q + 1), 0:BZ] = lo

    tf = packed.both(weights, "tf")
    for n0, n1 in LANES:
        B[:, n0:n1] = stacked(left_dot(tf, A[0:ROWS, n0:n1], A[ROWS:, n0:n1]))

    for i, (n0, n1, _, _) in enumerate(WINDOWS):
        size = n1 - n0
        c = stack_dot(B[:, n0:n1], packed.get(weights, "sf" + str(i))).reshape(BX, PY, size)
        c = (c * inverse[:, :, 256 * i : 256 * i + size]).reshape(ROWS, size)
        c = stack_dot(stacked(c), packed.get(weights, "sb" + str(i)))
        A[:, 256 * i : 256 * i + size] = stacked(c)

    tb = packed.both(weights, "tb")
    for i, (n0, n1, _, _) in enumerate(WINDOWS):
        here = slice(256 * i, 256 * i + n1 - n0)
        c = left_dot(tb, A[0:ROWS, here], A[ROWS:, here]).reshape(BX, PY, n1 - n0)
        smoothed[:, :, n0:n1] = c[:, 0:BY]

    lane4 = lax.broadcasted_iota(jnp.int32, (4, 128), 1)
    row4 = lax.broadcasted_iota(jnp.int32, (4, 128), 0)
    for vx in range(EX):
        total = own[5 * vx : 5 * vx + 4, :]
        if vx == 0:
            total = total + hx_lo[20:24, 0:128]
        total = total + jnp.where(
            row4 == 0, jnp.broadcast_to(hy_lo[10 + vx : 11 + vx, 0:128], (4, 128)), 0.0
        )
        k = ZEDGE + vx
        total = total + jnp.where(
            lane4 == 0, jnp.broadcast_to(hz_lo[0:4, k : k + 1], (4, 128)), 0.0
        )
        coarse[vx] = total


def constants():
    volume, lift, right, smooth, scales = (Packed() for _ in range(5))
    eye_x = np.eye(BX)
    volume.add("my", pad_both(np.kron(eye_x, -STEP * line_operator(EY, False))))
    right.add("ry", pad_both(np.kron(eye_x, -line_operator(EY, True))))
    volume.add_windows("bz", -STEP * line_operator(EZ, False).T)
    right.add_windows("rz", -line_operator(EZ, True).T)
    basis = eigen_basis_table()
    sx = np.kron(np.eye(EX), basis)
    sy = np.kron(np.eye(EY), basis)
    sz = np.kron(np.eye(EZ), basis)
    t = np.kron(sx, sy)
    smooth.add("tf", pad_both(t.T))
    smooth.add("tb", pad_both(t))
    smooth.add_windows("sf", sz, False)
    smooth.add_windows("sb", sz.T, False)
    spread = np.kron(np.eye(EZ), np.ones((1, 5)))
    rows_of = np.zeros((EX * PY, 8))
    for e in range(EX):
        for y in range(BY):
            rows_of[PY * e + y, EY * e + y // 5] = 1.0
    for packed, cuts in ((lift, LANES), (scales, WINDOWS)):
        packed.add("rows_of", rows_of, 1)
        for i, cut in enumerate(cuts):
            packed.add("spread" + str(i), spread[:, cut[0] : cut[1]], 1)
    values = eigen_value_table()
    modes = np.zeros((PY, BZ))
    for y in range(BY):
        modes[y] = values[y % 5] + np.tile(values, EZ)
    hx, hy, hz = hats_line(EX), hats_line(EY), hats_line(EZ)
    gx, gy, gz = slopes_line(EX), slopes_line(EY), slopes_line(EZ)
    for name, m in (("hz", hz), ("gz", gz)):
        wide = np.zeros((BZ, 256))
        wide[:, 0:EZ] = m[:EZ].T
        wide[:, 128 + ZEDGE] = m[EZ]
        lift.add(name, wide)
    half = 0.5 * LIFT * hat_weight_table()[0, 0]
    ex, ey = np.zeros_like(gx), np.zeros_like(gy)
    ex[0, 0] = -half
    ey[0, 0] = -half
    for name, m in (
        ("c0", np.kron(gx, hy)),
        ("c1", np.kron(hx, gy)),
        ("c2", np.kron(hx, hy)),
        ("d0", np.kron(ex, hy)),
        ("d1", np.kron(hx, ey)),
    ):
        lift.add(name, pad_to(pad_rows(-m), 16, ROWS))
    return volume, lift, right, smooth, scales, modes.astype(np.float32)


def shift(x, axis, by):
    size = lax.axis_size(axis)
    return lax.ppermute(x, axis, [(i, (i + by) % size) for i in range(size)])


def like(*shape):
    return jax.ShapeDtypeStruct(shape, F32)


def run(kernel, outs, operands, scratch=(), name=None, flops=0):
    vmem = pl.BlockSpec(memory_space=pltpu.VMEM)
    return pl.pallas_call(
        kernel,
        out_shape=outs,
        in_specs=[vmem] * len(operands),
        out_specs=[vmem] * len(outs),
        scratch_shapes=list(scratch),
        compiler_params=pltpu.CompilerParams(vmem_limit_bytes=32 * 2**20),
        cost_estimate=pl.CostEstimate(flops=flops, bytes_accessed=4 << 20, transcendentals=0),
        name=name,
    )(*operands)


def shards(velocity, obstacle_element_mask, element_metric_scale):
    volume, lift, right, smooth, scales, modes = constants()
    x_faces = run(
        face_kernel,
        [like(3, PY, BZ)] * 2,
        [velocity[:, 0], velocity[:, BX - 1]],
        name="face",
        flops=10**10,
    )
    faces = run(
        pack_kernel,
        [like(3 * BX, BZ)] * 2 + [like(PY, 128)] * 2,
        [velocity],
        name="pack",
        flops=10**10,
    )
    halo = [
        shift(x_faces[1], "gx", 1),
        shift(x_faces[0], "gx", -1),
        shift(faces[1], "gy", 1),
        shift(faces[0], "gy", -1),
        shift(faces[3], "gz", 1),
    ]
    halo[0], last = lax.optimization_barrier((halo[0], faces[2]))
    halo.append(shift(last, "gz", -1))
    field = like(3, BX, PY, BZ)
    half = jax.ShapeDtypeStruct((3, ROWS, BZ), BF16)
    v, conv = run(
        functools.partial(volume_kernel, volume),
        [field, field],
        [velocity, faces[2], volume.array()],
        scratch=[pltpu.VMEM((5, ROWS, BZ), BF16)] * 2,
        name="volume",
        flops=4 * 10**9,
    )
    prov, ph, plo, xp, xm, yp, ym, zp, zm, own = run(
        functools.partial(lift_kernel, lift),
        [field, half, half]
        + [like(PY, BZ), like(PY, BZ), like(16, BZ), like(16, BZ), like(PY, 128), like(PY, 128)]
        + [like(16, 128)],
        [v, conv, *halo, obstacle_element_mask, lift.array()],
        name="lift",
        flops=4 * 10**9,
    )
    (rhs,) = run(
        functools.partial(right_kernel, right),
        [like(BX, PY, BZ)],
        [prov, ph, plo, right.array()],
        name="right",
        flops=2 * 10**9,
    )
    gx_lo = shift(xp, "gx", 1)
    gz_hi = shift(zm, "gz", -1)
    gx_lo, gz_hi = lax.optimization_barrier((gx_lo, gz_hi))
    gx_hi = shift(xm, "gx", -1)
    yp = yp + jnp.pad(gx_lo[20:21, 256:512], ((10, 5), (0, BZ - 256)))
    gy_lo = shift(yp, "gy", 1)
    gy_hi = shift(ym, "gy", -1)
    zp = zp + jnp.pad(gx_lo[20:24, 128:256], ((0, 20), (0, 0)))
    zp = zp + jnp.pad(gy_lo[10:11, 128:256], ((0, 23), (0, 0)))
    gz_lo = shift(zp, "gz", 1)
    (inverse,) = run(
        functools.partial(divisor_kernel, scales),
        [like(BX, PY, 768)],
        [element_metric_scale, gy_lo, scales.array(), jnp.asarray(modes)],
        name="divisor",
        flops=2 * 10**9,
    )
    smoothed, coarse = run(
        functools.partial(smooth_kernel, smooth),
        [like(BX, BY, BZ), like(EX, EY, EZ)],
        [rhs, gx_lo, gx_hi, gy_lo, gy_hi, gz_lo, gz_hi, own, inverse]
        + [smooth.array()],
        scratch=[pltpu.VMEM((2 * ROWS, 768), BF16), pltpu.VMEM((2 * ROWS, BZ), BF16)],
        name="smooth",
        flops=3 * 10**9,
    )
    return (smoothed, coarse)


def solution(mesh):
    return jax.shard_map(
        shards,
        mesh=mesh,
        in_specs=(P(None, "gx", "gy", "gz"), P("gx", "gy", "gz"), P("gx", "gy", "gz")),
        out_specs=(P("gx", "gy", "gz"), P("gx", "gy", "gz")),
        check_vma=False,
    )
```

```python
import functools
import math

import jax
import jax.numpy as jnp
import ml_dtypes
import numpy as np
from jax import lax
from jax.experimental import pallas as pl
from jax.experimental.pallas import tpu as pltpu
from jax.sharding import PartitionSpec as P

LIFT = 10.0
STEP = 0.05
PENALTY = 4.0
LIFT_SCALE = -0.5 * LIFT * STEP

BX, BY, BZ = 10, 20, 640
EX, EY, EZ = 2, 4, 128
PY = 24
ROWS = BX * PY
TILES = BZ // 128
WINDOWS = ((0, 250, 0, 251), (250, 500, 249, 501), (500, 640, 499, 640))
LANES = ((0, 256), (256, 512), (512, 640))
ZEDGE = 16

F32 = jnp.float32
BF16 = jnp.bfloat16


def lobatto_points():
    return np.array([-1.0, -math.sqrt(3.0 / 7.0), 0.0, math.sqrt(3.0 / 7.0), 1.0])


def lobatto_weights():
    return np.array([0.1, 49.0 / 90.0, 32.0 / 45.0, 49.0 / 90.0, 0.1])


def derivative_matrix():
    points = lobatto_points()
    scales = np.array(
        [np.prod([points[i] - points[k] for k in range(5) if k != i]) for i in range(5)]
    )
    result = np.zeros((5, 5))
    for i in range(5):
        for j in range(5):
            if i != j:
                result[i, j] = scales[i] / (scales[j] * (points[i] - points[j]))
        result[i, i] = -np.sum(result[i])
    return result


def eigen_basis_table():
    return np.array(
        [
            [
                math.sqrt((1.0 if k == 0 else 2.0) / 5.0) * math.cos(math.pi * (i + 0.5) * k / 5.0)
                for k in range(5)
            ]
            for i in range(5)
        ]
    )


def eigen_value_table():
    return np.array([4.0 * math.sin(math.pi * k / 10.0) ** 2 for k in range(5)])


def hat_weight_table():
    points = lobatto_points()
    weights = lobatto_weights()
    return np.array([weights * (1.0 - points) / 2.0, weights * (1.0 + points) / 2.0])


def inner_matrix():
    result = derivative_matrix()
    result[0, 0] += 0.5 * LIFT
    result[4, 4] -= 0.5 * LIFT
    return result


def line_operator(elements, coupled):
    inner = inner_matrix()
    size = 5 * elements
    m = np.zeros((size, size))
    for e in range(elements):
        m[5 * e : 5 * e + 5, 5 * e : 5 * e + 5] = inner
        if coupled and e > 0:
            m[5 * e, 5 * e - 1] = -0.5 * LIFT
        if coupled and e < elements - 1:
            m[5 * e + 4, 5 * e + 5] = 0.5 * LIFT
    return m


def hats_line(elements):
    h = hat_weight_table()
    m = np.zeros((elements + 1, 5 * elements))
    for e in range(elements):
        m[e, 5 * e : 5 * e + 5] += h[0]
        m[e + 1, 5 * e : 5 * e + 5] += h[1]
    return m


def slopes_line(elements):
    h = hat_weight_table()
    d = derivative_matrix()
    g = h @ d
    g[0, 0] += LIFT * h[0, 0]
    g[1, 4] -= LIFT * h[1, 4]
    m = np.zeros((elements + 1, 5 * elements))
    for e in range(elements):
        m[e, 5 * e : 5 * e + 5] += g[0]
        m[e + 1, 5 * e : 5 * e + 5] += g[1]
    return m


def pad_rows(m):
    out = np.zeros((m.shape[0], BX, PY))
    out[:, :, :BY] = m.reshape(m.shape[0], BX, BY)
    return out.reshape(m.shape[0], ROWS)


def pad_both(m):
    return pad_rows(pad_rows(m).T).T


def pad_to(m, rows, columns):
    out = np.zeros((rows, columns))
    out[: m.shape[0], : m.shape[1]] = m
    return out


class Packed:

    def __init__(self):
        self.parts = []
        self.places = {}
        self.rows = 0

    def add(self, name, m, parts=2):
        m = np.asarray(m, np.float64)
        hi = m.astype(np.float32).astype(ml_dtypes.bfloat16)
        lo = (m - hi.astype(np.float64)).astype(np.float32).astype(ml_dtypes.bfloat16)
        places = []
        for part in (hi, lo)[:parts]:
            wide = np.zeros((part.shape[0], 256), ml_dtypes.bfloat16)
            wide[:, : part.shape[1]] = part
            places.append((self.rows, part.shape[0], part.shape[1]))
            self.parts.append(wide)
            self.rows += part.shape[0]
        self.places[name] = places

    def add_windows(self, name, m, coupled=True):
        for i, (n0, n1, k0, k1) in enumerate(WINDOWS):
            self.add(name + str(i), m[k0:k1, n0:n1] if coupled else m[n0:n1, n0:n1])

    def array(self):
        return jnp.asarray(np.concatenate(self.parts))

    def both(self, ref, name):
        r, n, c = self.places[name][0]
        return ref[r : r + 2 * n, 0:c]

    def get(self, ref, name):
        out = [ref[r : r + n, 0:c] for r, n, c in self.places[name]]
        return out[0] if len(out) == 1 else out


def split(x):
    hi = x.astype(BF16)
    return hi, (x - hi.astype(F32)).astype(BF16)


def stacked(x):
    return jnp.concatenate(split(x), axis=0)


def dot(a, b):
    return jnp.dot(a, b, preferred_element_type=F32)


def left_dot(m, hi, lo):
    rows = m.shape[0] // 2
    both = dot(m, hi)
    return both[:rows] + both[rows:] + dot(m[:rows], lo)


def right_dot(hi, lo, m):
    return dot(hi, m[0]) + dot(lo, m[0]) + dot(hi, m[1])


def stack_dot(x, m):
    rows = x.shape[0] // 2
    both = dot(x, m[0])
    return both[:rows] + both[rows:] + dot(x[:rows], m[1])


def flag(name, low):
    edge = 0 if low else lax.axis_size(name) - 1
    return jnp.where(lax.axis_index(name) == edge, 0.0, 1.0)


def face_kernel(v_lo, v_hi, x_lo, x_hi):
    for c in range(3):
        x_lo[c, 0:BY, :] = v_lo[c] * flag("gx", True)
        x_hi[c, 0:BY, :] = v_hi[c] * flag("gx", False)
        x_lo[c, BY:PY, :] = jnp.zeros((PY - BY, BZ), F32)
        x_hi[c, BY:PY, :] = jnp.zeros((PY - BY, BZ), F32)


def pack_kernel(v, y_lo, y_hi, z_lo, z_hi):
    y_low, y_high = flag("gy", True), flag("gy", False)
    lane = lax.broadcasted_iota(jnp.int32, (BY, 128), 1)
    low = jnp.zeros((BY, 128), F32)
    high = jnp.zeros((BY, 128), F32)
    for c in range(3):
        for x in range(BX):
            y_lo[BX * c + x : BX * c + x + 1, :] = v[c, x, 0:1, :] * y_low
            y_hi[BX * c + x : BX * c + x + 1, :] = v[c, x, BY - 1 : BY, :] * y_high
            here = lane == 16 * c + x
            low = jnp.where(here, jnp.broadcast_to(v[c, x, :, 0:1], (BY, 128)), low)
            high = jnp.where(here, jnp.broadcast_to(v[c, x, :, BZ - 1 : BZ], (BY, 128)), high)
    z_lo[0:BY, :] = low * flag("gz", True)
    z_hi[0:BY, :] = high * flag("gz", False)
    z_lo[BY:PY, :] = jnp.zeros((PY - BY, 128), F32)
    z_hi[BY:PY, :] = jnp.zeros((PY - BY, 128), F32)


def plane_sums(planes, scale):
    d = inner_matrix() * scale
    outs = []
    for i in range(5):
        total = None
        for j in range(5):
            if abs(d[i, j]) < 1e-12:
                continue
            term = float(d[i, j]) * planes[j]
            total = term if total is None else total + term
        outs.append(total)
    return outs


def add_lift(total, a, w, along, face, sign):
    p = face * jnp.maximum(jnp.abs(a[along]), jnp.abs(w[along]))
    q = p + sign * w[along]
    return [total[c] + (p * a[c] - q * w[c]) for c in range(3)]


def volume_kernel(packed, v, after, weights, V, conv, FH, FL):
    del after
    for c in range(3):
        for x in range(BX):
            V[c, x, 0:BY, :] = v[c, x]
            V[c, x, BY:PY, :] = jnp.zeros((PY - BY, BZ), F32)

    def products(t):
        dst = slice(128 * t, 128 * t + 128)
        for q in range(BX // 2):
            a = [V[c, 2 * q : 2 * q + 2, :, dst].reshape(2 * PY, 128) for c in range(3)]
            pairs = (a[0] * a[1], a[1] * a[1], a[1] * a[2], a[0] * a[2], a[2] * a[2])
            for f, value in enumerate(pairs):
                hi, lo = split(value)
                FH[f, 2 * PY * q : 2 * PY * (q + 1), dst] = hi
                FL[f, 2 * PY * q : 2 * PY * (q + 1), dst] = lo

    def along_z(i):
        n0, n1, k0, k1 = WINDOWS[i]
        high = FH[2:5, :, k0:k1].reshape(3 * ROWS, k1 - k0)
        low = FL[2:5, :, k0:k1].reshape(3 * ROWS, k1 - k0)
        z = right_dot(high, low, packed.get(weights, "bz" + str(i)))
        for c in range(3):
            place = ROWS * (1, 0, 2)[c]
            conv[c, :, :, n0:n1] = z[place : place + ROWS].reshape(BX, PY, n1 - n0)
    my = packed.both(weights, "my")

    def along_y(i, c):
        n0, n1 = LANES[i]
        y = left_dot(my, FH[c, :, n0:n1], FL[c, :, n0:n1]).reshape(BX, PY, n1 - n0)
        conv[c, :, :, n0:n1] = conv[c, :, :, n0:n1] + y

    def along_x(t):
        dst = slice(128 * t, 128 * t + 128)
        for e in range(EX):
            v0 = [V[0, 5 * e + i, :, dst] for i in range(5)]
            for c in range(3):
                flux = [v0[i] * V[c, 5 * e + i, :, dst] for i in range(5)]
                for i, total in enumerate(plane_sums(flux, -STEP)):
                    conv[c, 5 * e + i, :, dst] = conv[c, 5 * e + i, :, dst] + total


    lane = lax.broadcasted_iota(jnp.int32, (PY, 128), 1)
    row = lax.broadcasted_iota(jnp.int32, (PY, 128), 0)
    row_left = (lax.rem(row, 5) == 0) & (row > 0) & (row < BY)
    row_right = (lax.rem(row, 5) == 4) & (row < BY - 1)
    y_face = jnp.where(row_left | row_right, LIFT_SCALE, 0.0)
    y_sign = jnp.where(row_left, LIFT_SCALE, jnp.where(row_right, -LIFT_SCALE, 0.0))

    def inner_lifts(t):
        node = lane + 128 * t
        z_left = (lax.rem(node, 5) == 0) & (node > 0)
        z_right = (lax.rem(node, 5) == 4) & (node < BZ - 1)
        z_face = jnp.where(z_left | z_right, LIFT_SCALE, 0.0)
        z_sign = jnp.where(z_left, LIFT_SCALE, jnp.where(z_right, -LIFT_SCALE, 0.0))
        here = slice(128 * t, 128 + 128 * t)
        before = slice(128 * t - 128, 128 * t)
        after = slice(128 + 128 * t, 256 + 128 * t)
        for x in range(BX):
            a = [V[c, x, :, here] for c in range(3)]
            total = [conv[c, x, :, here] for c in range(3)]
            w = []
            for c in range(3):
                lo, hi = a[c], a[c]
                if t > 0:
                    lo = jnp.where(lane == 127, V[c, x, :, before], lo)
                if t < TILES - 1:
                    hi = jnp.where(lane == 0, V[c, x, :, after], hi)
                w.append(jnp.where(z_left, pltpu.roll(lo, 1, 1), pltpu.roll(hi, 127, 1)))
            total = add_lift(total, a, w, 2, z_face, z_sign)
            w = [
                jnp.where(row_left, pltpu.roll(a[c], 1, 0), pltpu.roll(a[c], PY - 1, 0))
                for c in range(3)
            ]
            total = add_lift(total, a, w, 1, y_face, y_sign)
            if x in (4, 5):
                sign = -1.0 if x == 4 else 1.0
                w = [V[c, 9 - x, :, here] for c in range(3)]
                total = add_lift(total, a, w, 0, LIFT_SCALE, sign * LIFT_SCALE)
            for c in range(3):
                conv[c, x, :, here] = total[c]

    for t in range(TILES):
        products(t)
        if t in (1, 3, 4):
            along_z((1, 3, 4).index(t))
    for t in range(TILES):
        inner_lifts(t)
        for job in range(2 * t, min(2 * t + 2, 9)):
            along_y(job // 3, job % 3)
        along_x(t)


def lift_kernel(
    packed, V, conv, hx_lo, hx_hi, hy_lo, hy_hi, hz_lo, hz_hi, mask, weights,
    prov, PH, PL, xp, xm, yp, ym, zp, zm, own,
):
    solid = spread_out(packed, weights, [mask[...].astype(F32).reshape(8, EZ).astype(BF16)])
    solid = jnp.concatenate(solid, axis=1)
    lane = lax.broadcasted_iota(jnp.int32, (PY, 128), 1)
    row8 = lax.broadcasted_iota(jnp.int32, (8, 128), 0)
    first_lane = jnp.where(lane == 0, LIFT_SCALE, 0.0)
    last_lane = jnp.where(lane == 127, LIFT_SCALE, 0.0)
    first_row = jnp.where(row8 == 0, LIFT_SCALE, 0.0)
    last_row = jnp.where(row8 == BY - 17, LIFT_SCALE, 0.0)
    damp = [1.0 / (1.0 + PENALTY * solid[PY * e : PY * (e + 1)]) for e in range(EX)]
    for t in range(TILES):
        here = slice(128 * t, 128 + 128 * t)
        for x in range(BX):
            a = [V[c, x, :, here] for c in range(3)]
            total = [conv[c, x, :, here] for c in range(3)]
            if t in (0, TILES - 1):
                edge = hz_lo if t == 0 else hz_hi
                w = [
                    jnp.broadcast_to(edge[:, 16 * c + x : 16 * c + x + 1], (PY, 128))
                    for c in range(3)
                ]
                face = first_lane if t == 0 else last_lane
                total = add_lift(total, a, w, 2, face, face if t == 0 else -face)
            if x in (0, BX - 1):
                w = [(hx_lo if x == 0 else hx_hi)[c, :, here] for c in range(3)]
                sign = 1.0 if x == 0 else -1.0
                total = add_lift(total, a, w, 0, LIFT_SCALE, sign * LIFT_SCALE)
            factor = damp[x // 5][:, here]
            done = [(a[c] + total[c]) * factor for c in range(3)]
            for c in range(3):
                prov[c, x, 8:16, here] = done[c][8:16]
            for r0, edge, face, sign in ((0, hy_lo, first_row, first_row), (16, hy_hi, last_row, -last_row)):
                w = [
                    jnp.broadcast_to(edge[BX * c + x : BX * c + x + 1, here], (8, 128))
                    for c in range(3)
                ]
                rows = slice(r0, r0 + 8)
                zero = [jnp.zeros((8, 128), F32)] * 3
                more = add_lift(zero, [part[rows] for part in a], w, 1, face, sign)
                for c in range(3):
                    prov[c, x, rows, here] = done[c][rows] + more[c] * factor[rows]

    for q in range(BX // 2):
        for c in range(3):
            hi, lo = split(prov[c, 2 * q : 2 * q + 2].reshape(2 * PY, BZ))
            PH[c, 2 * PY * q : 2 * PY * (q + 1), :] = hi
            PL[c, 2 * PY * q : 2 * PY * (q + 1), :] = lo
    first = [1.0 - flag(name, True) for name in ("gx", "gy", "gz")]
    x_low, y_low, z_low = (flag(name, True) for name in ("gx", "gy", "gz"))
    x_high, y_high, z_high = (flag(name, False) for name in ("gx", "gy", "gz"))
    parts = []
    c0, c1, c2, d0, d1 = (
        sum(part.astype(F32) for part in packed.get(weights, n)) for n in ("c0", "c1", "c2", "d0", "d1")
    )
    for c, m in enumerate((c0 + first[0] * d0, c1 + first[1] * d1, c2)):
        parts.append(left_dot(stacked(m), PH[c], PL[c]))
    coarse = stack_dot(stacked(parts[0] + parts[1]), packed.get(weights, "hz"))
    coarse = coarse + stack_dot(stacked(parts[2]), packed.get(weights, "gz"))
    lane16 = lax.broadcasted_iota(jnp.int32, (16, 128), 1)
    vertices = coarse[:, 0:128] - jnp.where(
        lane16 == 0, (0.5 * LIFT * 0.1) * first[2] * parts[2][:, 0:128], 0.0
    )
    row16 = lax.broadcasted_iota(jnp.int32, (16, 128), 0)
    there = jnp.where(row16 >= 10, x_high, 1.0) * jnp.where(lax.rem(row16, 5) == 4, y_high, 1.0)
    vertices = vertices * there
    edge = coarse[:, 128:256] * (there * z_high)
    edge_next = pltpu.roll(edge, 1, 1)
    own[...] = vertices

    xp[0:PY, :] = prov[0, BX - 1] * x_high
    xm[...] = prov[0, 0] * x_low
    xp[BY:PY, :] = jnp.zeros((PY - BY, BZ), F32)
    xp[20:24, 0:128] = vertices[10:14]
    xp[20:24, 128:256] = edge[10:14]
    xp[20:21, 256:384] = vertices[14:15]
    xp[20:21, 384:512] = edge[14:15]
    yp[8:16, :] = jnp.zeros((8, BZ), F32)
    ym[8:16, :] = jnp.zeros((8, BZ), F32)
    lane24 = lax.broadcasted_iota(jnp.int32, (PY, 128), 1)
    low = jnp.zeros((PY, 128), F32)
    high = jnp.zeros((PY, 128), F32)
    for x in range(BX):
        yp[x : x + 1, :] = prov[1, x, BY - 1 : BY, :] * y_high
        ym[x : x + 1, :] = prov[1, x, 0:1, :] * y_low
        low = jnp.where(lane24 == x, jnp.broadcast_to(prov[2, x, :, 0:1], (PY, 128)), low)
        high = jnp.where(lane24 == x, jnp.broadcast_to(prov[2, x, :, BZ - 1 : BZ], (PY, 128)), high)
    yp[10:11, 0:128] = vertices[4:5]
    yp[11:12, 0:128] = vertices[9:10]
    yp[10:11, 128:256] = edge[4:5] + edge_next[9:10]
    zm[...] = low * z_low
    zp[...] = high * z_high
    zp[0:4, :] = zp[0:4, :] + (edge[0:4] + edge_next[5:9])


def right_kernel(packed, prov, PH, PL, weights, rhs):
    for i, (n0, n1, k0, k1) in enumerate(WINDOWS):
        z = right_dot(PH[2, :, k0:k1], PL[2, :, k0:k1], packed.get(weights, "rz" + str(i)))
        rhs[:, :, n0:n1] = z.reshape(BX, PY, n1 - n0)
    ry = packed.both(weights, "ry")
    for n0, n1 in LANES:
        y = left_dot(ry, PH[1, :, n0:n1], PL[1, :, n0:n1]).reshape(BX, PY, n1 - n0)
        rhs[:, :, n0:n1] = rhs[:, :, n0:n1] + y

    def right_x(t, carry):
        dst = pl.ds(pl.multiple_of(128 * t, 128), 128)
        planes = [prov[0, x, :, dst] for x in range(BX)]
        outs = plane_sums(planes[:5], -1.0) + plane_sums(planes[5:], -1.0)
        outs[4] = outs[4] - 0.5 * LIFT * planes[5]
        outs[5] = outs[5] + 0.5 * LIFT * planes[4]
        for x in range(BX):
            rhs[x, :, dst] = rhs[x, :, dst] + outs[x]
        return carry

    lax.fori_loop(0, TILES, right_x, 0, unroll=True)


def spread_out(packed, weights, parts):
    rows_of = packed.get(weights, "rows_of")
    nodes = []
    for i in range(3):
        m = packed.get(weights, "spread" + str(i))
        wide = sum(dot(part, m) for part in parts)
        nodes.append(sum(dot(rows_of, part) for part in split(wide)[: len(parts)]))
    return nodes


def divisor_kernel(packed, scale, after, weights, modes, inverse):
    del after
    factor = spread_out(packed, weights, split(scale[...].reshape(8, EZ)))
    values = eigen_value_table()
    for i, (n0, n1, _, _) in enumerate(WINDOWS):
        for x in range(BX):
            f = factor[i][PY * (x // 5) : PY * (x // 5 + 1)]
            inverse[x, :, 256 * i : 256 * i + n1 - n0] = 1.0 / (
                f * (modes[:, 0 : n1 - n0] + float(values[x % 5])) + 1.0
            )


def smooth_kernel(
    packed, rhs, hx_lo, hx_hi, hy_lo, hy_hi, hz_lo, hz_hi, own, inverse, weights,
    smoothed, coarse, A, B,
):
    lift = 0.5 * LIFT
    lane = lax.broadcasted_iota(jnp.int32, (PY, 128), 1)
    row = lax.broadcasted_iota(jnp.int32, (PY, BZ), 0)
    for q in range(BX // 2):
        planes = []
        for x in (2 * q, 2 * q + 1):
            r = rhs[x]
            if x == 0:
                r = r + lift * hx_lo[...]
            if x == BX - 1:
                r = r - lift * hx_hi[...]
            r = r + jnp.where(row == 0, lift * jnp.broadcast_to(hy_lo[x : x + 1, :], (PY, BZ)), 0.0)
            r = r - jnp.where(
                row == BY - 1, lift * jnp.broadcast_to(hy_hi[x : x + 1, :], (PY, BZ)), 0.0
            )
            left = r[:, 0:128] + jnp.where(
                lane == 0, lift * jnp.broadcast_to(hz_lo[:, x : x + 1], (PY, 128)), 0.0
            )
            right = r[:, BZ - 128 : BZ] - jnp.where(
                lane == 127, lift * jnp.broadcast_to(hz_hi[:, x : x + 1], (PY, 128)), 0.0
            )
            planes.append(jnp.concatenate([left, r[:, 128 : BZ - 128], right], axis=1))
        hi, lo = split(jnp.concatenate(planes, axis=0))
        A[2 * PY * q : 2 * PY * (q + 1), 0:BZ] = hi
        A[ROWS + 2 * PY * q : ROWS + 2 * PY * (q + 1), 0:BZ] = lo

    tf = packed.both(weights, "tf")
    for n0, n1 in LANES:
        B[:, n0:n1] = stacked(left_dot(tf, A[0:ROWS, n0:n1], A[ROWS:, n0:n1]))

    for i, (n0, n1, _, _) in enumerate(WINDOWS):
        size = n1 - n0
        c = stack_dot(B[:, n0:n1], packed.get(weights, "sf" + str(i))).reshape(BX, PY, size)
        c = (c * inverse[:, :, 256 * i : 256 * i + size]).reshape(ROWS, size)
        c = stack_dot(stacked(c), packed.get(weights, "sb" + str(i)))
        A[:, 256 * i : 256 * i + size] = stacked(c)

    tb = packed.both(weights, "tb")
    for i, (n0, n1, _, _) in enumerate(WINDOWS):
        here = slice(256 * i, 256 * i + n1 - n0)
        c = left_dot(tb, A[0:ROWS, here], A[ROWS:, here]).reshape(BX, PY, n1 - n0)
        smoothed[:, :, n0:n1] = c[:, 0:BY]

    lane4 = lax.broadcasted_iota(jnp.int32, (4, 128), 1)
    row4 = lax.broadcasted_iota(jnp.int32, (4, 128), 0)
    for vx in range(EX):
        total = own[5 * vx : 5 * vx + 4, :]
        if vx == 0:
            total = total + hx_lo[20:24, 0:128]
        total = total + jnp.where(
            row4 == 0, jnp.broadcast_to(hy_lo[10 + vx : 11 + vx, 0:128], (4, 128)), 0.0
        )
        k = ZEDGE + vx
        total = total + jnp.where(
            lane4 == 0, jnp.broadcast_to(hz_lo[0:4, k : k + 1], (4, 128)), 0.0
        )
        coarse[vx] = total


def constants():
    volume, lift, right, smooth, scales = (Packed() for _ in range(5))
    eye_x = np.eye(BX)
    volume.add("my", pad_both(np.kron(eye_x, -STEP * line_operator(EY, False))))
    right.add("ry", pad_both(np.kron(eye_x, -line_operator(EY, True))))
    volume.add_windows("bz", -STEP * line_operator(EZ, False).T)
    right.add_windows("rz", -line_operator(EZ, True).T)
    basis = eigen_basis_table()
    sx = np.kron(np.eye(EX), basis)
    sy = np.kron(np.eye(EY), basis)
    sz = np.kron(np.eye(EZ), basis)
    t = np.kron(sx, sy)
    smooth.add("tf", pad_both(t.T))
    smooth.add("tb", pad_both(t))
    smooth.add_windows("sf", sz, False)
    smooth.add_windows("sb", sz.T, False)
    spread = np.kron(np.eye(EZ), np.ones((1, 5)))
    rows_of = np.zeros((EX * PY, 8))
    for e in range(EX):
        for y in range(BY):
            rows_of[PY * e + y, EY * e + y // 5] = 1.0
    for packed, cuts in ((lift, LANES), (scales, WINDOWS)):
        packed.add("rows_of", rows_of, 1)
        for i, cut in enumerate(cuts):
            packed.add("spread" + str(i), spread[:, cut[0] : cut[1]], 1)
    values = eigen_value_table()
    modes = np.zeros((PY, BZ))
    for y in range(BY):
        modes[y] = values[y % 5] + np.tile(values, EZ)
    hx, hy, hz = hats_line(EX), hats_line(EY), hats_line(EZ)
    gx, gy, gz = slopes_line(EX), slopes_line(EY), slopes_line(EZ)
    for name, m in (("hz", hz), ("gz", gz)):
        wide = np.zeros((BZ, 256))
        wide[:, 0:EZ] = m[:EZ].T
        wide[:, 128 + ZEDGE] = m[EZ]
        lift.add(name, wide)
    half = 0.5 * LIFT * hat_weight_table()[0, 0]
    ex, ey = np.zeros_like(gx), np.zeros_like(gy)
    ex[0, 0] = -half
    ey[0, 0] = -half
    for name, m in (
        ("c0", np.kron(gx, hy)),
        ("c1", np.kron(hx, gy)),
        ("c2", np.kron(hx, hy)),
        ("d0", np.kron(ex, hy)),
        ("d1", np.kron(hx, ey)),
    ):
        lift.add(name, pad_to(pad_rows(-m), 16, ROWS))
    return volume, lift, right, smooth, scales, modes.astype(np.float32)


def shift(x, axis, by):
    size = lax.axis_size(axis)
    return lax.ppermute(x, axis, [(i, (i + by) % size) for i in range(size)])


def like(*shape):
    return jax.ShapeDtypeStruct(shape, F32)


def run(kernel, outs, operands, scratch=(), name=None, flops=0):
    vmem = pl.BlockSpec(memory_space=pltpu.VMEM)
    return pl.pallas_call(
        kernel,
        out_shape=outs,
        in_specs=[vmem] * len(operands),
        out_specs=[vmem] * len(outs),
        scratch_shapes=list(scratch),
        compiler_params=pltpu.CompilerParams(vmem_limit_bytes=32 * 2**20),
        cost_estimate=pl.CostEstimate(flops=flops, bytes_accessed=4 << 20, transcendentals=0),
        name=name,
    )(*operands)


def shards(velocity, obstacle_element_mask, element_metric_scale):
    volume, lift, right, smooth, scales, modes = constants()
    x_faces = run(
        face_kernel,
        [like(3, PY, BZ)] * 2,
        [velocity[:, 0], velocity[:, BX - 1]],
        name="face",
        flops=10**10,
    )
    faces = run(
        pack_kernel,
        [like(3 * BX, BZ)] * 2 + [like(PY, 128)] * 2,
        [velocity],
        name="pack",
        flops=10**10,
    )
    halo = [
        shift(x_faces[1], "gx", 1),
        shift(x_faces[0], "gx", -1),
        shift(faces[1], "gy", 1),
        shift(faces[0], "gy", -1),
        shift(faces[3], "gz", 1),
    ]
    halo[0], last = lax.optimization_barrier((halo[0], faces[2]))
    halo.append(shift(last, "gz", -1))
    field = like(3, BX, PY, BZ)
    half = jax.ShapeDtypeStruct((3, ROWS, BZ), BF16)
    v, conv = run(
        functools.partial(volume_kernel, volume),
        [field, field],
        [velocity, faces[2], volume.array()],
        scratch=[pltpu.VMEM((5, ROWS, BZ), BF16)] * 2,
        name="volume",
        flops=4 * 10**9,
    )
    prov, ph, plo, xp, xm, yp, ym, zp, zm, own = run(
        functools.partial(lift_kernel, lift),
        [field, half, half]
        + [like(PY, BZ), like(PY, BZ), like(16, BZ), like(16, BZ), like(PY, 128), like(PY, 128)]
        + [like(16, 128)],
        [v, conv, *halo, obstacle_element_mask, lift.array()],
        name="lift",
        flops=4 * 10**9,
    )
    (rhs,) = run(
        functools.partial(right_kernel, right),
        [like(BX, PY, BZ)],
        [prov, ph, plo, right.array()],
        name="right",
        flops=2 * 10**9,
    )
    gx_lo = shift(xp, "gx", 1)
    gz_hi = shift(zm, "gz", -1)
    gx_lo, gz_hi = lax.optimization_barrier((gx_lo, gz_hi))
    gx_hi = shift(xm, "gx", -1)
    yp = yp + jnp.pad(gx_lo[20:21, 256:512], ((10, 5), (0, BZ - 256)))
    gy_lo = shift(yp, "gy", 1)
    gy_hi = shift(ym, "gy", -1)
    zp = zp + jnp.pad(gx_lo[20:24, 128:256], ((0, 20), (0, 0)))
    zp = zp + jnp.pad(gy_lo[10:11, 128:256], ((0, 23), (0, 0)))
    gz_lo = shift(zp, "gz", 1)
    (inverse,) = run(
        functools.partial(divisor_kernel, scales),
        [like(BX, PY, 768)],
        [element_metric_scale, gy_lo, scales.array(), jnp.asarray(modes)],
        name="divisor",
        flops=2 * 10**9,
    )
    smoothed, coarse = run(
        functools.partial(smooth_kernel, smooth),
        [like(BX, BY, BZ), like(EX, EY, EZ)],
        [rhs, gx_lo, gx_hi, gy_lo, gy_hi, gz_lo, gz_hi, own, inverse]
        + [smooth.array()],
        scratch=[pltpu.VMEM((2 * ROWS, 768), BF16), pltpu.VMEM((2 * ROWS, BZ), BF16)],
        name="smooth",
        flops=3 * 10**9,
    )
    return (smoothed, coarse)


def solution(mesh):
    return jax.shard_map(
        shards,
        mesh=mesh,
        in_specs=(P(None, "gx", "gy", "gz"), P("gx", "gy", "gz"), P("gx", "gy", "gz")),
        out_specs=(P("gx", "gy", "gz"), P("gx", "gy", "gz")),
        check_vma=False,
    )
```

```python
import functools
import math

import jax
import jax.numpy as jnp
import ml_dtypes
import numpy as np
from jax import lax
from jax.experimental import pallas as pl
from jax.experimental.pallas import tpu as pltpu
from jax.sharding import PartitionSpec as P

LIFT = 10.0
STEP = 0.05
PENALTY = 4.0
LIFT_SCALE = -0.5 * LIFT * STEP

BX, BY, BZ = 10, 20, 640
EX, EY, EZ = 2, 4, 128
PY = 24
ROWS = BX * PY
TILES = BZ // 128
WINDOWS = ((0, 250, 0, 251), (250, 500, 249, 501), (500, 640, 499, 640))
LANES = ((0, 256), (256, 512), (512, 640))
ZEDGE = 16

F32 = jnp.float32
BF16 = jnp.bfloat16


def lobatto_points():
    return np.array([-1.0, -math.sqrt(3.0 / 7.0), 0.0, math.sqrt(3.0 / 7.0), 1.0])


def lobatto_weights():
    return np.array([0.1, 49.0 / 90.0, 32.0 / 45.0, 49.0 / 90.0, 0.1])


def derivative_matrix():
    points = lobatto_points()
    scales = np.array(
        [np.prod([points[i] - points[k] for k in range(5) if k != i]) for i in range(5)]
    )
    result = np.zeros((5, 5))
    for i in range(5):
        for j in range(5):
            if i != j:
                result[i, j] = scales[i] / (scales[j] * (points[i] - points[j]))
        result[i, i] = -np.sum(result[i])
    return result


def eigen_basis_table():
    return np.array(
        [
            [
                math.sqrt((1.0 if k == 0 else 2.0) / 5.0) * math.cos(math.pi * (i + 0.5) * k / 5.0)
                for k in range(5)
            ]
            for i in range(5)
        ]
    )


def eigen_value_table():
    return np.array([4.0 * math.sin(math.pi * k / 10.0) ** 2 for k in range(5)])


def hat_weight_table():
    points = lobatto_points()
    weights = lobatto_weights()
    return np.array([weights * (1.0 - points) / 2.0, weights * (1.0 + points) / 2.0])


def inner_matrix():
    result = derivative_matrix()
    result[0, 0] += 0.5 * LIFT
    result[4, 4] -= 0.5 * LIFT
    return result


def line_operator(elements, coupled):
    inner = inner_matrix()
    size = 5 * elements
    m = np.zeros((size, size))
    for e in range(elements):
        m[5 * e : 5 * e + 5, 5 * e : 5 * e + 5] = inner
        if coupled and e > 0:
            m[5 * e, 5 * e - 1] = -0.5 * LIFT
        if coupled and e < elements - 1:
            m[5 * e + 4, 5 * e + 5] = 0.5 * LIFT
    return m


def hats_line(elements):
    h = hat_weight_table()
    m = np.zeros((elements + 1, 5 * elements))
    for e in range(elements):
        m[e, 5 * e : 5 * e + 5] += h[0]
        m[e + 1, 5 * e : 5 * e + 5] += h[1]
    return m


def slopes_line(elements):
    h = hat_weight_table()
    d = derivative_matrix()
    g = h @ d
    g[0, 0] += LIFT * h[0, 0]
    g[1, 4] -= LIFT * h[1, 4]
    m = np.zeros((elements + 1, 5 * elements))
    for e in range(elements):
        m[e, 5 * e : 5 * e + 5] += g[0]
        m[e + 1, 5 * e : 5 * e + 5] += g[1]
    return m


def pad_rows(m):
    out = np.zeros((m.shape[0], BX, PY))
    out[:, :, :BY] = m.reshape(m.shape[0], BX, BY)
    return out.reshape(m.shape[0], ROWS)


def pad_both(m):
    return pad_rows(pad_rows(m).T).T


def pad_to(m, rows, columns):
    out = np.zeros((rows, columns))
    out[: m.shape[0], : m.shape[1]] = m
    return out


class Packed:

    def __init__(self):
        self.parts = []
        self.places = {}
        self.rows = 0

    def add(self, name, m, parts=2):
        m = np.asarray(m, np.float64)
        hi = m.astype(np.float32).astype(ml_dtypes.bfloat16)
        lo = (m - hi.astype(np.float64)).astype(np.float32).astype(ml_dtypes.bfloat16)
        places = []
        for part in (hi, lo)[:parts]:
            wide = np.zeros((part.shape[0], 256), ml_dtypes.bfloat16)
            wide[:, : part.shape[1]] = part
            places.append((self.rows, part.shape[0], part.shape[1]))
            self.parts.append(wide)
            self.rows += part.shape[0]
        self.places[name] = places

    def add_windows(self, name, m, coupled=True):
        for i, (n0, n1, k0, k1) in enumerate(WINDOWS):
            self.add(name + str(i), m[k0:k1, n0:n1] if coupled else m[n0:n1, n0:n1])

    def array(self):
        return jnp.asarray(np.concatenate(self.parts))

    def both(self, ref, name):
        r, n, c = self.places[name][0]
        return ref[r : r + 2 * n, 0:c]

    def get(self, ref, name):
        out = [ref[r : r + n, 0:c] for r, n, c in self.places[name]]
        return out[0] if len(out) == 1 else out


def split(x):
    hi = x.astype(BF16)
    return hi, (x - hi.astype(F32)).astype(BF16)


def stacked(x):
    return jnp.concatenate(split(x), axis=0)


def dot(a, b):
    return jnp.dot(a, b, preferred_element_type=F32)


def left_dot(m, hi, lo):
    rows = m.shape[0] // 2
    both = dot(m, hi)
    return both[:rows] + both[rows:] + dot(m[:rows], lo)


def right_dot(hi, lo, m):
    return dot(hi, m[0]) + dot(lo, m[0]) + dot(hi, m[1])


def stack_dot(x, m):
    rows = x.shape[0] // 2
    both = dot(x, m[0])
    return both[:rows] + both[rows:] + dot(x[:rows], m[1])


def flag(name, low):
    edge = 0 if low else lax.axis_size(name) - 1
    return jnp.where(lax.axis_index(name) == edge, 0.0, 1.0)


def face_kernel(v_lo, v_hi, x_lo, x_hi):
    for c in range(3):
        x_lo[c, 0:BY, :] = v_lo[c] * flag("gx", True)
        x_hi[c, 0:BY, :] = v_hi[c] * flag("gx", False)
        x_lo[c, BY:PY, :] = jnp.zeros((PY - BY, BZ), F32)
        x_hi[c, BY:PY, :] = jnp.zeros((PY - BY, BZ), F32)


def pack_kernel(v, y_lo, y_hi, z_lo, z_hi):
    y_low, y_high = flag("gy", True), flag("gy", False)
    lane = lax.broadcasted_iota(jnp.int32, (BY, 128), 1)
    low = jnp.zeros((BY, 128), F32)
    high = jnp.zeros((BY, 128), F32)
    for c in range(3):
        for x in range(BX):
            y_lo[BX * c + x : BX * c + x + 1, :] = v[c, x, 0:1, :] * y_low
            y_hi[BX * c + x : BX * c + x + 1, :] = v[c, x, BY - 1 : BY, :] * y_high
            here = lane == 16 * c + x
            low = jnp.where(here, jnp.broadcast_to(v[c, x, :, 0:1], (BY, 128)), low)
            high = jnp.where(here, jnp.broadcast_to(v[c, x, :, BZ - 1 : BZ], (BY, 128)), high)
    z_lo[0:BY, :] = low * flag("gz", True)
    z_hi[0:BY, :] = high * flag("gz", False)
    z_lo[BY:PY, :] = jnp.zeros((PY - BY, 128), F32)
    z_hi[BY:PY, :] = jnp.zeros((PY - BY, 128), F32)


def plane_sums(planes, scale):
    d = inner_matrix() * scale
    outs = []
    for i in range(5):
        total = None
        for j in range(5):
            if abs(d[i, j]) < 1e-12:
                continue
            term = float(d[i, j]) * planes[j]
            total = term if total is None else total + term
        outs.append(total)
    return outs


def add_lift(total, a, w, along, face, sign):
    p = face * jnp.maximum(jnp.abs(a[along]), jnp.abs(w[along]))
    q = p + sign * w[along]
    return [total[c] + (p * a[c] - q * w[c]) for c in range(3)]


def volume_kernel(packed, v, after, weights, V, conv, FH, FL):
    del after
    for c in range(3):
        for x in range(BX):
            V[c, x, 0:BY, :] = v[c, x]
            V[c, x, BY:PY, :] = jnp.zeros((PY - BY, BZ), F32)

    def products(t):
        dst = slice(128 * t, 128 * t + 128)
        for q in range(BX // 2):
            a = [V[c, 2 * q : 2 * q + 2, :, dst].reshape(2 * PY, 128) for c in range(3)]
            pairs = (a[0] * a[1], a[1] * a[1], a[1] * a[2], a[0] * a[2], a[2] * a[2])
            for f, value in enumerate(pairs):
                hi, lo = split(value)
                FH[f, 2 * PY * q : 2 * PY * (q + 1), dst] = hi
                FL[f, 2 * PY * q : 2 * PY * (q + 1), dst] = lo

    def along_z(i):
        n0, n1, k0, k1 = WINDOWS[i]
        high = FH[2:5, :, k0:k1].reshape(3 * ROWS, k1 - k0)
        low = FL[2:5, :, k0:k1].reshape(3 * ROWS, k1 - k0)
        z = right_dot(high, low, packed.get(weights, "bz" + str(i)))
        for c in range(3):
            place = ROWS * (1, 0, 2)[c]
            conv[c, :, :, n0:n1] = z[place : place + ROWS].reshape(BX, PY, n1 - n0)
    my = packed.both(weights, "my")

    def along_y(i, c):
        n0, n1 = LANES[i]
        y = left_dot(my, FH[c, :, n0:n1], FL[c, :, n0:n1]).reshape(BX, PY, n1 - n0)
        conv[c, :, :, n0:n1] = conv[c, :, :, n0:n1] + y

    def along_x(t):
        dst = slice(128 * t, 128 * t + 128)
        for e in range(EX):
            v0 = [V[0, 5 * e + i, :, dst] for i in range(5)]
            for c in range(3):
                flux = [v0[i] * V[c, 5 * e + i, :, dst] for i in range(5)]
                for i, total in enumerate(plane_sums(flux, -STEP)):
                    conv[c, 5 * e + i, :, dst] = conv[c, 5 * e + i, :, dst] + total


    lane = lax.broadcasted_iota(jnp.int32, (PY, 128), 1)
    row = lax.broadcasted_iota(jnp.int32, (PY, 128), 0)
    row_left = (lax.rem(row, 5) == 0) & (row > 0) & (row < BY)
    row_right = (lax.rem(row, 5) == 4) & (row < BY - 1)
    y_face = jnp.where(row_left | row_right, LIFT_SCALE, 0.0)
    y_sign = jnp.where(row_left, LIFT_SCALE, jnp.where(row_right, -LIFT_SCALE, 0.0))

    def inner_lifts(t):
        node = lane + 128 * t
        z_left = (lax.rem(node, 5) == 0) & (node > 0)
        z_right = (lax.rem(node, 5) == 4) & (node < BZ - 1)
        z_face = jnp.where(z_left | z_right, LIFT_SCALE, 0.0)
        z_sign = jnp.where(z_left, LIFT_SCALE, jnp.where(z_right, -LIFT_SCALE, 0.0))
        here = slice(128 * t, 128 + 128 * t)
        before = slice(128 * t - 128, 128 * t)
        after = slice(128 + 128 * t, 256 + 128 * t)
        for x in range(BX):
            a = [V[c, x, :, here] for c in range(3)]
            total = [conv[c, x, :, here] for c in range(3)]
            w = []
            for c in range(3):
                lo, hi = a[c], a[c]
                if t > 0:
                    lo = jnp.where(lane == 127, V[c, x, :, before], lo)
                if t < TILES - 1:
                    hi = jnp.where(lane == 0, V[c, x, :, after], hi)
                w.append(jnp.where(z_left, pltpu.roll(lo, 1, 1), pltpu.roll(hi, 127, 1)))
            total = add_lift(total, a, w, 2, z_face, z_sign)
            w = [
                jnp.where(row_left, pltpu.roll(a[c], 1, 0), pltpu.roll(a[c], PY - 1, 0))
                for c in range(3)
            ]
            total = add_lift(total, a, w, 1, y_face, y_sign)
            if x in (4, 5):
                sign = -1.0 if x == 4 else 1.0
                w = [V[c, 9 - x, :, here] for c in range(3)]
                total = add_lift(total, a, w, 0, LIFT_SCALE, sign * LIFT_SCALE)
            for c in range(3):
                conv[c, x, :, here] = total[c]

    for t in range(TILES):
        products(t)
        if t in (1, 3, 4):
            along_z((1, 3, 4).index(t))
    for t in range(TILES):
        inner_lifts(t)
        for job in range(2 * t, min(2 * t + 2, 9)):
            along_y(job // 3, job % 3)
        along_x(t)


def lift_kernel(
    packed, V, conv, hx_lo, hx_hi, hy_lo, hy_hi, hz_lo, hz_hi, mask, weights,
    prov, PH, PL, xp, xm, yp, ym, zp, zm, own,
):
    solid = spread_out(packed, weights, [mask[...].astype(F32).reshape(8, EZ).astype(BF16)])
    solid = jnp.concatenate(solid, axis=1)
    lane = lax.broadcasted_iota(jnp.int32, (PY, 128), 1)
    row8 = lax.broadcasted_iota(jnp.int32, (8, 128), 0)
    first_lane = jnp.where(lane == 0, LIFT_SCALE, 0.0)
    last_lane = jnp.where(lane == 127, LIFT_SCALE, 0.0)
    first_row = jnp.where(row8 == 0, LIFT_SCALE, 0.0)
    last_row = jnp.where(row8 == BY - 17, LIFT_SCALE, 0.0)
    damp = [1.0 / (1.0 + PENALTY * solid[PY * e : PY * (e + 1)]) for e in range(EX)]
    for t in range(TILES):
        here = slice(128 * t, 128 + 128 * t)
        for x in range(BX):
            a = [V[c, x, :, here] for c in range(3)]
            total = [conv[c, x, :, here] for c in range(3)]
            if t in (0, TILES - 1):
                edge = hz_lo if t == 0 else hz_hi
                w = [
                    jnp.broadcast_to(edge[:, 16 * c + x : 16 * c + x + 1], (PY, 128))
                    for c in range(3)
                ]
                face = first_lane if t == 0 else last_lane
                total = add_lift(total, a, w, 2, face, face if t == 0 else -face)
            if x in (0, BX - 1):
                w = [(hx_lo if x == 0 else hx_hi)[c, :, here] for c in range(3)]
                sign = 1.0 if x == 0 else -1.0
                total = add_lift(total, a, w, 0, LIFT_SCALE, sign * LIFT_SCALE)
            factor = damp[x // 5][:, here]
            done = [(a[c] + total[c]) * factor for c in range(3)]
            for c in range(3):
                prov[c, x, 8:16, here] = done[c][8:16]
            for r0, edge, face, sign in ((0, hy_lo, first_row, first_row), (16, hy_hi, last_row, -last_row)):
                w = [
                    jnp.broadcast_to(edge[BX * c + x : BX * c + x + 1, here], (8, 128))
                    for c in range(3)
                ]
                rows = slice(r0, r0 + 8)
                zero = [jnp.zeros((8, 128), F32)] * 3
                more = add_lift(zero, [part[rows] for part in a], w, 1, face, sign)
                for c in range(3):
                    prov[c, x, rows, here] = done[c][rows] + more[c] * factor[rows]

    for q in range(BX // 2):
        for c in range(3):
            hi, lo = split(prov[c, 2 * q : 2 * q + 2].reshape(2 * PY, BZ))
            PH[c, 2 * PY * q : 2 * PY * (q + 1), :] = hi
            PL[c, 2 * PY * q : 2 * PY * (q + 1), :] = lo
    first = [1.0 - flag(name, True) for name in ("gx", "gy", "gz")]
    x_low, y_low, z_low = (flag(name, True) for name in ("gx", "gy", "gz"))
    x_high, y_high, z_high = (flag(name, False) for name in ("gx", "gy", "gz"))
    parts = []
    c0, c1, c2, d0, d1 = (
        sum(part.astype(F32) for part in packed.get(weights, n)) for n in ("c0", "c1", "c2", "d0", "d1")
    )
    for c, m in enumerate((c0 + first[0] * d0, c1 + first[1] * d1, c2)):
        parts.append(left_dot(stacked(m), PH[c], PL[c]))
    coarse = stack_dot(stacked(parts[0] + parts[1]), packed.get(weights, "hz"))
    coarse = coarse + stack_dot(stacked(parts[2]), packed.get(weights, "gz"))
    lane16 = lax.broadcasted_iota(jnp.int32, (16, 128), 1)
    vertices = coarse[:, 0:128] - jnp.where(
        lane16 == 0, (0.5 * LIFT * 0.1) * first[2] * parts[2][:, 0:128], 0.0
    )
    row16 = lax.broadcasted_iota(jnp.int32, (16, 128), 0)
    there = jnp.where(row16 >= 10, x_high, 1.0) * jnp.where(lax.rem(row16, 5) == 4, y_high, 1.0)
    vertices = vertices * there
    edge = coarse[:, 128:256] * (there * z_high)
    edge_next = pltpu.roll(edge, 1, 1)
    own[...] = vertices

    xp[0:PY, :] = prov[0, BX - 1] * x_high
    xm[...] = prov[0, 0] * x_low
    xp[BY:PY, :] = jnp.zeros((PY - BY, BZ), F32)
    xp[20:24, 0:128] = vertices[10:14]
    xp[20:24, 128:256] = edge[10:14]
    xp[20:21, 256:384] = vertices[14:15]
    xp[20:21, 384:512] = edge[14:15]
    yp[8:16, :] = jnp.zeros((8, BZ), F32)
    ym[8:16, :] = jnp.zeros((8, BZ), F32)
    lane24 = lax.broadcasted_iota(jnp.int32, (PY, 128), 1)
    low = jnp.zeros((PY, 128), F32)
    high = jnp.zeros((PY, 128), F32)
    for x in range(BX):
        yp[x : x + 1, :] = prov[1, x, BY - 1 : BY, :] * y_high
        ym[x : x + 1, :] = prov[1, x, 0:1, :] * y_low
        low = jnp.where(lane24 == x, jnp.broadcast_to(prov[2, x, :, 0:1], (PY, 128)), low)
        high = jnp.where(lane24 == x, jnp.broadcast_to(prov[2, x, :, BZ - 1 : BZ], (PY, 128)), high)
    yp[10:11, 0:128] = vertices[4:5]
    yp[11:12, 0:128] = vertices[9:10]
    yp[10:11, 128:256] = edge[4:5] + edge_next[9:10]
    zm[...] = low * z_low
    zp[...] = high * z_high
    zp[0:4, :] = zp[0:4, :] + (edge[0:4] + edge_next[5:9])


def right_kernel(packed, prov, PH, PL, weights, rhs):
    for i, (n0, n1, k0, k1) in enumerate(WINDOWS):
        z = right_dot(PH[2, :, k0:k1], PL[2, :, k0:k1], packed.get(weights, "rz" + str(i)))
        rhs[:, :, n0:n1] = z.reshape(BX, PY, n1 - n0)
    ry = packed.both(weights, "ry")
    for n0, n1 in LANES:
        y = left_dot(ry, PH[1, :, n0:n1], PL[1, :, n0:n1]).reshape(BX, PY, n1 - n0)
        rhs[:, :, n0:n1] = rhs[:, :, n0:n1] + y

    def right_x(t, carry):
        dst = pl.ds(pl.multiple_of(128 * t, 128), 128)
        planes = [prov[0, x, :, dst] for x in range(BX)]
        outs = plane_sums(planes[:5], -1.0) + plane_sums(planes[5:], -1.0)
        outs[4] = outs[4] - 0.5 * LIFT * planes[5]
        outs[5] = outs[5] + 0.5 * LIFT * planes[4]
        for x in range(BX):
            rhs[x, :, dst] = rhs[x, :, dst] + outs[x]
        return carry

    lax.fori_loop(0, TILES, right_x, 0, unroll=True)


def spread_out(packed, weights, parts):
    rows_of = packed.get(weights, "rows_of")
    nodes = []
    for i in range(3):
        m = packed.get(weights, "spread" + str(i))
        wide = sum(dot(part, m) for part in parts)
        nodes.append(sum(dot(rows_of, part) for part in split(wide)[: len(parts)]))
    return nodes


def divisor_kernel(packed, scale, after, weights, modes, inverse):
    del after
    factor = spread_out(packed, weights, split(scale[...].reshape(8, EZ)))
    values = eigen_value_table()
    for i, (n0, n1, _, _) in enumerate(WINDOWS):
        for x in range(BX):
            f = factor[i][PY * (x // 5) : PY * (x // 5 + 1)]
            inverse[x, :, 256 * i : 256 * i + n1 - n0] = 1.0 / (
                f * (modes[:, 0 : n1 - n0] + float(values[x % 5])) + 1.0
            )


def smooth_kernel(
    packed, rhs, hx_lo, hx_hi, hy_lo, hy_hi, hz_lo, hz_hi, own, inverse, weights,
    smoothed, coarse, A, B,
):
    lift = 0.5 * LIFT
    lane = lax.broadcasted_iota(jnp.int32, (PY, 128), 1)
    row = lax.broadcasted_iota(jnp.int32, (PY, BZ), 0)
    for q in range(BX // 2):
        planes = []
        for x in (2 * q, 2 * q + 1):
            r = rhs[x]
            if x == 0:
                r = r + lift * hx_lo[...]
            if x == BX - 1:
                r = r - lift * hx_hi[...]
            r = r + jnp.where(row == 0, lift * jnp.broadcast_to(hy_lo[x : x + 1, :], (PY, BZ)), 0.0)
            r = r - jnp.where(
                row == BY - 1, lift * jnp.broadcast_to(hy_hi[x : x + 1, :], (PY, BZ)), 0.0
            )
            left = r[:, 0:128] + jnp.where(
                lane == 0, lift * jnp.broadcast_to(hz_lo[:, x : x + 1], (PY, 128)), 0.0
            )
            right = r[:, BZ - 128 : BZ] - jnp.where(
                lane == 127, lift * jnp.broadcast_to(hz_hi[:, x : x + 1], (PY, 128)), 0.0
            )
            planes.append(jnp.concatenate([left, r[:, 128 : BZ - 128], right], axis=1))
        hi, lo = split(jnp.concatenate(planes, axis=0))
        A[2 * PY * q : 2 * PY * (q + 1), 0:BZ] = hi
        A[ROWS + 2 * PY * q : ROWS + 2 * PY * (q + 1), 0:BZ] = lo

    tf = packed.both(weights, "tf")

    tb = packed.both(weights, "tb")
    for i, (n0, n1, _, _) in enumerate(WINDOWS):
        l0, l1 = LANES[i]
        B[:, l0:l1] = stacked(left_dot(tf, A[0:ROWS, l0:l1], A[ROWS:, l0:l1]))
        size = n1 - n0
        c = stack_dot(B[:, n0:n1], packed.get(weights, "sf" + str(i))).reshape(BX, PY, size)
        c = (c * inverse[:, :, 256 * i : 256 * i + size]).reshape(ROWS, size)
        c = stack_dot(stacked(c), packed.get(weights, "sb" + str(i)))
        A[:, 256 * i : 256 * i + size] = stacked(c)
        here = slice(256 * i, 256 * i + n1 - n0)
        c = left_dot(tb, A[0:ROWS, here], A[ROWS:, here]).reshape(BX, PY, n1 - n0)
        smoothed[:, :, n0:n1] = c[:, 0:BY]

    lane4 = lax.broadcasted_iota(jnp.int32, (4, 128), 1)
    row4 = lax.broadcasted_iota(jnp.int32, (4, 128), 0)
    for vx in range(EX):
        total = own[5 * vx : 5 * vx + 4, :]
        if vx == 0:
            total = total + hx_lo[20:24, 0:128]
        total = total + jnp.where(
            row4 == 0, jnp.broadcast_to(hy_lo[10 + vx : 11 + vx, 0:128], (4, 128)), 0.0
        )
        k = ZEDGE + vx
        total = total + jnp.where(
            lane4 == 0, jnp.broadcast_to(hz_lo[0:4, k : k + 1], (4, 128)), 0.0
        )
        coarse[vx] = total


def constants():
    volume, lift, right, smooth, scales = (Packed() for _ in range(5))
    eye_x = np.eye(BX)
    volume.add("my", pad_both(np.kron(eye_x, -STEP * line_operator(EY, False))))
    right.add("ry", pad_both(np.kron(eye_x, -line_operator(EY, True))))
    volume.add_windows("bz", -STEP * line_operator(EZ, False).T)
    right.add_windows("rz", -line_operator(EZ, True).T)
    basis = eigen_basis_table()
    sx = np.kron(np.eye(EX), basis)
    sy = np.kron(np.eye(EY), basis)
    sz = np.kron(np.eye(EZ), basis)
    t = np.kron(sx, sy)
    smooth.add("tf", pad_both(t.T))
    smooth.add("tb", pad_both(t))
    smooth.add_windows("sf", sz, False)
    smooth.add_windows("sb", sz.T, False)
    spread = np.kron(np.eye(EZ), np.ones((1, 5)))
    rows_of = np.zeros((EX * PY, 8))
    for e in range(EX):
        for y in range(BY):
            rows_of[PY * e + y, EY * e + y // 5] = 1.0
    for packed, cuts in ((lift, LANES), (scales, WINDOWS)):
        packed.add("rows_of", rows_of, 1)
        for i, cut in enumerate(cuts):
            packed.add("spread" + str(i), spread[:, cut[0] : cut[1]], 1)
    values = eigen_value_table()
    modes = np.zeros((PY, BZ))
    for y in range(BY):
        modes[y] = values[y % 5] + np.tile(values, EZ)
    hx, hy, hz = hats_line(EX), hats_line(EY), hats_line(EZ)
    gx, gy, gz = slopes_line(EX), slopes_line(EY), slopes_line(EZ)
    for name, m in (("hz", hz), ("gz", gz)):
        wide = np.zeros((BZ, 256))
        wide[:, 0:EZ] = m[:EZ].T
        wide[:, 128 + ZEDGE] = m[EZ]
        lift.add(name, wide)
    half = 0.5 * LIFT * hat_weight_table()[0, 0]
    ex, ey = np.zeros_like(gx), np.zeros_like(gy)
    ex[0, 0] = -half
    ey[0, 0] = -half
    for name, m in (
        ("c0", np.kron(gx, hy)),
        ("c1", np.kron(hx, gy)),
        ("c2", np.kron(hx, hy)),
        ("d0", np.kron(ex, hy)),
        ("d1", np.kron(hx, ey)),
    ):
        lift.add(name, pad_to(pad_rows(-m), 16, ROWS))
    return volume, lift, right, smooth, scales, modes.astype(np.float32)


def shift(x, axis, by):
    size = lax.axis_size(axis)
    return lax.ppermute(x, axis, [(i, (i + by) % size) for i in range(size)])


def like(*shape):
    return jax.ShapeDtypeStruct(shape, F32)


def run(kernel, outs, operands, scratch=(), name=None, flops=0):
    vmem = pl.BlockSpec(memory_space=pltpu.VMEM)
    return pl.pallas_call(
        kernel,
        out_shape=outs,
        in_specs=[vmem] * len(operands),
        out_specs=[vmem] * len(outs),
        scratch_shapes=list(scratch),
        compiler_params=pltpu.CompilerParams(vmem_limit_bytes=32 * 2**20),
        cost_estimate=pl.CostEstimate(flops=flops, bytes_accessed=4 << 20, transcendentals=0),
        name=name,
    )(*operands)


def shards(velocity, obstacle_element_mask, element_metric_scale):
    volume, lift, right, smooth, scales, modes = constants()
    x_faces = run(
        face_kernel,
        [like(3, PY, BZ)] * 2,
        [velocity[:, 0], velocity[:, BX - 1]],
        name="face",
        flops=10**10,
    )
    faces = run(
        pack_kernel,
        [like(3 * BX, BZ)] * 2 + [like(PY, 128)] * 2,
        [velocity],
        name="pack",
        flops=10**10,
    )
    halo = [
        shift(x_faces[1], "gx", 1),
        shift(x_faces[0], "gx", -1),
        shift(faces[1], "gy", 1),
        shift(faces[0], "gy", -1),
        shift(faces[3], "gz", 1),
    ]
    halo[0], last = lax.optimization_barrier((halo[0], faces[2]))
    halo.append(shift(last, "gz", -1))
    field = like(3, BX, PY, BZ)
    half = jax.ShapeDtypeStruct((3, ROWS, BZ), BF16)
    v, conv = run(
        functools.partial(volume_kernel, volume),
        [field, field],
        [velocity, faces[2], volume.array()],
        scratch=[pltpu.VMEM((5, ROWS, BZ), BF16)] * 2,
        name="volume",
        flops=4 * 10**9,
    )
    prov, ph, plo, xp, xm, yp, ym, zp, zm, own = run(
        functools.partial(lift_kernel, lift),
        [field, half, half]
        + [like(PY, BZ), like(PY, BZ), like(16, BZ), like(16, BZ), like(PY, 128), like(PY, 128)]
        + [like(16, 128)],
        [v, conv, *halo, obstacle_element_mask, lift.array()],
        name="lift",
        flops=4 * 10**9,
    )
    (rhs,) = run(
        functools.partial(right_kernel, right),
        [like(BX, PY, BZ)],
        [prov, ph, plo, right.array()],
        name="right",
        flops=2 * 10**9,
    )
    gx_lo = shift(xp, "gx", 1)
    gz_hi = shift(zm, "gz", -1)
    gx_lo, gz_hi = lax.optimization_barrier((gx_lo, gz_hi))
    gx_hi = shift(xm, "gx", -1)
    yp = yp + jnp.pad(gx_lo[20:21, 256:512], ((10, 5), (0, BZ - 256)))
    gy_lo = shift(yp, "gy", 1)
    gy_hi = shift(ym, "gy", -1)
    zp = zp + jnp.pad(gx_lo[20:24, 128:256], ((0, 20), (0, 0)))
    zp = zp + jnp.pad(gy_lo[10:11, 128:256], ((0, 23), (0, 0)))
    gz_lo = shift(zp, "gz", 1)
    (inverse,) = run(
        functools.partial(divisor_kernel, scales),
        [like(BX, PY, 768)],
        [element_metric_scale, gy_lo, scales.array(), jnp.asarray(modes)],
        name="divisor",
        flops=2 * 10**9,
    )
    smoothed, coarse = run(
        functools.partial(smooth_kernel, smooth),
        [like(BX, BY, BZ), like(EX, EY, EZ)],
        [rhs, gx_lo, gx_hi, gy_lo, gy_hi, gz_lo, gz_hi, own, inverse]
        + [smooth.array()],
        scratch=[pltpu.VMEM((2 * ROWS, 768), BF16), pltpu.VMEM((2 * ROWS, BZ), BF16)],
        name="smooth",
        flops=3 * 10**9,
    )
    return (smoothed, coarse)


def solution(mesh):
    return jax.shard_map(
        shards,
        mesh=mesh,
        in_specs=(P(None, "gx", "gy", "gz"), P("gx", "gy", "gz"), P("gx", "gy", "gz")),
        out_specs=(P("gx", "gy", "gz"), P("gx", "gy", "gz")),
        check_vma=False,
    )
```
